32 devices in a mesh: occ: 16 (over z, y, x), vir: 2 (over core).
Axes of the slice: x: 2, y: 2, z: 4, core: 2. Of those that a mesh axis runs over, the one named last changes fastest.
Arguments:
- amplitudes: bfloat16 [64, 8, 64, 4096], P(('occ', 'vir')), may hold values from -6 to 6
- tile_counts: int32 [64], P(('occ', 'vir')), may hold values from 1 to 8, 384 in all
- tile_owner: int32 [64, 8], P(('occ', 'vir')), may hold values from 0 to 15, all different within a row; in each aligned block of 2 rows (0 to 1, 2 to 3, ...) at most 2 rows name the same one
- tile_local: int32 [64, 8], P(('occ', 'vir')), may hold values from 0 to 15
- pair_map: int32 [256], replicated, may hold values from 0 to 255, each once
- hole_weight: bfloat16 [64, 64, 64], P(('occ', 'vir')), may hold values from -0.75 to 0.75
- fock_tiles: bfloat16 [16, 64, 64], replicated, may hold values from -0.75 to 0.75
- ladder_panels: bfloat16 [256, 4096, 128], P('occ', 'vir'), may hold values from -0.03125 to 0.03125
Outputs:
- local_residual: bfloat16 [64, 8, 64, 4096], P(('occ', 'vir'))
- ladder_panel: bfloat16 [64, 64, 128], P(('occ', 'vir'))
The draws below stay inside these ranges and needn't reach their ends.
Inputs may be any that keep to these rules, and one draw needn't show every extreme that they name: `tile_counts`: entries of a list at or past its count are not used. `tile_owner`: the 8 entries of a pair tile name different owners; among the pair tiles of one device no owner is named by more than 2 entries. `pair_map`: every virtual tile pair stands at exactly one owner position.
All inputs are finite; a program needn't handle non-finite values. No bound on the sum of `tile_counts` on one device may be relied on, other than what follows from the above.
Results may differ from the reference program's by a relative error of at most 0.001.
Values may be sent and summed in bfloat16 or wider, within the bound.
No kernel may reach another device: no remote copies, remote signals or barrier semaphores. Data moves between devices by JAX's collectives and lax.ppermute only.
A program may use at most 320 MiB of HBM per device.

```python
import math
import jax
import jax.numpy as jnp
import numpy as np
from jax import lax

VT = 64
NVT = 16
OPT = 64
SLOTS = 8
PT_DEV = 2
CAP = 2
PANEL = 128
NTILES = 256
TILE_SZ = 4096
OWNERS = 16
TILE_OWN = 16
PTILES = 64


def place_ends(array, own_key, least, largest):
    longest = array.shape.index(max(array.shape))
    spots = []
    for shift in (0, 1):
        where = [jax.random.randint(jax.random.fold_in(own_key, axis), (), 0, length) for axis, length in enumerate(array.shape)]
        where[longest] = (where[longest] + shift) % array.shape[longest]
        spots.append(tuple(where))
    return array.at[spots[0]].set(least).at[spots[1]].set(largest)


def shard_levels(rng, dims, shards, least, top_value):
    gain, own = 1.0, jax.random.fold_in(rng, 6)
    for axis_at, shards_of in shards:
        steps = jnp.exp(jax.random.uniform(jax.random.fold_in(own, axis_at), (shards_of,), jnp.float32, least / len(shards), top_value / len(shards)))
        gain = gain * jnp.repeat(steps, dims[axis_at] // shards_of).reshape([-1 if axis == axis_at else 1 for axis in range(len(dims))])
    return gain


def split_up(number_of, total, most, slope):
    portions = [(1 << 20) // math.isqrt(rank ** slope) + 1 for rank in range(2, number_of + 1)]
    spare, counts = total - most - (number_of - 1), [1] * (number_of - 1)
    while spare > 0:
        candidates = [i for i in range(number_of - 1) if counts[i] < most]
        mass, left = sum([portions[i] for i in candidates]), spare
        for i in candidates:
            more = min(most - counts[i], max(1, left * portions[i] // mass), spare)
            counts[i] = counts[i] + more
            spare = spare - more
    return np.array([most] + counts)


def uneven(own_key, count, total, reach, skew):
    if count == 2:
        one = jax.random.randint(own_key, (), max(1, total - reach), min(reach, total - 1) + 1)
        return jnp.stack([one, total - one])
    tallies = jnp.asarray(split_up(count, total, reach, skew), jnp.int32)
    twos = (count - 1) // 2
    donor, receiver = tallies[1:1 + 2 * twos:2], tallies[2:2 + 2 * twos:2]
    room = jnp.minimum(donor - 1, reach - receiver)
    passed = jax.random.randint(jax.random.fold_in(own_key, 1), (twos,), 0, 1 << 20) % (room + 1)
    tallies = tallies.at[1:1 + 2 * twos:2].set(donor - passed).at[2:2 + 2 * twos:2].set(receiver + passed)
    return tallies[jax.random.permutation(jax.random.fold_in(own_key, 2), count)]


def deal_out(rng, own, number, rows, number_of, top, reach, skew):
    ranking = jax.random.permutation(rng, number_of)
    heavy_load, usual = load_shares(number_of, rows * top, reach, skew, True), load_shares(number_of, rows * top, reach, skew, False)
    places = jnp.arange(number_of)

    def named(sizes, offset_by):
        used = int((sizes > 0).sum())
        fixed = max(1, used // 4)
        shifted = fixed + (places - fixed + offset_by * (used - fixed)) % max(1, number_of - fixed)
        return jnp.zeros((number_of,), jnp.int32).at[ranking[jnp.where(places < fixed, places, shifted)]].set(jnp.asarray(sizes, jnp.int32))

    sizes = jnp.where(number % 4 == 0, named(heavy_load, number // 4), named(usual, number - number // 4 - 1))
    mixed = jax.random.permutation(jax.random.fold_in(own, 3), number_of)
    source_of, sink = mixed[0:number_of // 2 * 2:2], mixed[1:number_of // 2 * 2:2]
    margin = jnp.minimum(sizes[source_of] - 1, reach - sizes[sink]) // 2
    margin = jnp.where((source_of == ranking[0]) | (sink == ranking[0]) | (sizes[sink] == 0), 0, jnp.maximum(margin, 0))
    shifted = jax.random.randint(jax.random.fold_in(own, 4), (number_of // 2,), 0, 1 << 20) % (margin + 1)
    sizes = sizes.at[source_of].add(-shifted).at[sink].add(shifted)
    members = jnp.searchsorted(jnp.cumsum(sizes), jnp.arange(rows * top), side="right").astype(jnp.int32)
    grid = members.reshape(top, rows).T
    grid = grid[jax.random.permutation(jax.random.fold_in(own, 1), rows)]
    offset_by = jax.random.randint(jax.random.fold_in(own, 2), (rows, 1), 0, top)
    return jnp.take_along_axis(grid, (jnp.arange(top)[None, :] + offset_by) % top, axis=1)


def load_shares(amount, total, most, skew, full):
    portions = [(1 << 20) // math.isqrt(rank ** skew) + 1 for rank in range(1, amount + 1)]
    largest = most if full else min(most, max(-(-total // amount), total * portions[0] // sum(portions)))
    least = 1 if total - largest >= amount - 1 else 0
    given, spare = [largest] + [least] * (amount - 1), total - largest - least * (amount - 1)
    while spare > 0:
        candidates = [i for i in range(1, amount) if given[i] < largest] or [i for i in range(1, amount) if given[i] < most]
        mass, left = sum([portions[i] for i in candidates]), spare
        for i in candidates:
            more = min(most - given[i], max(1, left * portions[i] // mass), spare)
            given[i] = given[i] + more
            spare = spare - more
    return np.array(given)


def centred(own_key, dims, scale, bound, pieces=(), kind=jnp.bfloat16):
    gain = shard_levels(own_key, dims, pieces, -0.22, 0.18) if pieces else 1.0
    values = jax.random.normal(own_key, dims, jnp.float32) * scale * gain
    return jnp.minimum(jnp.maximum(values, -bound), bound).astype(kind)


def setup_inputs(seed: int = 0) -> dict:
    keys = jax.random.split(jax.random.key(seed), 9)
    amplitudes = centred(keys[0], (PTILES, SLOTS, OPT, TILE_SZ), 1.0, 6.0, ((0, 32),))
    tile_counts = uneven(keys[1], PTILES, PTILES * 3 * SLOTS // 4, SLOTS, 1).astype(jnp.int32)
    tile_owner_keys = jax.random.split(jax.random.fold_in(keys[2], 1), PTILES // PT_DEV)
    tile_owner_turns = jax.random.permutation(jax.random.fold_in(keys[2], 3), PTILES // PT_DEV)
    tile_owner = jax.vmap(lambda own, number: deal_out(jax.random.fold_in(keys[2], 2), own, number, PT_DEV, OWNERS, SLOTS, CAP, 2))(tile_owner_keys, tile_owner_turns).reshape((PTILES, SLOTS))
    tile_local = place_ends(jax.random.randint(keys[3], (PTILES, SLOTS), 0, TILE_OWN), jax.random.fold_in(keys[3], 1), 0, TILE_OWN - 1).astype(jnp.int32)
    pair_map = jax.random.permutation(keys[4], NTILES).astype(jnp.int32)
    hole_weight = centred(keys[5], (PTILES, OPT, OPT), OPT ** -0.5, 0.75, ((0, 32),))
    fock_tiles = centred(keys[6], (NVT, VT, VT), VT ** -0.5, 0.75)
    ladder_panels = centred(keys[7], (NTILES, TILE_SZ, PANEL), (TILE_SZ * SLOTS) ** -0.5, 0.03125, ((0, 16), (1, 2)))
    return dict(amplitudes=amplitudes, tile_counts=tile_counts, tile_owner=tile_owner, tile_local=tile_local, pair_map=pair_map, hole_weight=hole_weight, fock_tiles=fock_tiles, ladder_panels=ladder_panels)


def reference(amplitudes, tile_counts, tile_owner, tile_local, pair_map, hole_weight, fock_tiles, ladder_panels):
    tile_pos = (tile_owner * TILE_OWN + tile_local).astype(jnp.int32)
    tile_ident = pair_map[tile_pos].astype(jnp.int32)
    row_tile = (tile_ident // NVT).astype(jnp.int32)
    col_tile = (tile_ident % NVT).astype(jnp.int32)
    used_mask = (jnp.arange(SLOTS, dtype=jnp.int32)[None, :] < tile_counts[:, None]).astype(jnp.float32)
    left_fock = fock_tiles[row_tile].astype(jnp.float32)
    right_fock = fock_tiles[col_tile].astype(jnp.float32)

    def one_tile(inputs):
        blocks, weight, positions, mask_row, left_part, right_part = inputs
        blocks_wide = blocks.astype(jnp.float32)
        hole = jnp.einsum('pq,sqx->spx', weight.astype(jnp.float32), blocks_wide)
        shaped = blocks_wide.reshape(SLOTS, OPT, VT, VT)
        fock_part = jnp.einsum('spce,sed->spcd', shaped, right_part) + jnp.einsum('sce,sped->spcd', left_part, shaped)
        summed = (hole + fock_part.reshape(SLOTS, OPT, TILE_SZ)) * mask_row[:, None, None]
        panels = ladder_panels[positions].astype(jnp.float32)
        ladder = jnp.einsum('spx,sxq->pq', blocks_wide * mask_row[:, None, None], panels)
        return summed.astype(jnp.bfloat16), ladder.astype(jnp.bfloat16)

    local_residual, ladder_panel = lax.map(one_tile, (amplitudes, hole_weight, tile_pos, used_mask, left_fock, right_fock))
    return local_residual, ladder_panel
```

```python
import functools

import jax
import jax.numpy as jnp
from jax import lax
from jax.experimental import pallas as pl
from jax.experimental.pallas import tpu as pltpu
from jax.sharding import PartitionSpec as P

AXES = ("occ", "vir")
CHUNKS = 4
EXTRA = 2
VMEM_LIMIT = 48 * 1024 * 1024


def pack_kernel(owner_ref, count_ref, amp_ref, *refs):
    outs, (slot_ref, sem) = refs[:-2], refs[-2:]
    devices, rows, width = outs[0].shape
    owners = slot_ref.shape[0]
    parts = devices // owners
    tiles, slots = owner_ref.shape
    for o in range(owners):
        slot_ref[o] = 0
    for t in reversed(range(tiles)):
        for s in range(slots):

            @pl.when(s < count_ref[t])
            def _():
                slot_ref[owner_ref[t, s]] = t * slots + s

    def copies(o):
        entry = slot_ref[o]
        t, s = entry // slots, entry % slots
        for v in range(parts):
            for i, out in enumerate(outs):
                first = (v * len(outs) + i) * width
                yield pltpu.make_async_copy(
                    amp_ref.at[t, s, :, pl.ds(first, width)], out.at[o * parts + v], sem
                )

    def start(o, carry):
        for copy in copies(o):
            copy.start()
        return carry

    def wait(o, carry):
        for copy in copies(o):
            copy.wait()
        return carry

    lax.fori_loop(0, owners, start, 0)
    lax.fori_loop(0, owners, wait, 0)


def pack(tile_owner, tile_counts, amplitudes, owners, parts):
    _, _, rows, size = amplitudes.shape
    width = size // parts // CHUNKS
    return pl.pallas_call(
        pack_kernel,
        grid_spec=pltpu.PrefetchScalarGridSpec(
            num_scalar_prefetch=2,
            grid=(1,),
            in_specs=[pl.BlockSpec(memory_space=pl.ANY)],
            out_specs=[pl.BlockSpec(memory_space=pl.ANY)] * CHUNKS,
            scratch_shapes=[pltpu.SMEM((owners,), jnp.int32), pltpu.SemaphoreType.DMA],
        ),
        out_shape=[jax.ShapeDtypeStruct((owners * parts, rows, width), amplitudes.dtype)] * CHUNKS,
        name="pack_first",
    )(tile_owner, tile_counts, amplitudes)


def pack_extra_kernel(pick_ref, amp_ref, out_ref, sem):
    parts, extra, _, width = out_ref.shape
    copies = [
        pltpu.make_async_copy(
            amp_ref.at[1, pick_ref[j], :, pl.ds(v * width, width)], out_ref.at[v, j], sem
        )
        for j in range(extra)
        for v in range(parts)
    ]
    for copy in copies:
        copy.start()
    for copy in copies:
        copy.wait()


def pack_extra(pick, amplitudes, parts):
    _, _, rows, size = amplitudes.shape
    return pl.pallas_call(
        pack_extra_kernel,
        grid_spec=pltpu.PrefetchScalarGridSpec(
            num_scalar_prefetch=1,
            grid=(1,),
            in_specs=[pl.BlockSpec(memory_space=pl.ANY)],
            out_specs=pl.BlockSpec(memory_space=pl.ANY),
            scratch_shapes=[pltpu.SemaphoreType.DMA],
        ),
        out_shape=jax.ShapeDtypeStruct((parts, EXTRA, rows, size // parts), amplitudes.dtype),
        name="pack_extra",
    )(pick, amplitudes)


def ladder_kernel(block_ref, tile_ref, row_ref, count_ref, acc_in_ref, x_ref, panel_ref, acc_ref):
    i = pl.program_id(0)

    @pl.when(i == 0)
    def _():
        acc_ref[...] = acc_in_ref[...]

    @pl.when(i < count_ref[0])
    def _():
        row = row_ref[i]
        acc_ref[row] = acc_ref[row] + jnp.dot(
            x_ref[0], panel_ref[0], preferred_element_type=jnp.float32
        )


def ladder(lists, acc, blocks, panels, chunk):
    block, tile, row, count = lists
    steps = block.shape[0]
    _, rows, width = blocks.shape
    panel_width = panels.shape[2]
    whole = pl.BlockSpec(acc.shape, lambda i, *_: (0, 0, 0))
    return pl.pallas_call(
        ladder_kernel,
        grid_spec=pltpu.PrefetchScalarGridSpec(
            num_scalar_prefetch=4,
            grid=(steps,),
            in_specs=[
                whole,
                pl.BlockSpec((1, rows, width), lambda i, b, t, r, c: (b[i], 0, 0)),
                pl.BlockSpec((1, width, panel_width), lambda i, b, t, r, c: (t[i], chunk, 0)),
            ],
            out_specs=whole,
        ),
        out_shape=jax.ShapeDtypeStruct(acc.shape, jnp.float32),
        input_output_aliases={4: 0},
        compiler_params=pltpu.CompilerParams(vmem_limit_bytes=VMEM_LIMIT),
        cost_estimate=pl.CostEstimate(
            flops=2 * steps * rows * width * panel_width,
            bytes_accessed=2 * steps * width * (rows + panel_width),
            transcendentals=0,
        ),
        name="ladder",
    )(block, tile, row, count, acc, blocks, panels)


def residual_kernel(
    owner_ref,
    local_ref,
    count_ref,
    map_ref,
    amp_ref,
    weight_ref,
    left_ref,
    right_ref,
    out_ref,
    diag_ref,
    rows_ref,
    turned_ref,
):
    slots = owner_ref.shape[1]
    i = pl.program_id(0)
    used = i % slots < count_ref[i // slots]
    _, _, rows, size = amp_ref.shape
    vt = left_ref.shape[1]
    half = vt // 2
    lanes = 2 * vt
    pieces = size // lanes
    wide = diag_ref.shape[0]

    @pl.when(i == 0)
    def _():
        diag_ref[...] = jnp.zeros_like(diag_ref)

    @pl.when(jnp.logical_not(used))
    def _():
        out_ref[...] = jnp.zeros_like(out_ref)

    @pl.when(used)
    def _():
        for k in range(wide // vt):
            diag_ref[k * vt : (k + 1) * vt, k * vt : (k + 1) * vt] = right_ref[0]
        low = lax.broadcasted_iota(jnp.int32, (half, lanes), 1) < vt
        for k in range(pieces):
            rows_ref[pl.ds(k, rows, stride=pieces), :] = amp_ref[
                0, 0, :, k * lanes : (k + 1) * lanes
            ].astype(jnp.float32)
        for j in range(rows // 2):
            even = rows_ref[(2 * j) * pieces : (2 * j + 1) * pieces, :]
            odd = rows_ref[(2 * j + 1) * pieces : (2 * j + 2) * pieces, :]
            top = jnp.where(low, even, pltpu.roll(odd, vt, 1))
            bottom = jnp.where(low, pltpu.roll(even, vt, 1), odd)
            turned_ref[:, j * lanes : (j + 1) * lanes] = jnp.concatenate([top, bottom], 0).astype(
                jnp.bfloat16
            )
        for j in range(rows // 2):
            both = jnp.dot(
                left_ref[0],
                turned_ref[:, j * lanes : (j + 1) * lanes],
                preferred_element_type=jnp.float32,
            )
            top, bottom = both[:half], both[half:]
            rows_ref[(2 * j) * pieces : (2 * j + 1) * pieces, :] = jnp.where(
                low, top, pltpu.roll(bottom, vt, 1)
            )
            rows_ref[(2 * j + 1) * pieces : (2 * j + 2) * pieces, :] = jnp.where(
                low, pltpu.roll(top, vt, 1), bottom
            )
        for j in range(size // wide):
            at = slice(j * wide, (j + 1) * wide)
            block = amp_ref[0, 0, :, at]
            total = jnp.dot(weight_ref[0], block, preferred_element_type=jnp.float32)
            total = total + jnp.dot(block, diag_ref[...], preferred_element_type=jnp.float32)
            for k in range(wide // lanes):
                piece = j * (wide // lanes) + k
                left = rows_ref[pl.ds(piece, rows, stride=pieces), :]
                out_ref[0, 0, :, piece * lanes : (piece + 1) * lanes] = (
                    total[:, k * lanes : (k + 1) * lanes] + left
                ).astype(jnp.bfloat16)


def residual(tile_owner, tile_local, tile_counts, pair_map, amplitudes, hole_weight, fock_tiles, per_owner):
    tiles, slots, rows, size = amplitudes.shape
    tile_count, vt, _ = fock_tiles.shape
    left = fock_tiles.reshape(tile_count, vt // 2, 2, vt // 2, 2).transpose(0, 2, 1, 4, 3)
    left = left.reshape(tile_count, vt, vt)
    wide = 4 * vt

    def ident(i, owner, local, pairs):
        t, s = i // slots, i % slots
        return pairs[owner[t, s] * per_owner + local[t, s]]

    return pl.pallas_call(
        residual_kernel,
        grid_spec=pltpu.PrefetchScalarGridSpec(
            num_scalar_prefetch=4,
            grid=(tiles * slots,),
            in_specs=[
                pl.BlockSpec((1, 1, rows, size), lambda i, *_: (i // slots, i % slots, 0, 0)),
                pl.BlockSpec((1, rows, rows), lambda i, *_: (i // slots, 0, 0)),
                pl.BlockSpec(
                    (1, vt, vt), lambda i, o, l, c, m: (ident(i, o, l, m) // tile_count, 0, 0)
                ),
                pl.BlockSpec(
                    (1, vt, vt), lambda i, o, l, c, m: (ident(i, o, l, m) % tile_count, 0, 0)
                ),
            ],
            out_specs=pl.BlockSpec((1, 1, rows, size), lambda i, *_: (i // slots, i % slots, 0, 0)),
            scratch_shapes=[
                pltpu.VMEM((wide, wide), jnp.bfloat16),
                pltpu.VMEM((rows * size // (2 * vt), 2 * vt), jnp.float32),
                pltpu.VMEM((vt, rows * vt), jnp.bfloat16),
            ],
        ),
        out_shape=jax.ShapeDtypeStruct(amplitudes.shape, jnp.bfloat16),
        compiler_params=pltpu.CompilerParams(vmem_limit_bytes=VMEM_LIMIT),
        cost_estimate=pl.CostEstimate(
            flops=40 * amplitudes.size * vt, bytes_accessed=4 * amplitudes.size, transcendentals=0
        ),
        name="residual",
    )(tile_owner, tile_local, tile_counts, pair_map, amplitudes, hole_weight, left, fock_tiles)


def squeeze_list(valid, *columns):
    length = valid.shape[0]
    at = jnp.arange(length, dtype=jnp.int32)
    ahead = jnp.cumsum(valid.astype(jnp.int32))
    count = ahead[-1]
    wanted = jnp.minimum(at, jnp.maximum(count - 1, 0))
    chosen = (valid[None, :] & (ahead[None, :] - 1 == wanted[:, None])).astype(jnp.int32)
    return [jnp.sum(chosen * c[None, :], axis=1) for c in columns] + [count.reshape(1)]


def per_device(
    amplitudes,
    tile_counts,
    tile_owner,
    tile_local,
    pair_map,
    hole_weight,
    fock_tiles,
    ladder_panels,
):
    owners, parts = lax.axis_size("occ"), lax.axis_size("vir")
    per_owner, part_rows, panel_width = ladder_panels.shape
    tiles, slots, pair_rows, tile_size = amplitudes.shape
    devices = owners * parts
    slot_at = jnp.arange(slots, dtype=jnp.int32)

    sent = pack(tile_owner, tile_counts, amplitudes, owners, parts)

    mine = jnp.concatenate([tile_owner, tile_local, tile_counts[:, None]], axis=1)
    table = lax.all_gather(mine, AXES, axis=0, tiled=True).reshape(devices, tiles, 2 * slots + 1)
    owner, local = table[:, :, :slots], table[:, :, slots : 2 * slots]
    used = slot_at < table[:, :, 2 * slots :]
    repeat = used[:, 1] & jnp.any(
        used[:, 0, :, None] & (owner[:, 0, :, None] == owner[:, 1, None, :]), axis=1
    )
    turn = jnp.cumsum(repeat.astype(jnp.int32), axis=1) - repeat
    rounds = (jnp.max(jnp.sum(repeat, axis=1)) + EXTRA - 1) // EXTRA
    hit = used & (owner == lax.axis_index("occ"))
    named = jnp.any(hit, axis=2)
    tile = jnp.sum(jnp.where(hit, local, 0), axis=2)
    device = jnp.arange(devices, dtype=jnp.int32)
    first = squeeze_list(
        named[:, 0] | named[:, 1],
        device,
        jnp.where(named[:, 0], tile[:, 0], tile[:, 1]),
        jnp.where(named[:, 0], 2 * device, 2 * device + 1),
    )
    doubled = named[:, 0] & named[:, 1]
    my_turn = jnp.sum(jnp.where(hit[:, 1], turn, 0), axis=1)

    my_used = slot_at < tile_counts[:, None]
    my_repeat = my_used[1] & jnp.any(
        my_used[0, :, None] & (tile_owner[0, :, None] == tile_owner[1, None, :]), axis=0
    )
    own_turn = jnp.cumsum(my_repeat.astype(jnp.int32)) - my_repeat

    def extra_blocks(k):
        wanted = k * EXTRA + jnp.arange(EXTRA, dtype=jnp.int32)
        pick = jnp.sum(
            jnp.where(my_repeat & (own_turn == wanted[:, None]), slot_at, 0), axis=1
        ).astype(jnp.int32)
        packed = pack_extra(pick, amplitudes, parts)
        swapped = lax.all_to_all(packed, "vir", split_axis=0, concat_axis=0, tiled=True)
        got = lax.all_gather(swapped, "occ", axis=0, tiled=True)
        return got.reshape(devices * EXTRA, pair_rows, part_rows)

    def extra_list(k):
        return squeeze_list(
            doubled & (my_turn // EXTRA == k),
            device * EXTRA + my_turn % EXTRA,
            tile[:, 1],
            2 * device + 1,
        )

    second = extra_blocks(0)
    arrived = [lax.all_to_all(x, AXES, split_axis=0, concat_axis=0, tiled=True) for x in sent]
    local_residual = residual(
        tile_owner, tile_local, tile_counts, pair_map, amplitudes, hole_weight, fock_tiles, per_owner
    )
    acc = jnp.zeros((devices * tiles, pair_rows, panel_width), jnp.float32)
    acc = ladder(extra_list(0), acc, second, ladder_panels, 0)
    for chunk, blocks in enumerate(arrived):
        acc = ladder(first, acc, blocks, ladder_panels, chunk)

    def more(k, acc):
        return ladder(extra_list(k), acc, extra_blocks(k), ladder_panels, 0)

    acc = lax.fori_loop(1, rounds, more, acc)
    ladder_panel = lax.psum_scatter(acc, AXES, scatter_dimension=0, tiled=True)
    return (local_residual, ladder_panel.astype(jnp.bfloat16))


def solution(mesh):
    in_specs = (
        P(("occ", "vir"), None, None, None),
        P(("occ", "vir")),
        P(("occ", "vir"), None),
        P(("occ", "vir"), None),
        P(),
        P(("occ", "vir"), None, None),
        P(),
        P("occ", "vir", None),
    )
    out_specs = (P(("occ", "vir"), None, None, None), P(("occ", "vir"), None, None))
    return jax.shard_map(
        per_device, mesh=mesh, in_specs=in_specs, out_specs=out_specs, check_vma=False
    )
```

```python
import functools

import jax
import jax.numpy as jnp
from jax import lax
from jax.experimental import pallas as pl
from jax.experimental.pallas import tpu as pltpu
from jax.sharding import PartitionSpec as P

AXES = ("occ", "vir")
EXTRA = 2
VMEM_LIMIT = 48 * 1024 * 1024


def pack_kernel(owner_ref, count_ref, amp_ref, *outs):
    del owner_ref, count_ref
    parts = outs[0].shape[0]
    part = amp_ref.shape[3] // parts
    for v in range(parts):
        first = v * part
        for out in outs:
            width = out.shape[2]
            out[v] = amp_ref[0, 0, :, first : first + width]
            first += width


def pack(tile_owner, tile_counts, amplitudes, owners, parts, widths):
    tiles, slots, rows, size = amplitudes.shape

    def entry(o, owner, count):
        at = 0
        for t in reversed(range(tiles)):
            for s in range(slots):
                named = jnp.logical_and(owner[t, s] == o, s < count[t])
                at = jnp.where(named, t * slots + s, at)
        return at // slots, at % slots, 0, 0

    return pl.pallas_call(
        pack_kernel,
        grid_spec=pltpu.PrefetchScalarGridSpec(
            num_scalar_prefetch=2,
            grid=(owners,),
            in_specs=[pl.BlockSpec((1, 1, rows, size), entry)],
            out_specs=[pl.BlockSpec((parts, rows, w), lambda o, *_: (o, 0, 0)) for w in widths],
        ),
        out_shape=[
            jax.ShapeDtypeStruct((owners * parts, rows, w), amplitudes.dtype) for w in widths
        ],
        name="pack_first",
    )(tile_owner, tile_counts, amplitudes)


def pack_extra_kernel(pick_ref, amp_ref, out_ref):
    del pick_ref
    parts, _, _, width = out_ref.shape
    for v in range(parts):
        out_ref[v, 0] = amp_ref[0, 0, :, v * width : (v + 1) * width]


def pack_extra(pick, amplitudes, parts):
    _, _, rows, size = amplitudes.shape
    width = size // parts
    return pl.pallas_call(
        pack_extra_kernel,
        grid_spec=pltpu.PrefetchScalarGridSpec(
            num_scalar_prefetch=1,
            grid=(EXTRA,),
            in_specs=[pl.BlockSpec((1, 1, rows, size), lambda j, pick: (1, pick[j], 0, 0))],
            out_specs=pl.BlockSpec((parts, 1, rows, width), lambda j, _: (0, j, 0, 0)),
        ),
        out_shape=jax.ShapeDtypeStruct((parts, EXTRA, rows, width), amplitudes.dtype),
        name="pack_extra",
    )(pick, amplitudes)


def ladder_kernel(block_ref, tile_ref, row_ref, count_ref, acc_in_ref, x_ref, panel_ref, acc_ref):
    i = pl.program_id(0)

    @pl.when(i == 0)
    def _():
        acc_ref[...] = acc_in_ref[...]

    @pl.when(i < count_ref[0])
    def _():
        row = row_ref[i]
        acc_ref[row] = acc_ref[row] + jnp.dot(
            x_ref[0], panel_ref[0], preferred_element_type=jnp.float32
        )


def ladder(lists, acc, blocks, panels, chunk):
    block, tile, row, count = lists
    steps = block.shape[0]
    _, rows, width = blocks.shape
    panel_width = panels.shape[2]
    whole = pl.BlockSpec(acc.shape, lambda i, *_: (0, 0, 0))
    return pl.pallas_call(
        ladder_kernel,
        grid_spec=pltpu.PrefetchScalarGridSpec(
            num_scalar_prefetch=4,
            grid=(steps,),
            in_specs=[
                whole,
                pl.BlockSpec((1, rows, width), lambda i, b, t, r, c: (b[i], 0, 0)),
                pl.BlockSpec((1, width, panel_width), lambda i, b, t, r, c: (t[i], chunk, 0)),
            ],
            out_specs=whole,
        ),
        out_shape=jax.ShapeDtypeStruct(acc.shape, jnp.float32),
        input_output_aliases={4: 0},
        compiler_params=pltpu.CompilerParams(vmem_limit_bytes=VMEM_LIMIT),
        cost_estimate=pl.CostEstimate(
            flops=2 * steps * rows * width * panel_width,
            bytes_accessed=2 * steps * width * (rows + panel_width),
            transcendentals=0,
        ),
        name="ladder",
    )(block, tile, row, count, acc, blocks, panels)


def residual_kernel(
    owner_ref,
    local_ref,
    count_ref,
    map_ref,
    amp_ref,
    weight_ref,
    left_ref,
    right_ref,
    out_ref,
    diag_ref,
    rows_ref,
    turned_ref,
):
    slots = owner_ref.shape[1]
    i = pl.program_id(0)
    used = i % slots < count_ref[i // slots]
    _, _, rows, size = amp_ref.shape
    vt = left_ref.shape[1]
    half = vt // 2
    lanes = 2 * vt
    pieces = size // lanes
    wide = diag_ref.shape[0]

    @pl.when(i == 0)
    def _():
        diag_ref[...] = jnp.zeros_like(diag_ref)

    @pl.when(jnp.logical_not(used))
    def _():
        out_ref[...] = jnp.zeros_like(out_ref)

    @pl.when(used)
    def _():
        for k in range(wide // vt):
            diag_ref[k * vt : (k + 1) * vt, k * vt : (k + 1) * vt] = right_ref[0]
        low = lax.broadcasted_iota(jnp.int32, (half, lanes), 1) < vt
        for k in range(pieces):
            rows_ref[pl.ds(k, rows, stride=pieces), :] = amp_ref[
                0, 0, :, k * lanes : (k + 1) * lanes
            ].astype(jnp.float32)
        for j in range(rows // 2):
            even = rows_ref[(2 * j) * pieces : (2 * j + 1) * pieces, :]
            odd = rows_ref[(2 * j + 1) * pieces : (2 * j + 2) * pieces, :]
            top = jnp.where(low, even, pltpu.roll(odd, vt, 1))
            bottom = jnp.where(low, pltpu.roll(even, vt, 1), odd)
            turned_ref[:, j * lanes : (j + 1) * lanes] = jnp.concatenate([top, bottom], 0).astype(
                jnp.bfloat16
            )
        for j in range(rows // 2):
            both = jnp.dot(
                left_ref[0],
                turned_ref[:, j * lanes : (j + 1) * lanes],
                preferred_element_type=jnp.float32,
            )
            top, bottom = both[:half], both[half:]
            rows_ref[(2 * j) * pieces : (2 * j + 1) * pieces, :] = jnp.where(
                low, top, pltpu.roll(bottom, vt, 1)
            )
            rows_ref[(2 * j + 1) * pieces : (2 * j + 2) * pieces, :] = jnp.where(
                low, pltpu.roll(top, vt, 1), bottom
            )
        for j in range(size // wide):
            at = slice(j * wide, (j + 1) * wide)
            block = amp_ref[0, 0, :, at]
            total = jnp.dot(weight_ref[0], block, preferred_element_type=jnp.float32)
            total = total + jnp.dot(block, diag_ref[...], preferred_element_type=jnp.float32)
            for k in range(wide // lanes):
                piece = j * (wide // lanes) + k
                left = rows_ref[pl.ds(piece, rows, stride=pieces), :]
                out_ref[0, 0, :, piece * lanes : (piece + 1) * lanes] = (
                    total[:, k * lanes : (k + 1) * lanes] + left
                ).astype(jnp.bfloat16)


def residual(tile_owner, tile_local, tile_counts, pair_map, amplitudes, hole_weight, fock_tiles, per_owner):
    tiles, slots, rows, size = amplitudes.shape
    tile_count, vt, _ = fock_tiles.shape
    left = fock_tiles.reshape(tile_count, vt // 2, 2, vt // 2, 2).transpose(0, 2, 1, 4, 3)
    left = left.reshape(tile_count, vt, vt)
    wide = 4 * vt

    def ident(i, owner, local, pairs):
        t, s = i // slots, i % slots
        return pairs[owner[t, s] * per_owner + local[t, s]]

    return pl.pallas_call(
        residual_kernel,
        grid_spec=pltpu.PrefetchScalarGridSpec(
            num_scalar_prefetch=4,
            grid=(tiles * slots,),
            in_specs=[
                pl.BlockSpec((1, 1, rows, size), lambda i, *_: (i // slots, i % slots, 0, 0)),
                pl.BlockSpec((1, rows, rows), lambda i, *_: (i // slots, 0, 0)),
                pl.BlockSpec(
                    (1, vt, vt), lambda i, o, l, c, m: (ident(i, o, l, m) // tile_count, 0, 0)
                ),
                pl.BlockSpec(
                    (1, vt, vt), lambda i, o, l, c, m: (ident(i, o, l, m) % tile_count, 0, 0)
                ),
            ],
            out_specs=pl.BlockSpec((1, 1, rows, size), lambda i, *_: (i // slots, i % slots, 0, 0)),
            scratch_shapes=[
                pltpu.VMEM((wide, wide), jnp.bfloat16),
                pltpu.VMEM((rows * size // (2 * vt), 2 * vt), jnp.float32),
                pltpu.VMEM((vt, rows * vt), jnp.bfloat16),
            ],
        ),
        out_shape=jax.ShapeDtypeStruct(amplitudes.shape, jnp.bfloat16),
        compiler_params=pltpu.CompilerParams(vmem_limit_bytes=VMEM_LIMIT),
        cost_estimate=pl.CostEstimate(
            flops=40 * amplitudes.size * vt, bytes_accessed=4 * amplitudes.size, transcendentals=0
        ),
        name="residual",
    )(tile_owner, tile_local, tile_counts, pair_map, amplitudes, hole_weight, left, fock_tiles)


def squeeze_list(valid, *columns):
    length = valid.shape[0]
    at = jnp.arange(length, dtype=jnp.int32)
    ahead = jnp.cumsum(valid.astype(jnp.int32))
    count = ahead[-1]
    wanted = jnp.minimum(at, jnp.maximum(count - 1, 0))
    chosen = (valid[None, :] & (ahead[None, :] - 1 == wanted[:, None])).astype(jnp.int32)
    return [jnp.sum(chosen * c[None, :], axis=1) for c in columns] + [count.reshape(1)]


def per_device(
    amplitudes,
    tile_counts,
    tile_owner,
    tile_local,
    pair_map,
    hole_weight,
    fock_tiles,
    ladder_panels,
):
    owners, parts = lax.axis_size("occ"), lax.axis_size("vir")
    per_owner, part_rows, panel_width = ladder_panels.shape
    tiles, slots, pair_rows, tile_size = amplitudes.shape
    devices = owners * parts
    slot_at = jnp.arange(slots, dtype=jnp.int32)

    mine = jnp.concatenate([tile_owner, tile_local, tile_counts[:, None]], axis=1)
    table = lax.all_gather(mine, AXES, axis=0, tiled=True).reshape(devices, tiles, 2 * slots + 1)
    table, pack_owner = lax.optimization_barrier((table, tile_owner))
    owner, local = table[:, :, :slots], table[:, :, slots : 2 * slots]
    used = slot_at < table[:, :, 2 * slots :]
    repeat = used[:, 1] & jnp.any(
        used[:, 0, :, None] & (owner[:, 0, :, None] == owner[:, 1, None, :]), axis=1
    )
    turn = jnp.cumsum(repeat.astype(jnp.int32), axis=1) - repeat
    rounds = (jnp.max(jnp.sum(repeat, axis=1)) + EXTRA - 1) // EXTRA
    hit = used & (owner == lax.axis_index("occ"))
    named = jnp.any(hit, axis=2)
    tile = jnp.sum(jnp.where(hit, local, 0), axis=2)
    device = jnp.arange(devices, dtype=jnp.int32)
    first = squeeze_list(
        named[:, 0] | named[:, 1],
        device,
        jnp.where(named[:, 0], tile[:, 0], tile[:, 1]),
        device,
    )
    doubled = named[:, 0] & named[:, 1]
    my_turn = jnp.sum(jnp.where(hit[:, 1], turn, 0), axis=1)

    my_used = slot_at < tile_counts[:, None]
    my_repeat = my_used[1] & jnp.any(
        my_used[0, :, None] & (tile_owner[0, :, None] == tile_owner[1, None, :]), axis=0
    )
    own_turn = jnp.cumsum(my_repeat.astype(jnp.int32)) - my_repeat

    def extra_blocks(k):
        wanted = k * EXTRA + jnp.arange(EXTRA, dtype=jnp.int32)
        pick = jnp.sum(
            jnp.where(my_repeat & (own_turn == wanted[:, None]), slot_at, 0), axis=1
        ).astype(jnp.int32)
        packed = pack_extra(pick, amplitudes, parts)
        swapped = lax.all_to_all(packed, "vir", split_axis=0, concat_axis=0, tiled=True)
        got = lax.all_gather(swapped, "occ", axis=0, tiled=True)
        return got.reshape(devices * EXTRA, pair_rows, part_rows)

    def extra_list(k):
        return squeeze_list(
            doubled & (my_turn // EXTRA == k),
            device * EXTRA + my_turn % EXTRA,
            tile[:, 1],
            device,
        )

    second = extra_blocks(0)
    tail = part_rows // 4
    widths = (part_rows - tail, tail)
    sent = pack(pack_owner, tile_counts, amplitudes, owners, parts, widths)
    sent, late_owner = lax.optimization_barrier((sent, tile_owner))
    arrived = [lax.all_to_all(x, AXES, split_axis=0, concat_axis=0, tiled=True) for x in sent]
    local_residual = residual(
        late_owner, tile_local, tile_counts, pair_map, amplitudes, hole_weight, fock_tiles, per_owner
    )
    local_residual, early = lax.optimization_barrier((local_residual, arrived[0]))
    empty = jnp.zeros((devices, pair_rows, panel_width), jnp.float32)
    acc_second = ladder(extra_list(0), empty, second, ladder_panels, 0)

    def more(k, acc):
        return ladder(extra_list(k), acc, extra_blocks(k), ladder_panels, 0)

    acc_second = lax.fori_loop(1, rounds, more, acc_second)
    acc_first = ladder(first, empty, early, ladder_panels, 0)
    acc_first = ladder(first, acc_first, arrived[1], ladder_panels, widths[0] // widths[1])

    def back(x):
        x = lax.all_to_all(x, AXES, split_axis=0, concat_axis=0, tiled=True)
        return jnp.sum(x.reshape(owners, parts, pair_rows, panel_width), axis=1)

    back_second, back_first = back(acc_second), back(acc_first)
    at = jnp.arange(owners, dtype=jnp.int32)
    names = jnp.any(
        my_used[:, :, None] & (tile_owner[:, :, None] == at[None, None, :]), axis=1
    )[:, :, None, None]
    total = [
        jnp.sum(jnp.where(names[0], back_first, 0.0), axis=0),
        jnp.sum(jnp.where(names[1], jnp.where(names[0], back_second, back_first), 0.0), axis=0),
    ]
    return (local_residual, jnp.stack(total).astype(jnp.bfloat16))


def solution(mesh):
    in_specs = (
        P(("occ", "vir"), None, None, None),
        P(("occ", "vir")),
        P(("occ", "vir"), None),
        P(("occ", "vir"), None),
        P(),
        P(("occ", "vir"), None, None),
        P(),
        P("occ", "vir", None),
    )
    out_specs = (P(("occ", "vir"), None, None, None), P(("occ", "vir"), None, None))
    return jax.shard_map(
        per_device, mesh=mesh, in_specs=in_specs, out_specs=out_specs, check_vma=False
    )
```

```python
import functools

import jax
import jax.numpy as jnp
from jax import lax
from jax.experimental import pallas as pl
from jax.experimental.pallas import tpu as pltpu
from jax.sharding import PartitionSpec as P

AXES = ("occ", "vir")
GROUP = 4
MAIN = 4
VMEM_LIMIT = 48 * 1024 * 1024


def pack_kernel(owner_ref, count_ref, first_ref, amp_ref, out_ref):
    del owner_ref, count_ref, first_ref
    _, group, parts, _, _, width = out_ref.shape
    for v in range(parts):
        for j in range(group):
            first = (v * group + j) * width
            out_ref[0, j, v, 0] = amp_ref[0, 0, :, first : first + width]


def pack(tile_owner, tile_counts, first, amplitudes, owners, parts, length):
    tiles, slots, rows, size = amplitudes.shape
    groups = owners // GROUP
    width = size // (GROUP * parts)

    def entry(z, k, owner, count, first):
        at, seen = 0, 0
        for t in range(tiles):
            for s in range(slots):
                named = jnp.logical_and(owner[t, s] // GROUP == z, s < count[t])
                at = jnp.where(jnp.logical_and(named, seen == first[0] + k), t * slots + s, at)
                seen = seen + named.astype(jnp.int32)
        return at // slots, at % slots, 0, 0

    return pl.pallas_call(
        pack_kernel,
        grid_spec=pltpu.PrefetchScalarGridSpec(
            num_scalar_prefetch=3,
            grid=(groups, length),
            in_specs=[pl.BlockSpec((1, 1, rows, size), entry)],
            out_specs=pl.BlockSpec(
                (1, GROUP, parts, 1, rows, width), lambda z, k, *_: (z, 0, 0, k, 0, 0)
            ),
        ),
        out_shape=jax.ShapeDtypeStruct(
            (groups, GROUP, parts, length, rows, width), amplitudes.dtype
        ),
        name="pack",
    )(tile_owner, tile_counts, first, amplitudes)


def ladder_kernel(tile_ref, row_ref, acc_in_ref, x_ref, panel_ref, acc_ref):
    g = pl.program_id(0)
    here = x_ref.shape[0]
    parts, _, rows, _ = acc_ref.shape

    @pl.when(g == 0)
    def _():
        acc_ref[...] = acc_in_ref[...]

    def step(i, carry):
        at = g * here + i

        @pl.when(tile_ref[at] >= 0)
        def _():
            row = row_ref[at]
            value = jnp.dot(
                x_ref[i], panel_ref[tile_ref[at]], preferred_element_type=jnp.float32
            )
            for v in range(parts):
                acc_ref[v, row] = acc_ref[v, row] + value[v * rows : (v + 1) * rows]

        return carry

    lax.fori_loop(0, here, step, 0)


def ladder(tile, row, acc, blocks, panels):
    count, rows, width = blocks.shape
    panel_width = panels.shape[2]
    steps = 4
    whole = pl.BlockSpec(acc.shape, lambda i, *_: (0, 0, 0, 0))
    return pl.pallas_call(
        ladder_kernel,
        grid_spec=pltpu.PrefetchScalarGridSpec(
            num_scalar_prefetch=2,
            grid=(steps,),
            in_specs=[
                whole,
                pl.BlockSpec((count // steps, rows, width), lambda i, *_: (i, 0, 0)),
                pl.BlockSpec(panels.shape, lambda i, *_: (0, 0, 0)),
            ],
            out_specs=whole,
        ),
        out_shape=jax.ShapeDtypeStruct(acc.shape, jnp.float32),
        input_output_aliases={2: 0},
        compiler_params=pltpu.CompilerParams(vmem_limit_bytes=VMEM_LIMIT),
        cost_estimate=pl.CostEstimate(
            flops=2 * count * rows * width * panel_width,
            bytes_accessed=2 * (blocks.size + panels.size),
            transcendentals=0,
        ),
        name="ladder",
    )(tile, row, acc, blocks, panels)


def residual_kernel(
    owner_ref,
    local_ref,
    count_ref,
    map_ref,
    amp_ref,
    weight_ref,
    left_ref,
    right_ref,
    out_ref,
    diag_ref,
    rows_ref,
    turned_ref,
):
    slots = owner_ref.shape[1]
    i = pl.program_id(0)
    used = i % slots < count_ref[i // slots]
    _, _, rows, size = amp_ref.shape
    vt = left_ref.shape[1]
    half = vt // 2
    lanes = 2 * vt
    pieces = size // lanes
    wide = diag_ref.shape[0]

    @pl.when(i == 0)
    def _():
        diag_ref[...] = jnp.zeros_like(diag_ref)

    @pl.when(jnp.logical_not(used))
    def _():
        out_ref[...] = jnp.zeros_like(out_ref)

    @pl.when(used)
    def _():
        for k in range(wide // vt):
            diag_ref[k * vt : (k + 1) * vt, k * vt : (k + 1) * vt] = right_ref[0]
        low = lax.broadcasted_iota(jnp.int32, (half, lanes), 1) < vt
        for k in range(pieces):
            rows_ref[pl.ds(k, rows, stride=pieces), :] = amp_ref[
                0, 0, :, k * lanes : (k + 1) * lanes
            ].astype(jnp.float32)
        for j in range(rows // 2):
            even = rows_ref[(2 * j) * pieces : (2 * j + 1) * pieces, :]
            odd = rows_ref[(2 * j + 1) * pieces : (2 * j + 2) * pieces, :]
            top = jnp.where(low, even, pltpu.roll(odd, vt, 1))
            bottom = jnp.where(low, pltpu.roll(even, vt, 1), odd)
            turned_ref[:, j * lanes : (j + 1) * lanes] = jnp.concatenate([top, bottom], 0).astype(
                jnp.bfloat16
            )
        for j in range(rows // 2):
            both = jnp.dot(
                left_ref[0],
                turned_ref[:, j * lanes : (j + 1) * lanes],
                preferred_element_type=jnp.float32,
            )
            top, bottom = both[:half], both[half:]
            rows_ref[(2 * j) * pieces : (2 * j + 1) * pieces, :] = jnp.where(
                low, top, pltpu.roll(bottom, vt, 1)
            )
            rows_ref[(2 * j + 1) * pieces : (2 * j + 2) * pieces, :] = jnp.where(
                low, pltpu.roll(top, vt, 1), bottom
            )
        for j in range(size // wide):
            at = slice(j * wide, (j + 1) * wide)
            block = amp_ref[0, 0, :, at]
            total = jnp.dot(weight_ref[0], block, preferred_element_type=jnp.float32)
            total = total + jnp.dot(block, diag_ref[...], preferred_element_type=jnp.float32)
            for k in range(wide // lanes):
                piece = j * (wide // lanes) + k
                left = rows_ref[pl.ds(piece, rows, stride=pieces), :]
                out_ref[0, 0, :, piece * lanes : (piece + 1) * lanes] = (
                    total[:, k * lanes : (k + 1) * lanes] + left
                ).astype(jnp.bfloat16)


def residual(tile_owner, tile_local, tile_counts, pair_map, amplitudes, hole_weight, fock_tiles, per_owner):
    tiles, slots, rows, size = amplitudes.shape
    tile_count, vt, _ = fock_tiles.shape
    left = fock_tiles.reshape(tile_count, vt // 2, 2, vt // 2, 2).transpose(0, 2, 1, 4, 3)
    left = left.reshape(tile_count, vt, vt)
    wide = 4 * vt

    def ident(i, owner, local, pairs):
        t, s = i // slots, i % slots
        return pairs[owner[t, s] * per_owner + local[t, s]]

    return pl.pallas_call(
        residual_kernel,
        grid_spec=pltpu.PrefetchScalarGridSpec(
            num_scalar_prefetch=4,
            grid=(tiles * slots,),
            in_specs=[
                pl.BlockSpec((1, 1, rows, size), lambda i, *_: (i // slots, i % slots, 0, 0)),
                pl.BlockSpec((1, rows, rows), lambda i, *_: (i // slots, 0, 0)),
                pl.BlockSpec(
                    (1, vt, vt), lambda i, o, l, c, m: (ident(i, o, l, m) // tile_count, 0, 0)
                ),
                pl.BlockSpec(
                    (1, vt, vt), lambda i, o, l, c, m: (ident(i, o, l, m) % tile_count, 0, 0)
                ),
            ],
            out_specs=pl.BlockSpec((1, 1, rows, size), lambda i, *_: (i // slots, i % slots, 0, 0)),
            scratch_shapes=[
                pltpu.VMEM((wide, wide), jnp.bfloat16),
                pltpu.VMEM((rows * size // (2 * vt), 2 * vt), jnp.float32),
                pltpu.VMEM((vt, rows * vt), jnp.bfloat16),
            ],
        ),
        out_shape=jax.ShapeDtypeStruct(amplitudes.shape, jnp.bfloat16),
        compiler_params=pltpu.CompilerParams(vmem_limit_bytes=VMEM_LIMIT),
        cost_estimate=pl.CostEstimate(
            flops=40 * amplitudes.size * vt, bytes_accessed=4 * amplitudes.size, transcendentals=0
        ),
        name="residual",
    )(tile_owner, tile_local, tile_counts, pair_map, amplitudes, hole_weight, left, fock_tiles)


def per_device(
    amplitudes,
    tile_counts,
    tile_owner,
    tile_local,
    pair_map,
    hole_weight,
    fock_tiles,
    ladder_panels,
):
    owners, parts = lax.axis_size("occ"), lax.axis_size("vir")
    per_owner, part_rows, panel_width = ladder_panels.shape
    tiles, slots, pair_rows, tile_size = amplitudes.shape
    devices = owners * parts
    width = part_rows // GROUP
    me = lax.axis_index("occ")
    place = me % GROUP
    slot_at = jnp.arange(slots, dtype=jnp.int32)

    def columns(k):
        return lax.dynamic_slice_in_dim(ladder_panels, (place ^ k) * width, width, axis=1)

    panels = [columns(0)]
    for k in range(1, GROUP):
        panels.append(lax.ppermute(columns(k), "occ", [(o, o ^ k) for o in range(owners)]))
    panels = jnp.concatenate(panels, axis=0)

    mine = jnp.concatenate([tile_owner, tile_local, tile_counts[:, None]], axis=1)
    table = lax.all_gather(mine, AXES, axis=0, tiled=True)
    table, pack_owner = lax.optimization_barrier((table, tile_owner))
    owner, local = table[:, :slots], table[:, slots : 2 * slots]
    hit = (slot_at < table[:, 2 * slots :]) & (owner // GROUP == me // GROUP)
    hit = hit.reshape(devices, tiles * slots)
    turn = jnp.cumsum(hit.astype(jnp.int32), axis=1) - hit
    tile = (((owner % GROUP) ^ place) * per_owner + local).reshape(devices, tiles * slots)
    row = jnp.arange(devices * tiles, dtype=jnp.int32)[:, None] + jnp.zeros_like(owner)
    row = row.reshape(devices, tiles * slots)
    of_group = (owner // GROUP)[:, :, None] == jnp.arange(owners // GROUP, dtype=jnp.int32)
    of_group = of_group & (slot_at < table[:, 2 * slots :])[:, :, None]
    longest = jnp.max(jnp.sum(of_group.reshape(devices, tiles * slots, -1), axis=1))

    def lists(first, length):
        at = first + jnp.arange(length, dtype=jnp.int32)
        chosen = hit[:, None, :] & (turn[:, None, :] == at[None, :, None])
        tiles_of = jnp.sum(jnp.where(chosen, tile[:, None, :] + 1, 0), axis=2) - 1
        rows_of = jnp.sum(jnp.where(chosen, row[:, None, :], 0), axis=2)
        return tiles_of.reshape(-1), rows_of.reshape(-1)

    def send(packed):
        length = packed.shape[3]
        packed = packed.reshape(devices, length, pair_rows, width)
        return lax.all_to_all(packed, AXES, split_axis=0, concat_axis=0, tiled=True)

    def first_of(k):
        return jnp.full((1,), k, jnp.int32)

    main = pack(pack_owner, tile_counts, first_of(0), amplitudes, owners, parts, MAIN)
    extra = pack(pack_owner, tile_counts, first_of(MAIN), amplitudes, owners, parts, 1)
    main, extra, late_owner = lax.optimization_barrier((main, extra, tile_owner))
    main = send(main)
    local_residual = residual(
        late_owner, tile_local, tile_counts, pair_map, amplitudes, hole_weight, fock_tiles, per_owner
    )
    main, extra, local_residual = lax.optimization_barrier((main, extra, local_residual))
    extra = send(extra)
    acc = jnp.zeros((parts, devices * tiles, pair_rows // parts, panel_width), jnp.float32)

    def add(acc, blocks, first, length):
        tiles_of, rows_of = lists(first, length)
        blocks = blocks.reshape(devices * length, pair_rows, width)
        return ladder(tiles_of, rows_of, acc, blocks, panels)

    acc = add(acc, main, 0, MAIN)
    acc = add(acc, extra, MAIN, 1)

    def more(k, acc):
        packed = pack(tile_owner, tile_counts, k.reshape(1), amplitudes, owners, parts, 1)
        return add(acc, send(packed), k, 1)

    acc = lax.fori_loop(MAIN + 1, longest, more, acc)
    acc = jnp.sum(lax.all_to_all(acc, "vir", split_axis=0, concat_axis=0, tiled=True), axis=0)
    acc = acc.reshape(devices, tiles, pair_rows // parts, panel_width)
    acc = lax.all_to_all(acc, AXES, split_axis=0, concat_axis=0, tiled=True)
    acc = jnp.sum(acc.reshape(owners, parts, tiles, pair_rows // parts, panel_width), axis=0)
    ladder_panel = acc.transpose(1, 0, 2, 3).reshape(tiles, pair_rows, panel_width)
    return (local_residual, ladder_panel.astype(jnp.bfloat16))


def solution(mesh):
    in_specs = (
        P(("occ", "vir"), None, None, None),
        P(("occ", "vir")),
        P(("occ", "vir"), None),
        P(("occ", "vir"), None),
        P(),
        P(("occ", "vir"), None, None),
        P(),
        P("occ", "vir", None),
    )
    out_specs = (P(("occ", "vir"), None, None, None), P(("occ", "vir"), None, None))
    return jax.shard_map(
        per_device, mesh=mesh, in_specs=in_specs, out_specs=out_specs, check_vma=False
    )
```

```python
import functools

import jax
import jax.numpy as jnp
from jax import lax
from jax.experimental import pallas as pl
from jax.experimental.pallas import tpu as pltpu
from jax.sharding import PartitionSpec as P

AXES = ("occ", "vir")
GROUP = 4
MAIN = 4
VMEM_LIMIT = 48 * 1024 * 1024


def pack_kernel(parts, entry_ref, amp_ref, out_ref):
    del entry_ref
    _, group, _, _, across = out_ref.shape
    width = across // parts
    for j in range(group):
        for v in range(parts):
            first = (v * group + j) * width
            out_ref[0, j, 0, :, v * width : (v + 1) * width] = amp_ref[
                0, 0, :, first : first + width
            ]


def pack(entries, amplitudes, parts):
    _, slots, rows, size = amplitudes.shape
    groups, length = entries.shape
    across = size // GROUP
    return pl.pallas_call(
        functools.partial(pack_kernel, parts),
        grid_spec=pltpu.PrefetchScalarGridSpec(
            num_scalar_prefetch=1,
            grid=(groups, length),
            in_specs=[
                pl.BlockSpec(
                    (1, 1, rows, size),
                    lambda z, k, e: (
                        e[z * length + k] // slots,
                        e[z * length + k] % slots,
                        0,
                        0,
                    ),
                )
            ],
            out_specs=pl.BlockSpec(
                (1, GROUP, 1, rows, across), lambda z, k, _: (z, 0, k, 0, 0)
            ),
        ),
        out_shape=jax.ShapeDtypeStruct((groups, GROUP, length, rows, across), amplitudes.dtype),
        cost_estimate=pl.CostEstimate(
            flops=0, bytes_accessed=4 * groups * length * rows * size, transcendentals=0
        ),
        name="pack",
    )(entries.reshape(-1), amplitudes)


def ladder_kernel(tile_ref, row_ref, acc_in_ref, x_ref, panel_ref, acc_ref):
    g = pl.program_id(0)
    here = x_ref.shape[0]
    parts, _, width, _ = panel_ref.shape

    @pl.when(g == 0)
    def _():
        acc_ref[...] = acc_in_ref[...]

    def step(i, carry):
        at = g * here + i
        tile = tile_ref[at]

        @pl.when(tile >= 0)
        def _():
            row = row_ref[at]
            value = acc_ref[row]
            for v in range(parts):
                value = value + jnp.dot(
                    x_ref[i, :, v * width : (v + 1) * width],
                    panel_ref[v, tile],
                    preferred_element_type=jnp.float32,
                )
            acc_ref[row] = value

        return carry

    lax.fori_loop(0, here, step, 0)


def ladder(tile, row, acc, blocks, panels):
    count, rows, across = blocks.shape
    parts, tiles, width, panel_width = panels.shape
    steps = 4
    whole = pl.BlockSpec(acc.shape, lambda i, *_: (0, 0, 0))
    return pl.pallas_call(
        ladder_kernel,
        grid_spec=pltpu.PrefetchScalarGridSpec(
            num_scalar_prefetch=2,
            grid=(steps,),
            in_specs=[
                whole,
                pl.BlockSpec((count // steps, rows, across), lambda i, *_: (i, 0, 0)),
                pl.BlockSpec(
                    panels.shape, lambda i, *_: (0, 0, 0, 0), pipeline_mode=pl.Buffered(1)
                ),
            ],
            out_specs=whole,
        ),
        out_shape=jax.ShapeDtypeStruct(acc.shape, jnp.float32),
        input_output_aliases={2: 0},
        compiler_params=pltpu.CompilerParams(vmem_limit_bytes=VMEM_LIMIT),
        cost_estimate=pl.CostEstimate(
            flops=2 * count * rows * across * panel_width,
            bytes_accessed=2 * (blocks.size + panels.size),
            transcendentals=0,
        ),
        name="ladder",
    )(tile, row, acc, blocks, panels)


def residual_kernel(
    owner_ref,
    local_ref,
    count_ref,
    map_ref,
    amp_ref,
    weight_ref,
    left_ref,
    right_ref,
    out_ref,
    diag_ref,
    rows_ref,
    turned_ref,
):
    slots = owner_ref.shape[1]
    i = pl.program_id(0)
    used = i % slots < count_ref[i // slots]
    _, _, rows, size = amp_ref.shape
    vt = left_ref.shape[1]
    half = vt // 2
    lanes = 2 * vt
    pieces = size // lanes
    wide = diag_ref.shape[0]

    @pl.when(i == 0)
    def _():
        diag_ref[...] = jnp.zeros_like(diag_ref)

    @pl.when(jnp.logical_not(used))
    def _():
        out_ref[...] = jnp.zeros_like(out_ref)

    @pl.when(used)
    def _():
        for k in range(wide // vt):
            diag_ref[k * vt : (k + 1) * vt, k * vt : (k + 1) * vt] = right_ref[0]
        low = lax.broadcasted_iota(jnp.int32, (half, lanes), 1) < vt
        for k in range(pieces):
            rows_ref[pl.ds(k, rows, stride=pieces), :] = amp_ref[
                0, 0, :, k * lanes : (k + 1) * lanes
            ].astype(jnp.float32)
        for j in range(rows // 2):
            even = rows_ref[(2 * j) * pieces : (2 * j + 1) * pieces, :]
            odd = rows_ref[(2 * j + 1) * pieces : (2 * j + 2) * pieces, :]
            top = jnp.where(low, even, pltpu.roll(odd, vt, 1))
            bottom = jnp.where(low, pltpu.roll(even, vt, 1), odd)
            turned_ref[:, j * lanes : (j + 1) * lanes] = jnp.concatenate([top, bottom], 0).astype(
                jnp.bfloat16
            )
        for j in range(rows // 2):
            both = jnp.dot(
                left_ref[0],
                turned_ref[:, j * lanes : (j + 1) * lanes],
                preferred_element_type=jnp.float32,
            )
            top, bottom = both[:half], both[half:]
            rows_ref[(2 * j) * pieces : (2 * j + 1) * pieces, :] = jnp.where(
                low, top, pltpu.roll(bottom, vt, 1)
            )
            rows_ref[(2 * j + 1) * pieces : (2 * j + 2) * pieces, :] = jnp.where(
                low, pltpu.roll(top, vt, 1), bottom
            )
        for j in range(size // wide):
            at = slice(j * wide, (j + 1) * wide)
            block = amp_ref[0, 0, :, at]
            total = jnp.dot(weight_ref[0], block, preferred_element_type=jnp.float32)
            total = total + jnp.dot(block, diag_ref[...], preferred_element_type=jnp.float32)
            for k in range(wide // lanes):
                piece = j * (wide // lanes) + k
                left = rows_ref[pl.ds(piece, rows, stride=pieces), :]
                out_ref[0, 0, :, piece * lanes : (piece + 1) * lanes] = (
                    total[:, k * lanes : (k + 1) * lanes] + left
                ).astype(jnp.bfloat16)


def residual(tile_owner, tile_local, tile_counts, pair_map, amplitudes, hole_weight, fock_tiles, per_owner):
    tiles, slots, rows, size = amplitudes.shape
    tile_count, vt, _ = fock_tiles.shape
    left = fock_tiles.reshape(tile_count, vt // 2, 2, vt // 2, 2).transpose(0, 2, 1, 4, 3)
    left = left.reshape(tile_count, vt, vt)
    wide = 4 * vt

    def ident(i, owner, local, pairs):
        t, s = i // slots, i % slots
        return pairs[owner[t, s] * per_owner + local[t, s]]

    return pl.pallas_call(
        residual_kernel,
        grid_spec=pltpu.PrefetchScalarGridSpec(
            num_scalar_prefetch=4,
            grid=(tiles * slots,),
            in_specs=[
                pl.BlockSpec((1, 1, rows, size), lambda i, *_: (i // slots, i % slots, 0, 0)),
                pl.BlockSpec((1, rows, rows), lambda i, *_: (i // slots, 0, 0)),
                pl.BlockSpec(
                    (1, vt, vt), lambda i, o, l, c, m: (ident(i, o, l, m) // tile_count, 0, 0)
                ),
                pl.BlockSpec(
                    (1, vt, vt), lambda i, o, l, c, m: (ident(i, o, l, m) % tile_count, 0, 0)
                ),
            ],
            out_specs=pl.BlockSpec((1, 1, rows, size), lambda i, *_: (i // slots, i % slots, 0, 0)),
            scratch_shapes=[
                pltpu.VMEM((wide, wide), jnp.bfloat16),
                pltpu.VMEM((rows * size // (2 * vt), 2 * vt), jnp.float32),
                pltpu.VMEM((vt, rows * vt), jnp.bfloat16),
            ],
        ),
        out_shape=jax.ShapeDtypeStruct(amplitudes.shape, jnp.bfloat16),
        compiler_params=pltpu.CompilerParams(vmem_limit_bytes=VMEM_LIMIT),
        cost_estimate=pl.CostEstimate(
            flops=40 * amplitudes.size * vt, bytes_accessed=4 * amplitudes.size, transcendentals=0
        ),
        name="residual",
    )(tile_owner, tile_local, tile_counts, pair_map, amplitudes, hole_weight, left, fock_tiles)


def per_device(
    amplitudes,
    tile_counts,
    tile_owner,
    tile_local,
    pair_map,
    hole_weight,
    fock_tiles,
    ladder_panels,
):
    owners, parts = lax.axis_size("occ"), lax.axis_size("vir")
    per_owner, part_rows, panel_width = ladder_panels.shape
    tiles, slots, pair_rows, tile_size = amplitudes.shape
    groups = owners // GROUP
    width = part_rows // GROUP
    across = parts * width
    me = lax.axis_index("occ")
    place = me % GROUP
    slot_at = jnp.arange(slots, dtype=jnp.int32)
    group_at = jnp.arange(groups, dtype=jnp.int32)

    mine = jnp.concatenate([tile_owner, tile_local, tile_counts[:, None]], axis=1)
    table = lax.all_to_all(
        jnp.broadcast_to(mine, (owners * parts,) + mine.shape), AXES, 0, 0, tiled=True
    )
    named = (slot_at < tile_counts[:, None])[None] & (tile_owner // GROUP == group_at[:, None, None])
    named = named.reshape(groups, tiles * slots)
    own_turn = jnp.cumsum(named.astype(jnp.int32), axis=1) - named
    entry_at = jnp.arange(tiles * slots, dtype=jnp.int32)

    def entries(first, length):
        at = first + jnp.arange(length, dtype=jnp.int32)
        chosen = named[:, None, :] & (own_turn[:, None, :] == at[None, :, None])
        return jnp.sum(jnp.where(chosen, entry_at, 0), axis=2).astype(jnp.int32)

    def send(packed):
        packed = packed.reshape((owners,) + packed.shape[2:])
        return lax.all_to_all(packed, "occ", split_axis=0, concat_axis=0, tiled=True)

    most = tiles * GROUP
    main = pack(entries(0, MAIN), amplitudes, parts)
    main, table, late = lax.optimization_barrier((main, table, amplitudes))
    main = send(main)

    def columns(k):
        return lax.dynamic_slice_in_dim(ladder_panels, (place ^ k) * width, width, axis=1)

    shared = [columns(0)]
    for k in range(1, GROUP):
        shared.append(lax.ppermute(columns(k), "occ", [(o, o ^ k) for o in range(owners)]))
    shared = jnp.concatenate(shared, axis=0)
    panels = lax.all_gather(shared, "vir", axis=0, tiled=False)

    local_residual = residual(
        tile_owner, tile_local, tile_counts, pair_map, late, hole_weight, fock_tiles, per_owner
    )
    extras = [pack(entries(MAIN, length), late, parts) for length in (1, 2)]

    used = slot_at < table[:, :, 2 * slots :]
    owner, local = table[:, :, :slots], table[:, :, slots : 2 * slots]
    of_group = used[..., None] & ((owner // GROUP)[..., None] == group_at)
    longest = jnp.max(jnp.sum(of_group, axis=(1, 2)))

    def of_core(x):
        x = x.reshape(owners, parts, tiles, slots)
        x = lax.dynamic_index_in_dim(x, lax.axis_index("vir"), axis=1, keepdims=False)
        return x.reshape(owners, tiles * slots)

    hit = of_core(used & (owner // GROUP == me // GROUP))
    turn = jnp.cumsum(hit.astype(jnp.int32), axis=1) - hit
    tile = of_core(((owner % GROUP) ^ place) * per_owner + local)
    row = jnp.arange(owners, dtype=jnp.int32)[:, None] * tiles + entry_at // slots

    def lists(first, length):
        at = first + jnp.arange(length, dtype=jnp.int32)
        chosen = hit[:, None, :] & (turn[:, None, :] == at[None, :, None])
        tiles_of = jnp.sum(jnp.where(chosen, tile[:, None, :] + 1, 0), axis=2) - 1
        rows_of = jnp.sum(jnp.where(chosen, row[:, None, :], 0), axis=2)
        return tiles_of.reshape(-1), rows_of.reshape(-1)

    def add(acc, blocks, lists_of, panels):
        return ladder(*lists_of, acc, blocks.reshape(-1, pair_rows, across), panels)

    main, extras, local_residual, _ = lax.optimization_barrier(
        (main, extras, local_residual, shared)
    )
    empty = jnp.zeros((owners * tiles, pair_rows, panel_width), jnp.float32)
    main_lists = lists(0, MAIN)
    extra_lists = [lists(MAIN, length) for length in range(1, most - MAIN + 1)]
    extra_entries = [entries(MAIN, length) for length in range(3, most - MAIN + 1)]

    def none(main, panels, lists_of, extra_lists, extras, extra_entries, amplitudes):
        return add(empty, main, lists_of, panels)

    def some(length, main, panels, lists_of, extra_lists, extras, extra_entries, amplitudes):
        if length <= len(extras):
            packed = extras[length - 1]
        else:
            packed = pack(extra_entries[length - 1 - len(extras)], amplitudes, parts)
        blocks = send(packed)
        acc = add(empty, main, lists_of, panels)
        return add(acc, blocks, extra_lists[length - 1], panels)

    branches = [none] + [functools.partial(some, n) for n in range(1, most - MAIN + 1)]
    acc = lax.switch(
        jnp.maximum(longest - MAIN, 0),
        branches,
        main,
        panels,
        main_lists,
        extra_lists,
        extras,
        extra_entries,
        amplitudes,
    )
    acc = acc.reshape(owners, tiles, pair_rows, panel_width)
    acc = lax.all_to_all(acc, "occ", split_axis=0, concat_axis=0, tiled=True)
    ladder_panel = jnp.sum(acc, axis=0).astype(jnp.bfloat16)
    return (local_residual, ladder_panel)


def solution(mesh):
    in_specs = (
        P(("occ", "vir"), None, None, None),
        P(("occ", "vir")),
        P(("occ", "vir"), None),
        P(("occ", "vir"), None),
        P(),
        P(("occ", "vir"), None, None),
        P(),
        P("occ", "vir", None),
    )
    out_specs = (P(("occ", "vir"), None, None, None), P(("occ", "vir"), None, None))
    return jax.shard_map(
        per_device, mesh=mesh, in_specs=in_specs, out_specs=out_specs, check_vma=False
    )
```

```python
import functools

import jax
import jax.numpy as jnp
from jax import lax
from jax.experimental import pallas as pl
from jax.experimental.pallas import tpu as pltpu
from jax.sharding import PartitionSpec as P

AXES = ("occ", "vir")
GROUP = 4
MAIN = 4
VMEM_LIMIT = 48 * 1024 * 1024


def pack_kernel(parts, entry_ref, amp_ref, out_ref):
    del entry_ref
    _, group, _, _, across = out_ref.shape
    width = across // parts
    for j in range(group):
        for v in range(parts):
            first = (v * group + j) * width
            out_ref[0, j, 0, :, v * width : (v + 1) * width] = amp_ref[
                0, 0, :, first : first + width
            ]


def pack(entries, amplitudes, parts):
    _, slots, rows, size = amplitudes.shape
    groups, length = entries.shape
    across = size // GROUP
    return pl.pallas_call(
        functools.partial(pack_kernel, parts),
        grid_spec=pltpu.PrefetchScalarGridSpec(
            num_scalar_prefetch=1,
            grid=(groups, length),
            in_specs=[
                pl.BlockSpec(
                    (1, 1, rows, size),
                    lambda z, k, e: (
                        e[z * length + k] // slots,
                        e[z * length + k] % slots,
                        0,
                        0,
                    ),
                )
            ],
            out_specs=pl.BlockSpec(
                (1, GROUP, 1, rows, across), lambda z, k, _: (z, 0, k, 0, 0)
            ),
        ),
        out_shape=jax.ShapeDtypeStruct((groups, GROUP, length, rows, across), amplitudes.dtype),
        cost_estimate=pl.CostEstimate(
            flops=0, bytes_accessed=4 * groups * length * rows * size, transcendentals=0
        ),
        name="pack",
    )(entries.reshape(-1), amplitudes)


def ladder_kernel(tile_ref, row_ref, part_ref, acc_in_ref, x_ref, *refs):
    panel_refs, acc_ref = refs[:-1], refs[-1]
    g = pl.program_id(0)
    here = x_ref.shape[0]
    width = panel_refs[0].shape[1]

    @pl.when(g == 0)
    def _():
        acc_ref[...] = acc_in_ref[...]

    def step(i, carry):
        at = g * here + i
        tile = tile_ref[at]

        @pl.when(tile >= 0)
        def _():
            row = row_ref[at]
            value = acc_ref[row]
            for r, panel_ref in enumerate(panel_refs):
                first = pl.multiple_of(part_ref[r] * width, width)
                value = value + jnp.dot(
                    x_ref[i, :, pl.ds(first, width)],
                    panel_ref[tile],
                    preferred_element_type=jnp.float32,
                )
            acc_ref[row] = value

        return carry

    lax.fori_loop(0, here, step, 0)


def ladder(lists, acc, blocks, parts, panels):
    tile, row = lists
    count, rows, across = blocks.shape
    steps = 4
    whole = pl.BlockSpec(acc.shape, lambda i, *_: (0, 0, 0))
    return pl.pallas_call(
        ladder_kernel,
        grid_spec=pltpu.PrefetchScalarGridSpec(
            num_scalar_prefetch=3,
            grid=(steps,),
            in_specs=[whole, pl.BlockSpec((count // steps, rows, across), lambda i, *_: (i, 0, 0))]
            + [
                pl.BlockSpec(x.shape, lambda i, *_: (0, 0, 0), pipeline_mode=pl.Buffered(1))
                for x in panels
            ],
            out_specs=whole,
        ),
        out_shape=jax.ShapeDtypeStruct(acc.shape, jnp.float32),
        input_output_aliases={3: 0},
        compiler_params=pltpu.CompilerParams(vmem_limit_bytes=VMEM_LIMIT),
        cost_estimate=pl.CostEstimate(
            flops=2 * len(panels) * count * rows * panels[0].shape[1] * acc.shape[2],
            bytes_accessed=2 * (blocks.size + sum(x.size for x in panels)),
            transcendentals=0,
        ),
        name="ladder",
    )(tile, row, parts, acc, blocks, *panels)


def few_kernel(at_ref, tile_ref, row_ref, count_ref, part_ref, acc_in_ref, x_ref, *refs):
    del at_ref, tile_ref
    panel_refs, acc_ref = refs[:-1], refs[-1]
    i = pl.program_id(0)
    width = panel_refs[0].shape[1]

    @pl.when(i == 0)
    def _():
        acc_ref[...] = acc_in_ref[...]

    @pl.when(i < count_ref[0])
    def _():
        row = row_ref[i]
        value = acc_ref[row]
        for r, panel_ref in enumerate(panel_refs):
            first = pl.multiple_of(part_ref[r] * width, width)
            value = value + jnp.dot(
                x_ref[0, :, pl.ds(first, width)],
                panel_ref[0],
                preferred_element_type=jnp.float32,
            )
        acc_ref[row] = value


def ladder_few(lists, acc, blocks, parts, panels):
    at, tile, row, count = lists
    _, rows, across = blocks.shape
    whole = pl.BlockSpec(acc.shape, lambda i, *_: (0, 0, 0))
    _, width, panel_width = panels[0].shape
    return pl.pallas_call(
        few_kernel,
        grid_spec=pltpu.PrefetchScalarGridSpec(
            num_scalar_prefetch=5,
            grid=(at.shape[0],),
            in_specs=[
                whole,
                pl.BlockSpec((1, rows, across), lambda i, at, *_: (at[i], 0, 0)),
            ]
            + [
                pl.BlockSpec((1, width, panel_width), lambda i, at, tile, *_: (tile[i], 0, 0))
                for _ in panels
            ],
            out_specs=whole,
        ),
        out_shape=jax.ShapeDtypeStruct(acc.shape, jnp.float32),
        input_output_aliases={5: 0},
        compiler_params=pltpu.CompilerParams(vmem_limit_bytes=VMEM_LIMIT),
        name="ladder_few",
    )(at, tile, row, count, parts, acc, blocks, *panels)


def squeeze(tile, row):
    length = tile.shape[0]
    at = jnp.arange(length, dtype=jnp.int32)
    valid = tile >= 0
    ahead = jnp.cumsum(valid.astype(jnp.int32))
    count = ahead[-1]
    wanted = jnp.minimum(at, jnp.maximum(count - 1, 0))
    chosen = (valid[None, :] & (ahead[None, :] - 1 == wanted[:, None])).astype(jnp.int32)
    return [jnp.sum(chosen * c[None, :], axis=1) for c in (at, tile, row)] + [count.reshape(1)]


def residual_kernel(
    owner_ref,
    local_ref,
    count_ref,
    map_ref,
    amp_ref,
    weight_ref,
    left_ref,
    right_ref,
    out_ref,
    diag_ref,
    rows_ref,
    turned_ref,
):
    slots = owner_ref.shape[1]
    i = pl.program_id(0)
    used = i % slots < count_ref[i // slots]
    _, _, rows, size = amp_ref.shape
    vt = left_ref.shape[1]
    half = vt // 2
    lanes = 2 * vt
    pieces = size // lanes
    wide = diag_ref.shape[0]

    @pl.when(i == 0)
    def _():
        diag_ref[...] = jnp.zeros_like(diag_ref)

    @pl.when(jnp.logical_not(used))
    def _():
        out_ref[...] = jnp.zeros_like(out_ref)

    @pl.when(used)
    def _():
        for k in range(wide // vt):
            diag_ref[k * vt : (k + 1) * vt, k * vt : (k + 1) * vt] = right_ref[0]
        low = lax.broadcasted_iota(jnp.int32, (half, lanes), 1) < vt
        for k in range(pieces):
            rows_ref[pl.ds(k, rows, stride=pieces), :] = amp_ref[
                0, 0, :, k * lanes : (k + 1) * lanes
            ].astype(jnp.float32)
        for j in range(rows // 2):
            even = rows_ref[(2 * j) * pieces : (2 * j + 1) * pieces, :]
            odd = rows_ref[(2 * j + 1) * pieces : (2 * j + 2) * pieces, :]
            top = jnp.where(low, even, pltpu.roll(odd, vt, 1))
            bottom = jnp.where(low, pltpu.roll(even, vt, 1), odd)
            turned_ref[:, j * lanes : (j + 1) * lanes] = jnp.concatenate([top, bottom], 0).astype(
                jnp.bfloat16
            )
        for j in range(rows // 2):
            both = jnp.dot(
                left_ref[0],
                turned_ref[:, j * lanes : (j + 1) * lanes],
                preferred_element_type=jnp.float32,
            )
            top, bottom = both[:half], both[half:]
            rows_ref[(2 * j) * pieces : (2 * j + 1) * pieces, :] = jnp.where(
                low, top, pltpu.roll(bottom, vt, 1)
            )
            rows_ref[(2 * j + 1) * pieces : (2 * j + 2) * pieces, :] = jnp.where(
                low, pltpu.roll(top, vt, 1), bottom
            )
        for j in range(size // wide):
            at = slice(j * wide, (j + 1) * wide)
            block = amp_ref[0, 0, :, at]
            total = jnp.dot(weight_ref[0], block, preferred_element_type=jnp.float32)
            total = total + jnp.dot(block, diag_ref[...], preferred_element_type=jnp.float32)
            for k in range(wide // lanes):
                piece = j * (wide // lanes) + k
                left = rows_ref[pl.ds(piece, rows, stride=pieces), :]
                out_ref[0, 0, :, piece * lanes : (piece + 1) * lanes] = (
                    total[:, k * lanes : (k + 1) * lanes] + left
                ).astype(jnp.bfloat16)


def residual(tile_owner, tile_local, tile_counts, pair_map, amplitudes, hole_weight, fock_tiles, per_owner):
    tiles, slots, rows, size = amplitudes.shape
    tile_count, vt, _ = fock_tiles.shape
    left = fock_tiles.reshape(tile_count, vt // 2, 2, vt // 2, 2).transpose(0, 2, 1, 4, 3)
    left = left.reshape(tile_count, vt, vt)
    wide = 4 * vt

    def ident(i, owner, local, pairs):
        t, s = i // slots, i % slots
        return pairs[owner[t, s] * per_owner + local[t, s]]

    return pl.pallas_call(
        residual_kernel,
        grid_spec=pltpu.PrefetchScalarGridSpec(
            num_scalar_prefetch=4,
            grid=(tiles * slots,),
            in_specs=[
                pl.BlockSpec((1, 1, rows, size), lambda i, *_: (i // slots, i % slots, 0, 0)),
                pl.BlockSpec((1, rows, rows), lambda i, *_: (i // slots, 0, 0)),
                pl.BlockSpec(
                    (1, vt, vt), lambda i, o, l, c, m: (ident(i, o, l, m) // tile_count, 0, 0)
                ),
                pl.BlockSpec(
                    (1, vt, vt), lambda i, o, l, c, m: (ident(i, o, l, m) % tile_count, 0, 0)
                ),
            ],
            out_specs=pl.BlockSpec((1, 1, rows, size), lambda i, *_: (i // slots, i % slots, 0, 0)),
            scratch_shapes=[
                pltpu.VMEM((wide, wide), jnp.bfloat16),
                pltpu.VMEM((rows * size // (2 * vt), 2 * vt), jnp.float32),
                pltpu.VMEM((vt, rows * vt), jnp.bfloat16),
            ],
        ),
        out_shape=jax.ShapeDtypeStruct(amplitudes.shape, jnp.bfloat16),
        compiler_params=pltpu.CompilerParams(vmem_limit_bytes=VMEM_LIMIT),
        cost_estimate=pl.CostEstimate(
            flops=40 * amplitudes.size * vt, bytes_accessed=4 * amplitudes.size, transcendentals=0
        ),
        name="residual",
    )(tile_owner, tile_local, tile_counts, pair_map, amplitudes, hole_weight, left, fock_tiles)


def per_device(
    amplitudes,
    tile_counts,
    tile_owner,
    tile_local,
    pair_map,
    hole_weight,
    fock_tiles,
    ladder_panels,
):
    owners, parts = lax.axis_size("occ"), lax.axis_size("vir")
    per_owner, part_rows, panel_width = ladder_panels.shape
    tiles, slots, pair_rows, tile_size = amplitudes.shape
    groups = owners // GROUP
    width = part_rows // GROUP
    across = parts * width
    me = lax.axis_index("occ")
    place = me % GROUP
    slot_at = jnp.arange(slots, dtype=jnp.int32)
    group_at = jnp.arange(groups, dtype=jnp.int32)

    mine = jnp.concatenate([tile_owner, tile_local, tile_counts[:, None]], axis=1)
    table = lax.all_to_all(
        jnp.broadcast_to(mine, (owners * parts,) + mine.shape), AXES, 0, 0, tiled=True
    )
    named = (slot_at < tile_counts[:, None])[None] & (tile_owner // GROUP == group_at[:, None, None])
    named = named.reshape(groups, tiles * slots)
    own_turn = jnp.cumsum(named.astype(jnp.int32), axis=1) - named
    entry_at = jnp.arange(tiles * slots, dtype=jnp.int32)

    def entries(first, length):
        at = first + jnp.arange(length, dtype=jnp.int32)
        chosen = named[:, None, :] & (own_turn[:, None, :] == at[None, :, None])
        return jnp.sum(jnp.where(chosen, entry_at, 0), axis=2).astype(jnp.int32)

    def send(packed):
        packed = packed.reshape((owners,) + packed.shape[2:])
        return lax.all_to_all(packed, "occ", split_axis=0, concat_axis=0, tiled=True)

    most = tiles * GROUP
    main = pack(entries(0, MAIN), amplitudes, parts)
    main, table, late = lax.optimization_barrier((main, table, amplitudes))
    main = send(main)

    def columns(k):
        return lax.dynamic_slice_in_dim(ladder_panels, (place ^ k) * width, width, axis=1)

    shared = [columns(0)]
    for k in range(1, GROUP):
        shared.append(lax.ppermute(columns(k), "occ", [(o, o ^ k) for o in range(owners)]))
    local_residual = residual(
        tile_owner, tile_local, tile_counts, pair_map, late, hole_weight, fock_tiles, per_owner
    )
    extras = [pack(entries(MAIN, length), late, parts) for length in (1, 2)]

    used = slot_at < table[:, :, 2 * slots :]
    owner, local = table[:, :, :slots], table[:, :, slots : 2 * slots]
    of_group = used[..., None] & ((owner // GROUP)[..., None] == group_at)
    longest = jnp.max(jnp.sum(of_group, axis=(1, 2)))

    def of_core(x):
        x = x.reshape(owners, parts, tiles, slots)
        x = lax.dynamic_index_in_dim(x, lax.axis_index("vir"), axis=1, keepdims=False)
        return x.reshape(owners, tiles * slots)

    hit = of_core(used & (owner // GROUP == me // GROUP))
    turn = jnp.cumsum(hit.astype(jnp.int32), axis=1) - hit
    tile = of_core(((owner % GROUP) ^ place) * per_owner + local)
    row = jnp.arange(owners, dtype=jnp.int32)[:, None] * tiles + entry_at // slots

    def lists(first, length):
        at = first + jnp.arange(length, dtype=jnp.int32)
        chosen = hit[:, None, :] & (turn[:, None, :] == at[None, :, None])
        tiles_of = jnp.sum(jnp.where(chosen, tile[:, None, :] + 1, 0), axis=2) - 1
        rows_of = jnp.sum(jnp.where(chosen, row[:, None, :], 0), axis=2)
        return tiles_of.reshape(-1), rows_of.reshape(-1)

    main, extras, local_residual, shared = lax.optimization_barrier(
        (main, extras, local_residual, shared)
    )
    empty = jnp.zeros((owners * tiles, pair_rows, panel_width), jnp.float32)
    main_lists = lists(0, MAIN)
    extra_lists = [squeeze(*lists(MAIN, length)) for length in range(1, most - MAIN + 1)]
    extra_entries = [entries(MAIN, length) for length in range(3, most - MAIN + 1)]
    core_parts = (lax.axis_index("vir") + jnp.arange(parts, dtype=jnp.int32)) % parts

    def some(length, main, shared, main_lists, extra_lists, extras, extra_entries, amplitudes):
        if length > len(extras):
            packed = pack(extra_entries[length - 1 - len(extras)], amplitudes, parts)
        elif length > 0:
            packed = extras[length - 1]
        if length > 0:
            blocks = send(packed).reshape(-1, pair_rows, across)
        panels = [jnp.concatenate(shared, axis=0)]
        for r in range(1, parts):
            back = [(v, (v - r) % parts) for v in range(parts)]
            panels.append(lax.ppermute(panels[0], "vir", back))
        main = main.reshape(-1, pair_rows, across)
        acc = ladder(main_lists, empty, main, core_parts[:1], panels[:1])
        if parts > 1:
            acc = ladder(main_lists, acc, main, core_parts[1:], panels[1:])
        if length > 0:
            acc = ladder_few(extra_lists[length - 1], acc, blocks, core_parts, panels)
        return acc

    acc = lax.switch(
        jnp.maximum(longest - MAIN, 0),
        [functools.partial(some, length) for length in range(most - MAIN + 1)],
        main,
        shared,
        main_lists,
        extra_lists,
        extras,
        extra_entries,
        amplitudes,
    )
    acc = acc.reshape(owners, tiles, pair_rows, panel_width)
    acc = lax.all_to_all(acc, "occ", split_axis=0, concat_axis=0, tiled=True)
    ladder_panel = jnp.sum(acc, axis=0).astype(jnp.bfloat16)
    return (local_residual, ladder_panel)


def solution(mesh):
    in_specs = (
        P(("occ", "vir"), None, None, None),
        P(("occ", "vir")),
        P(("occ", "vir"), None),
        P(("occ", "vir"), None),
        P(),
        P(("occ", "vir"), None, None),
        P(),
        P("occ", "vir", None),
    )
    out_specs = (P(("occ", "vir"), None, None, None), P(("occ", "vir"), None, None))
    return jax.shard_map(
        per_device, mesh=mesh, in_specs=in_specs, out_specs=out_specs, check_vma=False
    )
```

```python
import functools

import jax
import jax.numpy as jnp
from jax import lax
from jax.experimental import pallas as pl
from jax.experimental.pallas import tpu as pltpu
from jax.sharding import PartitionSpec as P

AXES = ("occ", "vir")
GROUP = 4
MAIN = 4
VMEM_LIMIT = 48 * 1024 * 1024


def pack_kernel(parts, entry_ref, amp_ref, out_ref, block_ref, in_sem, out_sem):
    groups, group, length, _, across = out_ref.shape
    slots = amp_ref.shape[1]
    width = across // parts

    def fetch(i):
        entry = jnp.maximum(entry_ref[i], 0)
        source = amp_ref.at[entry // slots, entry % slots]
        return pltpu.make_async_copy(source, block_ref.at[i], in_sem.at[i])

    def leave(i):
        return [
            pltpu.make_async_copy(
                block_ref.at[i, :, pl.ds((v * group + j) * width, width)],
                out_ref.at[i // length, j, i % length, :, pl.ds(v * width, width)],
                out_sem.at[i],
            )
            for j in range(group)
            for v in range(parts)
        ]

    def each(act):
        def step(i, carry):
            pl.when(entry_ref[i] >= 0)(lambda: act(i))
            return carry

        lax.fori_loop(0, groups * length, step, 0)

    def turn(i):
        fetch(i).wait()
        for copy in leave(i):
            copy.start()

    def finish(i):
        for copy in leave(i):
            copy.wait()

    each(lambda i: fetch(i).start())
    each(turn)
    each(finish)


def pack(entries, amplitudes, parts):
    _, slots, rows, size = amplitudes.shape
    groups, length = entries.shape
    across = size // GROUP
    return pl.pallas_call(
        functools.partial(pack_kernel, parts),
        grid_spec=pltpu.PrefetchScalarGridSpec(
            num_scalar_prefetch=1,
            grid=(1,),
            in_specs=[pl.BlockSpec(memory_space=pl.ANY)],
            out_specs=pl.BlockSpec(memory_space=pl.ANY),
            scratch_shapes=[
                pltpu.VMEM((groups * length, rows, size), amplitudes.dtype),
                pltpu.SemaphoreType.DMA((groups * length,)),
                pltpu.SemaphoreType.DMA((groups * length,)),
            ],
        ),
        out_shape=jax.ShapeDtypeStruct((groups, GROUP, length, rows, across), amplitudes.dtype),
        compiler_params=pltpu.CompilerParams(vmem_limit_bytes=VMEM_LIMIT),
        cost_estimate=pl.CostEstimate(
            flops=0, bytes_accessed=4 * groups * length * rows * size, transcendentals=0
        ),
        name="pack",
    )(entries.reshape(-1), amplitudes)


def ladder_kernel(counts, tile_ref, row_ref, part_ref, acc_in_ref, x_ref, *refs):
    piece_refs, (acc_ref, panel_ref, sem) = refs[:-3], refs[-3:]
    g = pl.program_id(0)
    here = x_ref.shape[0]
    parts, _, width, _ = panel_ref.shape

    @pl.when(g == 0)
    def _():
        copies = []
        for r in range(parts):
            first = 0
            for i, count in enumerate(counts):
                copies.append(
                    pltpu.make_async_copy(
                        piece_refs[r * len(counts) + i],
                        panel_ref.at[r, pl.ds(first, count)],
                        sem.at[r, i],
                    )
                )
                first += count
        for copy in copies:
            copy.start()
        acc_ref[...] = acc_in_ref[...]
        for copy in copies:
            copy.wait()

    def step(i, carry):
        at = g * here + i
        tile = tile_ref[at]

        @pl.when(tile >= 0)
        def _():
            row = row_ref[at]
            value = acc_ref[row]
            for r in range(parts):
                first = pl.multiple_of(part_ref[r] * width, width)
                value = value + jnp.dot(
                    x_ref[i, :, pl.ds(first, width)],
                    panel_ref[r, tile],
                    preferred_element_type=jnp.float32,
                )
            acc_ref[row] = value

        return carry

    lax.fori_loop(0, here, step, 0)


def ladder(lists, acc, blocks, parts, pieces):
    tile, row = lists
    count, rows, across = blocks.shape
    counts = tuple(x.shape[0] for x in pieces[0])
    _, width, panel_width = pieces[0][0].shape
    flat = [x for piece in pieces for x in piece]
    steps = 4
    whole = pl.BlockSpec(acc.shape, lambda i, *_: (0, 0, 0))
    return pl.pallas_call(
        functools.partial(ladder_kernel, counts),
        grid_spec=pltpu.PrefetchScalarGridSpec(
            num_scalar_prefetch=3,
            grid=(steps,),
            in_specs=[whole, pl.BlockSpec((count // steps, rows, across), lambda i, *_: (i, 0, 0))]
            + [pl.BlockSpec(memory_space=pl.ANY)] * len(flat),
            out_specs=whole,
            scratch_shapes=[
                pltpu.VMEM((len(pieces), sum(counts), width, panel_width), blocks.dtype),
                pltpu.SemaphoreType.DMA((len(pieces), len(counts))),
            ],
        ),
        out_shape=jax.ShapeDtypeStruct(acc.shape, jnp.float32),
        input_output_aliases={3: 0},
        compiler_params=pltpu.CompilerParams(vmem_limit_bytes=VMEM_LIMIT),
        cost_estimate=pl.CostEstimate(
            flops=2 * len(pieces) * count * rows * width * panel_width,
            bytes_accessed=2 * (blocks.size + sum(x.size for x in flat)),
            transcendentals=0,
        ),
        name="ladder",
    )(tile, row, parts, acc, blocks, *flat)


def few_kernel(
    counts, at_ref, tile_ref, row_ref, count_ref, part_ref, acc_in_ref, x_ref, *refs
):
    piece_refs, (acc_ref, block_ref, panel_ref, sem) = refs[:-4], refs[-4:]
    parts, _, width, _ = panel_ref.shape
    count = count_ref[0]

    def start(i, carry):
        pltpu.make_async_copy(x_ref.at[at_ref[i]], block_ref.at[i], sem.at[parts, i]).start()
        tile = tile_ref[i]
        for r in range(parts):
            first = 0
            for j, length in enumerate(counts):

                @pl.when(jnp.logical_and(tile >= first, tile < first + length))
                def _(r=r, j=j, first=first):
                    pltpu.make_async_copy(
                        piece_refs[r * len(counts) + j].at[tile - first],
                        panel_ref.at[r, i],
                        sem.at[r, i],
                    ).start()

                first += length
        return carry

    def step(i, carry):
        pltpu.make_async_copy(x_ref.at[0], block_ref.at[i], sem.at[parts, i]).wait()
        row = row_ref[i]
        value = acc_ref[row]
        for r in range(parts):
            pltpu.make_async_copy(piece_refs[0].at[0], panel_ref.at[r, i], sem.at[r, i]).wait()
            first = pl.multiple_of(part_ref[r] * width, width)
            value = value + jnp.dot(
                block_ref[i, :, pl.ds(first, width)],
                panel_ref[r, i],
                preferred_element_type=jnp.float32,
            )
        acc_ref[row] = value
        return carry

    lax.fori_loop(0, count, start, 0)
    acc_ref[...] = acc_in_ref[...]
    lax.fori_loop(0, count, step, 0)


def ladder_few(lists, acc, blocks, parts, pieces):
    at, tile, row, count = lists
    length, rows, across = blocks.shape
    counts = tuple(x.shape[0] for x in pieces[0])
    _, width, panel_width = pieces[0][0].shape
    flat = [x for piece in pieces for x in piece]
    whole = pl.BlockSpec(acc.shape, lambda i, *_: (0, 0, 0))
    return pl.pallas_call(
        functools.partial(few_kernel, counts),
        grid_spec=pltpu.PrefetchScalarGridSpec(
            num_scalar_prefetch=5,
            grid=(1,),
            in_specs=[whole] + [pl.BlockSpec(memory_space=pl.ANY)] * (1 + len(flat)),
            out_specs=whole,
            scratch_shapes=[
                pltpu.VMEM((length, rows, across), blocks.dtype),
                pltpu.VMEM((len(pieces), length, width, panel_width), blocks.dtype),
                pltpu.SemaphoreType.DMA((len(pieces) + 1, length)),
            ],
        ),
        out_shape=jax.ShapeDtypeStruct(acc.shape, jnp.float32),
        input_output_aliases={5: 0},
        compiler_params=pltpu.CompilerParams(vmem_limit_bytes=VMEM_LIMIT),
        name="ladder_few",
    )(at, tile, row, count, parts, acc, blocks, *flat)


def squeeze(tile, row):
    length = tile.shape[0]
    at = jnp.arange(length, dtype=jnp.int32)
    valid = tile >= 0
    ahead = jnp.cumsum(valid.astype(jnp.int32))
    count = ahead[-1]
    wanted = jnp.minimum(at, jnp.maximum(count - 1, 0))
    chosen = (valid[None, :] & (ahead[None, :] - 1 == wanted[:, None])).astype(jnp.int32)
    return [jnp.sum(chosen * c[None, :], axis=1) for c in (at, tile, row)] + [count.reshape(1)]


def residual_kernel(
    owner_ref,
    local_ref,
    count_ref,
    map_ref,
    amp_ref,
    weight_ref,
    left_ref,
    right_ref,
    out_ref,
    diag_ref,
    rows_ref,
    turned_ref,
):
    slots = owner_ref.shape[1]
    i = pl.program_id(0)
    used = i % slots < count_ref[i // slots]
    _, _, rows, size = amp_ref.shape
    vt = left_ref.shape[1]
    half = vt // 2
    lanes = 2 * vt
    pieces = size // lanes
    wide = diag_ref.shape[0]

    @pl.when(i == 0)
    def _():
        diag_ref[...] = jnp.zeros_like(diag_ref)

    @pl.when(jnp.logical_not(used))
    def _():
        out_ref[...] = jnp.zeros_like(out_ref)

    @pl.when(used)
    def _():
        for k in range(wide // vt):
            diag_ref[k * vt : (k + 1) * vt, k * vt : (k + 1) * vt] = right_ref[0]
        low = lax.broadcasted_iota(jnp.int32, (half, lanes), 1) < vt
        for k in range(pieces):
            rows_ref[pl.ds(k, rows, stride=pieces), :] = amp_ref[
                0, 0, :, k * lanes : (k + 1) * lanes
            ].astype(jnp.float32)
        for j in range(rows // 2):
            even = rows_ref[(2 * j) * pieces : (2 * j + 1) * pieces, :]
            odd = rows_ref[(2 * j + 1) * pieces : (2 * j + 2) * pieces, :]
            top = jnp.where(low, even, pltpu.roll(odd, vt, 1))
            bottom = jnp.where(low, pltpu.roll(even, vt, 1), odd)
            turned_ref[:, j * lanes : (j + 1) * lanes] = jnp.concatenate([top, bottom], 0).astype(
                jnp.bfloat16
            )
        for j in range(rows // 2):
            both = jnp.dot(
                left_ref[0],
                turned_ref[:, j * lanes : (j + 1) * lanes],
                preferred_element_type=jnp.float32,
            )
            top, bottom = both[:half], both[half:]
            rows_ref[(2 * j) * pieces : (2 * j + 1) * pieces, :] = jnp.where(
                low, top, pltpu.roll(bottom, vt, 1)
            )
            rows_ref[(2 * j + 1) * pieces : (2 * j + 2) * pieces, :] = jnp.where(
                low, pltpu.roll(top, vt, 1), bottom
            )
        for j in range(size // wide):
            at = slice(j * wide, (j + 1) * wide)
            block = amp_ref[0, 0, :, at]
            total = jnp.dot(weight_ref[0], block, preferred_element_type=jnp.float32)
            total = total + jnp.dot(block, diag_ref[...], preferred_element_type=jnp.float32)
            for k in range(wide // lanes):
                piece = j * (wide // lanes) + k
                left = rows_ref[pl.ds(piece, rows, stride=pieces), :]
                out_ref[0, 0, :, piece * lanes : (piece + 1) * lanes] = (
                    total[:, k * lanes : (k + 1) * lanes] + left
                ).astype(jnp.bfloat16)


def residual(tile_owner, tile_local, tile_counts, pair_map, amplitudes, hole_weight, fock_tiles, per_owner):
    tiles, slots, rows, size = amplitudes.shape
    tile_count, vt, _ = fock_tiles.shape
    left = fock_tiles.reshape(tile_count, vt // 2, 2, vt // 2, 2).transpose(0, 2, 1, 4, 3)
    left = left.reshape(tile_count, vt, vt)
    wide = 4 * vt

    def ident(i, owner, local, pairs):
        t, s = i // slots, i % slots
        return pairs[owner[t, s] * per_owner + local[t, s]]

    return pl.pallas_call(
        residual_kernel,
        grid_spec=pltpu.PrefetchScalarGridSpec(
            num_scalar_prefetch=4,
            grid=(tiles * slots,),
            in_specs=[
                pl.BlockSpec((1, 1, rows, size), lambda i, *_: (i // slots, i % slots, 0, 0)),
                pl.BlockSpec((1, rows, rows), lambda i, *_: (i // slots, 0, 0)),
                pl.BlockSpec(
                    (1, vt, vt), lambda i, o, l, c, m: (ident(i, o, l, m) // tile_count, 0, 0)
                ),
                pl.BlockSpec(
                    (1, vt, vt), lambda i, o, l, c, m: (ident(i, o, l, m) % tile_count, 0, 0)
                ),
            ],
            out_specs=pl.BlockSpec((1, 1, rows, size), lambda i, *_: (i // slots, i % slots, 0, 0)),
            scratch_shapes=[
                pltpu.VMEM((wide, wide), jnp.bfloat16),
                pltpu.VMEM((rows * size // (2 * vt), 2 * vt), jnp.float32),
                pltpu.VMEM((vt, rows * vt), jnp.bfloat16),
            ],
        ),
        out_shape=jax.ShapeDtypeStruct(amplitudes.shape, jnp.bfloat16),
        compiler_params=pltpu.CompilerParams(vmem_limit_bytes=VMEM_LIMIT),
        cost_estimate=pl.CostEstimate(
            flops=40 * amplitudes.size * vt, bytes_accessed=4 * amplitudes.size, transcendentals=0
        ),
        name="residual",
    )(tile_owner, tile_local, tile_counts, pair_map, amplitudes, hole_weight, left, fock_tiles)


def per_device(
    amplitudes,
    tile_counts,
    tile_owner,
    tile_local,
    pair_map,
    hole_weight,
    fock_tiles,
    ladder_panels,
):
    owners, parts = lax.axis_size("occ"), lax.axis_size("vir")
    per_owner, part_rows, panel_width = ladder_panels.shape
    tiles, slots, pair_rows, tile_size = amplitudes.shape
    groups = owners // GROUP
    width = part_rows // GROUP
    across = parts * width
    me = lax.axis_index("occ")
    place = me % GROUP
    slot_at = jnp.arange(slots, dtype=jnp.int32)
    group_at = jnp.arange(groups, dtype=jnp.int32)

    mine = jnp.concatenate([tile_owner, tile_local, tile_counts[:, None]], axis=1)
    table = lax.all_to_all(
        jnp.broadcast_to(mine, (owners * parts,) + mine.shape), AXES, 0, 0, tiled=True
    )
    named = (slot_at < tile_counts[:, None])[None] & (tile_owner // GROUP == group_at[:, None, None])
    named = named.reshape(groups, tiles * slots)
    own_turn = jnp.cumsum(named.astype(jnp.int32), axis=1) - named
    entry_at = jnp.arange(tiles * slots, dtype=jnp.int32)

    def entries(first, length):
        at = first + jnp.arange(length, dtype=jnp.int32)
        chosen = named[:, None, :] & (own_turn[:, None, :] == at[None, :, None])
        return jnp.sum(jnp.where(chosen, entry_at + 1, 0), axis=2).astype(jnp.int32) - 1

    def send(packed):
        packed = packed.reshape((owners,) + packed.shape[2:])
        return lax.all_to_all(packed, "occ", split_axis=0, concat_axis=0, tiled=True)

    most = tiles * GROUP

    def columns(k, first, count):
        start = (jnp.int32(first), (place ^ k) * width, jnp.int32(0))
        return lax.dynamic_slice(ladder_panels, start, (count, width, panel_width))

    def swap(k, x):
        return lax.ppermute(x, "occ", [(o, o ^ k) for o in range(owners)])

    half = per_owner // 2
    soon = [swap(k, columns(k, 0, half)) for k in (1, 2)]
    main = pack(entries(0, MAIN), amplitudes, parts)
    main, table, late, soon = lax.optimization_barrier((main, table, amplitudes, soon))
    main = send(main)
    later = [swap(k, columns(k, half, half)) for k in (1, 2)]
    later += [swap(k, columns(k, 0, per_owner)) for k in range(3, GROUP)]
    own = columns(0, 0, per_owner)

    local_residual = residual(
        tile_owner, tile_local, tile_counts, pair_map, late, hole_weight, fock_tiles, per_owner
    )
    extras = [pack(entries(MAIN, length), late, parts) for length in (1, 2)]

    used = slot_at < table[:, :, 2 * slots :]
    owner, local = table[:, :, :slots], table[:, :, slots : 2 * slots]
    of_group = used[..., None] & ((owner // GROUP)[..., None] == group_at)
    longest = jnp.max(jnp.sum(of_group, axis=(1, 2)))

    def of_core(x):
        x = x.reshape(owners, parts, tiles, slots)
        x = lax.dynamic_index_in_dim(x, lax.axis_index("vir"), axis=1, keepdims=False)
        return x.reshape(owners, tiles * slots)

    hit = of_core(used & (owner // GROUP == me // GROUP))
    turn = jnp.cumsum(hit.astype(jnp.int32), axis=1) - hit
    tile = of_core(((owner % GROUP) ^ place) * per_owner + local)
    row = jnp.arange(owners, dtype=jnp.int32)[:, None] * tiles + entry_at // slots

    def lists(first, length):
        at = first + jnp.arange(length, dtype=jnp.int32)
        chosen = hit[:, None, :] & (turn[:, None, :] == at[None, :, None])
        tiles_of = jnp.sum(jnp.where(chosen, tile[:, None, :] + 1, 0), axis=2) - 1
        rows_of = jnp.sum(jnp.where(chosen, row[:, None, :], 0), axis=2)
        return tiles_of.reshape(-1), rows_of.reshape(-1)

    main, extras, local_residual, later, own = lax.optimization_barrier(
        (main, extras, local_residual, later, own)
    )
    shared = [own]
    for k in (1, 2):
        shared += [soon[k - 1], later[k - 1]]
    shared += later[2:]
    empty = jnp.zeros((owners * tiles, pair_rows, panel_width), jnp.float32)
    main_lists = lists(0, MAIN)
    extra_lists = [squeeze(*lists(MAIN, length)) for length in range(1, most - MAIN + 1)]
    extra_entries = [entries(MAIN, length) for length in range(3, most - MAIN + 1)]
    core_parts = (lax.axis_index("vir") + jnp.arange(parts, dtype=jnp.int32)) % parts

    def some(length, main, shared, main_lists, extra_lists, extras, extra_entries, amplitudes):
        if length > len(extras):
            packed = pack(extra_entries[length - 1 - len(extras)], amplitudes, parts)
        elif length > 0:
            packed = extras[length - 1]
        if length > 0:
            blocks = send(packed).reshape(-1, pair_rows, across)
        panels = [shared]
        for r in range(1, parts):
            back = [(v, (v - r) % parts) for v in range(parts)]
            panels.append([lax.ppermute(x, "vir", back) for x in shared])
        main = main.reshape(-1, pair_rows, across)
        acc = ladder(main_lists, empty, main, core_parts[:1], panels[:1])
        if parts > 1:
            acc = ladder(main_lists, acc, main, core_parts[1:], panels[1:])
        if length > 0:
            acc = ladder_few(extra_lists[length - 1], acc, blocks, core_parts, panels)
        return acc

    acc = lax.switch(
        jnp.maximum(longest - MAIN, 0),
        [functools.partial(some, length) for length in range(most - MAIN + 1)],
        main,
        shared,
        main_lists,
        extra_lists,
        extras,
        extra_entries,
        amplitudes,
    )
    acc = acc.reshape(owners, tiles, pair_rows, panel_width)
    acc = lax.all_to_all(acc, "occ", split_axis=0, concat_axis=0, tiled=True)
    ladder_panel = jnp.sum(acc, axis=0).astype(jnp.bfloat16)
    return (local_residual, ladder_panel)


def solution(mesh):
    in_specs = (
        P(("occ", "vir"), None, None, None),
        P(("occ", "vir")),
        P(("occ", "vir"), None),
        P(("occ", "vir"), None),
        P(),
        P(("occ", "vir"), None, None),
        P(),
        P("occ", "vir", None),
    )
    out_specs = (P(("occ", "vir"), None, None, None), P(("occ", "vir"), None, None))
    return jax.shard_map(
        per_device, mesh=mesh, in_specs=in_specs, out_specs=out_specs, check_vma=False
    )
```

```python
import functools

import jax
import jax.numpy as jnp
from jax import lax
from jax.experimental import pallas as pl
from jax.experimental.pallas import tpu as pltpu
from jax.sharding import PartitionSpec as P

AXES = ("occ", "vir")
GROUP = 4
MAIN = 4
VMEM_LIMIT = 48 * 1024 * 1024


def pack_kernel(parts, entry_ref, amp_ref, out_ref, block_ref, in_sem, out_sem):
    groups, group, length, _, across = out_ref.shape
    slots = amp_ref.shape[1]
    width = across // parts

    def fetch(i):
        entry = jnp.maximum(entry_ref[i], 0)
        source = amp_ref.at[entry // slots, entry % slots]
        return pltpu.make_async_copy(source, block_ref.at[i], in_sem.at[i])

    def leave(i):
        return [
            pltpu.make_async_copy(
                block_ref.at[i, :, pl.ds((v * group + j) * width, width)],
                out_ref.at[i // length, j, i % length, :, pl.ds(v * width, width)],
                out_sem.at[i],
            )
            for j in range(group)
            for v in range(parts)
        ]

    def each(act):
        def step(i, carry):
            pl.when(entry_ref[i] >= 0)(lambda: act(i))
            return carry

        lax.fori_loop(0, groups * length, step, 0)

    def turn(i):
        fetch(i).wait()
        for copy in leave(i):
            copy.start()

    def finish(i):
        for copy in leave(i):
            copy.wait()

    each(lambda i: fetch(i).start())
    each(turn)
    each(finish)


def pack(entries, amplitudes, parts):
    _, slots, rows, size = amplitudes.shape
    groups, length = entries.shape
    across = size // GROUP
    return pl.pallas_call(
        functools.partial(pack_kernel, parts),
        grid_spec=pltpu.PrefetchScalarGridSpec(
            num_scalar_prefetch=1,
            grid=(1,),
            in_specs=[pl.BlockSpec(memory_space=pl.ANY)],
            out_specs=pl.BlockSpec(memory_space=pl.ANY),
            scratch_shapes=[
                pltpu.VMEM((groups * length, rows, size), amplitudes.dtype),
                pltpu.SemaphoreType.DMA((groups * length,)),
                pltpu.SemaphoreType.DMA((groups * length,)),
            ],
        ),
        out_shape=jax.ShapeDtypeStruct((groups, GROUP, length, rows, across), amplitudes.dtype),
        compiler_params=pltpu.CompilerParams(vmem_limit_bytes=VMEM_LIMIT),
        cost_estimate=pl.CostEstimate(
            flops=0, bytes_accessed=4 * groups * length * rows * size, transcendentals=0
        ),
        name="pack",
    )(entries.reshape(-1), amplitudes)


def ladder_kernel(counts, tile_ref, row_ref, part_ref, acc_in_ref, x_ref, *refs):
    piece_refs, (acc_ref, panel_ref, sem) = refs[:-3], refs[-3:]
    g = pl.program_id(0)
    here = x_ref.shape[0]
    parts, _, width, _ = panel_ref.shape

    @pl.when(g == 0)
    def _():
        copies = []
        for r in range(parts):
            first = 0
            for i, count in enumerate(counts):
                copies.append(
                    pltpu.make_async_copy(
                        piece_refs[r * len(counts) + i],
                        panel_ref.at[r, pl.ds(first, count)],
                        sem.at[r, i],
                    )
                )
                first += count
        for copy in copies:
            copy.start()
        acc_ref[...] = acc_in_ref[...]
        for copy in copies:
            copy.wait()

    def step(i, carry):
        at = g * here + i
        tile = tile_ref[at]

        @pl.when(tile >= 0)
        def _():
            row = row_ref[at]
            value = acc_ref[row]
            for r in range(parts):
                first = pl.multiple_of(part_ref[r] * width, width)
                value = value + jnp.dot(
                    x_ref[i, :, pl.ds(first, width)],
                    panel_ref[r, tile],
                    preferred_element_type=jnp.float32,
                )
            acc_ref[row] = value

        return carry

    lax.fori_loop(0, here, step, 0)


def ladder(lists, acc, blocks, parts, pieces):
    tile, row = lists
    count, rows, across = blocks.shape
    counts = tuple(x.shape[0] for x in pieces[0])
    _, width, panel_width = pieces[0][0].shape
    flat = [x for piece in pieces for x in piece]
    steps = 4
    whole = pl.BlockSpec(acc.shape, lambda i, *_: (0, 0, 0))
    return pl.pallas_call(
        functools.partial(ladder_kernel, counts),
        grid_spec=pltpu.PrefetchScalarGridSpec(
            num_scalar_prefetch=3,
            grid=(steps,),
            in_specs=[whole, pl.BlockSpec((count // steps, rows, across), lambda i, *_: (i, 0, 0))]
            + [pl.BlockSpec(memory_space=pl.ANY)] * len(flat),
            out_specs=whole,
            scratch_shapes=[
                pltpu.VMEM((len(pieces), sum(counts), width, panel_width), blocks.dtype),
                pltpu.SemaphoreType.DMA((len(pieces), len(counts))),
            ],
        ),
        out_shape=jax.ShapeDtypeStruct(acc.shape, jnp.float32),
        input_output_aliases={3: 0},
        compiler_params=pltpu.CompilerParams(vmem_limit_bytes=VMEM_LIMIT),
        cost_estimate=pl.CostEstimate(
            flops=2 * len(pieces) * count * rows * width * panel_width,
            bytes_accessed=2 * (blocks.size + sum(x.size for x in flat)),
            transcendentals=0,
        ),
        name="ladder",
    )(tile, row, parts, acc, blocks, *flat)


def few_kernel(
    counts, at_ref, tile_ref, row_ref, count_ref, part_ref, acc_in_ref, x_ref, *refs
):
    piece_refs, (acc_ref, block_ref, panel_ref, sem) = refs[:-4], refs[-4:]
    parts, _, width, _ = panel_ref.shape
    count = count_ref[0]

    def start(i, carry):
        pltpu.make_async_copy(x_ref.at[at_ref[i]], block_ref.at[i], sem.at[parts, i]).start()
        tile = tile_ref[i]
        for r in range(parts):
            first = 0
            for j, length in enumerate(counts):

                @pl.when(jnp.logical_and(tile >= first, tile < first + length))
                def _(r=r, j=j, first=first):
                    pltpu.make_async_copy(
                        piece_refs[r * len(counts) + j].at[tile - first],
                        panel_ref.at[r, i],
                        sem.at[r, i],
                    ).start()

                first += length
        return carry

    def step(i, carry):
        pltpu.make_async_copy(x_ref.at[0], block_ref.at[i], sem.at[parts, i]).wait()
        row = row_ref[i]
        value = acc_ref[row]
        for r in range(parts):
            pltpu.make_async_copy(piece_refs[0].at[0], panel_ref.at[r, i], sem.at[r, i]).wait()
            first = pl.multiple_of(part_ref[r] * width, width)
            value = value + jnp.dot(
                block_ref[i, :, pl.ds(first, width)],
                panel_ref[r, i],
                preferred_element_type=jnp.float32,
            )
        acc_ref[row] = value
        return carry

    lax.fori_loop(0, count, start, 0)
    acc_ref[...] = acc_in_ref[...]
    lax.fori_loop(0, count, step, 0)


def ladder_few(lists, acc, blocks, parts, pieces):
    at, tile, row, count = lists
    length, rows, across = blocks.shape
    counts = tuple(x.shape[0] for x in pieces[0])
    _, width, panel_width = pieces[0][0].shape
    flat = [x for piece in pieces for x in piece]
    whole = pl.BlockSpec(acc.shape, lambda i, *_: (0, 0, 0))
    return pl.pallas_call(
        functools.partial(few_kernel, counts),
        grid_spec=pltpu.PrefetchScalarGridSpec(
            num_scalar_prefetch=5,
            grid=(1,),
            in_specs=[whole] + [pl.BlockSpec(memory_space=pl.ANY)] * (1 + len(flat)),
            out_specs=whole,
            scratch_shapes=[
                pltpu.VMEM((length, rows, across), blocks.dtype),
                pltpu.VMEM((len(pieces), length, width, panel_width), blocks.dtype),
                pltpu.SemaphoreType.DMA((len(pieces) + 1, length)),
            ],
        ),
        out_shape=jax.ShapeDtypeStruct(acc.shape, jnp.float32),
        input_output_aliases={5: 0},
        compiler_params=pltpu.CompilerParams(vmem_limit_bytes=VMEM_LIMIT),
        name="ladder_few",
    )(at, tile, row, count, parts, acc, blocks, *flat)


def squeeze(tile, row):
    length = tile.shape[0]
    at = jnp.arange(length, dtype=jnp.int32)
    valid = tile >= 0
    ahead = jnp.cumsum(valid.astype(jnp.int32))
    count = ahead[-1]
    wanted = jnp.minimum(at, jnp.maximum(count - 1, 0))
    chosen = (valid[None, :] & (ahead[None, :] - 1 == wanted[:, None])).astype(jnp.int32)
    return [jnp.sum(chosen * c[None, :], axis=1) for c in (at, tile, row)] + [count.reshape(1)]


def residual_kernel(
    owner_ref,
    local_ref,
    count_ref,
    map_ref,
    amp_ref,
    weight_ref,
    left_ref,
    right_ref,
    out_ref,
    diag_ref,
    rows_ref,
    turned_ref,
):
    slots = owner_ref.shape[1]
    i = pl.program_id(0)
    used = i % slots < count_ref[i // slots]
    _, _, rows, size = amp_ref.shape
    vt = left_ref.shape[1]
    half = vt // 2
    lanes = 2 * vt
    pieces = size // lanes
    wide = diag_ref.shape[0]

    @pl.when(i == 0)
    def _():
        diag_ref[...] = jnp.zeros_like(diag_ref)

    @pl.when(jnp.logical_not(used))
    def _():
        out_ref[...] = jnp.zeros_like(out_ref)

    @pl.when(used)
    def _():
        for k in range(wide // vt):
            diag_ref[k * vt : (k + 1) * vt, k * vt : (k + 1) * vt] = right_ref[0]
        low = lax.broadcasted_iota(jnp.int32, (half, lanes), 1) < vt
        for k in range(pieces):
            rows_ref[pl.ds(k, rows, stride=pieces), :] = amp_ref[
                0, 0, :, k * lanes : (k + 1) * lanes
            ].astype(jnp.float32)
        for j in range(rows // 2):
            even = rows_ref[(2 * j) * pieces : (2 * j + 1) * pieces, :]
            odd = rows_ref[(2 * j + 1) * pieces : (2 * j + 2) * pieces, :]
            top = jnp.where(low, even, pltpu.roll(odd, vt, 1))
            bottom = jnp.where(low, pltpu.roll(even, vt, 1), odd)
            turned_ref[:, j * lanes : (j + 1) * lanes] = jnp.concatenate([top, bottom], 0).astype(
                jnp.bfloat16
            )
        for j in range(rows // 2):
            both = jnp.dot(
                left_ref[0],
                turned_ref[:, j * lanes : (j + 1) * lanes],
                preferred_element_type=jnp.float32,
            )
            top, bottom = both[:half], both[half:]
            rows_ref[(2 * j) * pieces : (2 * j + 1) * pieces, :] = jnp.where(
                low, top, pltpu.roll(bottom, vt, 1)
            )
            rows_ref[(2 * j + 1) * pieces : (2 * j + 2) * pieces, :] = jnp.where(
                low, pltpu.roll(top, vt, 1), bottom
            )
        for j in range(size // wide):
            at = slice(j * wide, (j + 1) * wide)
            block = amp_ref[0, 0, :, at]
            total = jnp.dot(weight_ref[0], block, preferred_element_type=jnp.float32)
            total = total + jnp.dot(block, diag_ref[...], preferred_element_type=jnp.float32)
            for k in range(wide // lanes):
                piece = j * (wide // lanes) + k
                left = rows_ref[pl.ds(piece, rows, stride=pieces), :]
                out_ref[0, 0, :, piece * lanes : (piece + 1) * lanes] = (
                    total[:, k * lanes : (k + 1) * lanes] + left
                ).astype(jnp.bfloat16)


def residual(tile_owner, tile_local, tile_counts, pair_map, amplitudes, hole_weight, fock_tiles, per_owner):
    tiles, slots, rows, size = amplitudes.shape
    tile_count, vt, _ = fock_tiles.shape
    left = fock_tiles.reshape(tile_count, vt // 2, 2, vt // 2, 2).transpose(0, 2, 1, 4, 3)
    left = left.reshape(tile_count, vt, vt)
    wide = 4 * vt

    def ident(i, owner, local, pairs):
        t, s = i // slots, i % slots
        return pairs[owner[t, s] * per_owner + local[t, s]]

    return pl.pallas_call(
        residual_kernel,
        grid_spec=pltpu.PrefetchScalarGridSpec(
            num_scalar_prefetch=4,
            grid=(tiles * slots,),
            in_specs=[
                pl.BlockSpec((1, 1, rows, size), lambda i, *_: (i // slots, i % slots, 0, 0)),
                pl.BlockSpec((1, rows, rows), lambda i, *_: (i // slots, 0, 0)),
                pl.BlockSpec(
                    (1, vt, vt), lambda i, o, l, c, m: (ident(i, o, l, m) // tile_count, 0, 0)
                ),
                pl.BlockSpec(
                    (1, vt, vt), lambda i, o, l, c, m: (ident(i, o, l, m) % tile_count, 0, 0)
                ),
            ],
            out_specs=pl.BlockSpec((1, 1, rows, size), lambda i, *_: (i // slots, i % slots, 0, 0)),
            scratch_shapes=[
                pltpu.VMEM((wide, wide), jnp.bfloat16),
                pltpu.VMEM((rows * size // (2 * vt), 2 * vt), jnp.float32),
                pltpu.VMEM((vt, rows * vt), jnp.bfloat16),
            ],
        ),
        out_shape=jax.ShapeDtypeStruct(amplitudes.shape, jnp.bfloat16),
        compiler_params=pltpu.CompilerParams(vmem_limit_bytes=VMEM_LIMIT),
        cost_estimate=pl.CostEstimate(
            flops=40 * amplitudes.size * vt, bytes_accessed=4 * amplitudes.size, transcendentals=0
        ),
        name="residual",
    )(tile_owner, tile_local, tile_counts, pair_map, amplitudes, hole_weight, left, fock_tiles)


def per_device(
    amplitudes,
    tile_counts,
    tile_owner,
    tile_local,
    pair_map,
    hole_weight,
    fock_tiles,
    ladder_panels,
):
    owners, parts = lax.axis_size("occ"), lax.axis_size("vir")
    per_owner, part_rows, panel_width = ladder_panels.shape
    tiles, slots, pair_rows, tile_size = amplitudes.shape
    groups = owners // GROUP
    width = part_rows // GROUP
    across = parts * width
    me = lax.axis_index("occ")
    place = me % GROUP
    slot_at = jnp.arange(slots, dtype=jnp.int32)
    group_at = jnp.arange(groups, dtype=jnp.int32)

    mine = jnp.concatenate([tile_owner, tile_local, tile_counts[:, None]], axis=1)
    table = lax.all_to_all(
        jnp.broadcast_to(mine, (owners * parts,) + mine.shape), AXES, 0, 0, tiled=True
    )
    named = (slot_at < tile_counts[:, None])[None] & (tile_owner // GROUP == group_at[:, None, None])
    named = named.reshape(groups, tiles * slots)
    own_turn = jnp.cumsum(named.astype(jnp.int32), axis=1) - named
    entry_at = jnp.arange(tiles * slots, dtype=jnp.int32)

    def entries(first, length):
        at = first + jnp.arange(length, dtype=jnp.int32)
        chosen = named[:, None, :] & (own_turn[:, None, :] == at[None, :, None])
        return jnp.sum(jnp.where(chosen, entry_at + 1, 0), axis=2).astype(jnp.int32) - 1

    def send(packed):
        packed = packed.reshape((owners,) + packed.shape[2:])
        return lax.all_to_all(packed, "occ", split_axis=0, concat_axis=0, tiled=True)

    most = tiles * GROUP

    def columns(k, first, count):
        start = (jnp.int32(first), (place ^ k) * width, jnp.int32(0))
        return lax.dynamic_slice(ladder_panels, start, (count, width, panel_width))

    def swap(k, x):
        return lax.ppermute(x, "occ", [(o, o ^ k) for o in range(owners)])

    main = pack(entries(0, MAIN), amplitudes, parts)
    main, table, late = lax.optimization_barrier((main, table, amplitudes))
    main = send(main)
    shared = [columns(0, 0, per_owner)]
    shared += [swap(k, columns(k, 0, per_owner)) for k in range(1, GROUP)]

    local_residual = residual(
        tile_owner, tile_local, tile_counts, pair_map, late, hole_weight, fock_tiles, per_owner
    )
    extras = [pack(entries(MAIN, length), late, parts) for length in (1, 2)]

    used = slot_at < table[:, :, 2 * slots :]
    owner, local = table[:, :, :slots], table[:, :, slots : 2 * slots]
    of_group = used[..., None] & ((owner // GROUP)[..., None] == group_at)
    longest = jnp.max(jnp.sum(of_group, axis=(1, 2)))

    def of_core(x):
        x = x.reshape(owners, parts, tiles, slots)
        x = lax.dynamic_index_in_dim(x, lax.axis_index("vir"), axis=1, keepdims=False)
        return x.reshape(owners, tiles * slots)

    hit = of_core(used & (owner // GROUP == me // GROUP))
    turn = jnp.cumsum(hit.astype(jnp.int32), axis=1) - hit
    tile = of_core(((owner % GROUP) ^ place) * per_owner + local)
    row = jnp.arange(owners, dtype=jnp.int32)[:, None] * tiles + entry_at // slots

    def lists(first, length):
        at = first + jnp.arange(length, dtype=jnp.int32)
        chosen = hit[:, None, :] & (turn[:, None, :] == at[None, :, None])
        tiles_of = jnp.sum(jnp.where(chosen, tile[:, None, :] + 1, 0), axis=2) - 1
        rows_of = jnp.sum(jnp.where(chosen, row[:, None, :], 0), axis=2)
        return tiles_of.reshape(-1), rows_of.reshape(-1)

    main, extras, local_residual, shared = lax.optimization_barrier(
        (main, extras, local_residual, shared)
    )
    empty = jnp.zeros((owners * tiles, pair_rows, panel_width), jnp.float32)
    main_lists = lists(0, MAIN)
    extra_lists = [squeeze(*lists(MAIN, length)) for length in range(1, most - MAIN + 1)]
    extra_entries = [entries(MAIN, length) for length in range(3, most - MAIN + 1)]
    core_parts = (lax.axis_index("vir") + jnp.arange(parts, dtype=jnp.int32)) % parts

    def some(length, main, shared, main_lists, extra_lists, extras, extra_entries, amplitudes):
        if length > len(extras):
            packed = pack(extra_entries[length - 1 - len(extras)], amplitudes, parts)
        elif length > 0:
            packed = extras[length - 1]
        if length > 0:
            blocks = send(packed).reshape(-1, pair_rows, across)
        panels = [shared]
        for r in range(1, parts):
            back = [(v, (v - r) % parts) for v in range(parts)]
            panels.append([lax.ppermute(x, "vir", back) for x in shared])
        main = main.reshape(-1, pair_rows, across)
        acc = ladder(main_lists, empty, main, core_parts[:1], panels[:1])
        if parts > 1:
            acc = ladder(main_lists, acc, main, core_parts[1:], panels[1:])
        if length > 0:
            acc = ladder_few(extra_lists[length - 1], acc, blocks, core_parts, panels)
        return acc

    acc = lax.switch(
        jnp.maximum(longest - MAIN, 0),
        [functools.partial(some, length) for length in range(most - MAIN + 1)],
        main,
        shared,
        main_lists,
        extra_lists,
        extras,
        extra_entries,
        amplitudes,
    )
    acc = acc.reshape(owners, tiles, pair_rows, panel_width)
    acc = lax.all_to_all(acc, "occ", split_axis=0, concat_axis=0, tiled=True)
    ladder_panel = jnp.sum(acc, axis=0).astype(jnp.bfloat16)
    return (local_residual, ladder_panel)


def solution(mesh):
    in_specs = (
        P(("occ", "vir"), None, None, None),
        P(("occ", "vir")),
        P(("occ", "vir"), None),
        P(("occ", "vir"), None),
        P(),
        P(("occ", "vir"), None, None),
        P(),
        P("occ", "vir", None),
    )
    out_specs = (P(("occ", "vir"), None, None, None), P(("occ", "vir"), None, None))
    return jax.shard_map(
        per_device, mesh=mesh, in_specs=in_specs, out_specs=out_specs, check_vma=False
    )
```

```python
import functools

import jax
import jax.numpy as jnp
from jax import lax
from jax.experimental import pallas as pl
from jax.experimental.pallas import tpu as pltpu
from jax.sharding import PartitionSpec as P

AXES = ("occ", "vir")
GROUP = 4
MAIN = 4
FIRST = 2
VMEM_LIMIT = 48 * 1024 * 1024


def pack_kernel(parts, entry_ref, amp_ref, out_ref, block_ref, in_sem, out_sem):
    groups, group, length, _, across = out_ref.shape
    slots = amp_ref.shape[1]
    width = across // parts

    def fetch(i):
        entry = jnp.maximum(entry_ref[i], 0)
        source = amp_ref.at[entry // slots, entry % slots]
        return pltpu.make_async_copy(source, block_ref.at[i], in_sem.at[i])

    def leave(i):
        return [
            pltpu.make_async_copy(
                block_ref.at[i, :, pl.ds((v * group + j) * width, width)],
                out_ref.at[i // length, j, i % length, :, pl.ds(v * width, width)],
                out_sem.at[i],
            )
            for j in range(group)
            for v in range(parts)
        ]

    def each(act):
        def step(i, carry):
            pl.when(entry_ref[i] >= 0)(lambda: act(i))
            return carry

        lax.fori_loop(0, groups * length, step, 0)

    def turn(i):
        fetch(i).wait()
        for copy in leave(i):
            copy.start()

    def finish(i):
        for copy in leave(i):
            copy.wait()

    each(lambda i: fetch(i).start())
    each(turn)
    each(finish)


def pack(entries, amplitudes, parts):
    _, slots, rows, size = amplitudes.shape
    groups, length = entries.shape
    across = size // GROUP
    return pl.pallas_call(
        functools.partial(pack_kernel, parts),
        grid_spec=pltpu.PrefetchScalarGridSpec(
            num_scalar_prefetch=1,
            grid=(1,),
            in_specs=[pl.BlockSpec(memory_space=pl.ANY)],
            out_specs=pl.BlockSpec(memory_space=pl.ANY),
            scratch_shapes=[
                pltpu.VMEM((groups * length, rows, size), amplitudes.dtype),
                pltpu.SemaphoreType.DMA((groups * length,)),
                pltpu.SemaphoreType.DMA((groups * length,)),
            ],
        ),
        out_shape=jax.ShapeDtypeStruct((groups, GROUP, length, rows, across), amplitudes.dtype),
        compiler_params=pltpu.CompilerParams(vmem_limit_bytes=VMEM_LIMIT),
        cost_estimate=pl.CostEstimate(
            flops=0, bytes_accessed=4 * groups * length * rows * size, transcendentals=0
        ),
        name="pack",
    )(entries.reshape(-1), amplitudes)


def ladder_kernel(counts, arrays, tile_ref, row_ref, part_ref, acc_in_ref, *refs):
    x_refs, piece_refs, (acc_ref, panel_ref, sem) = refs[:arrays], refs[arrays:-3], refs[-3:]
    g = pl.program_id(0)
    here = x_refs[0].shape[0]
    steps = pl.num_programs(0)
    parts, _, width, _ = panel_ref.shape

    @pl.when(g == 0)
    def _():
        copies = []
        for r in range(parts):
            first = 0
            for i, count in enumerate(counts):
                copies.append(
                    pltpu.make_async_copy(
                        piece_refs[r * len(counts) + i],
                        panel_ref.at[r, pl.ds(first, count)],
                        sem.at[r, i],
                    )
                )
                first += count
        for copy in copies:
            copy.start()
        acc_ref[...] = acc_in_ref[...]
        for copy in copies:
            copy.wait()

    for a, x_ref in enumerate(x_refs):

        def step(i, carry, a=a, x_ref=x_ref):
            at = (a * steps + g) * here + i
            tile = tile_ref[at]

            @pl.when(tile >= 0)
            def _():
                row = row_ref[at]
                value = acc_ref[row]
                for r in range(parts):
                    first = pl.multiple_of(part_ref[r] * width, width)
                    value = value + jnp.dot(
                        x_ref[i, :, pl.ds(first, width)],
                        panel_ref[r, tile],
                        preferred_element_type=jnp.float32,
                    )
                acc_ref[row] = value

            return carry

        lax.fori_loop(0, here, step, 0)


def ladder(lists, acc, blocks, parts, pieces):
    tile = jnp.concatenate([x for x, _ in lists])
    row = jnp.concatenate([x for _, x in lists])
    count, rows, across = blocks[0].shape
    counts = tuple(x.shape[0] for x in pieces[0])
    _, width, panel_width = pieces[0][0].shape
    flat = [x for piece in pieces for x in piece]
    steps = 4
    whole = pl.BlockSpec(acc.shape, lambda i, *_: (0, 0, 0))
    block = pl.BlockSpec((count // steps, rows, across), lambda i, *_: (i, 0, 0))
    return pl.pallas_call(
        functools.partial(ladder_kernel, counts, len(blocks)),
        grid_spec=pltpu.PrefetchScalarGridSpec(
            num_scalar_prefetch=3,
            grid=(steps,),
            in_specs=[whole]
            + [block] * len(blocks)
            + [pl.BlockSpec(memory_space=pl.ANY)] * len(flat),
            out_specs=whole,
            scratch_shapes=[
                pltpu.VMEM((len(pieces), sum(counts), width, panel_width), flat[0].dtype),
                pltpu.SemaphoreType.DMA((len(pieces), len(counts))),
            ],
        ),
        out_shape=jax.ShapeDtypeStruct(acc.shape, jnp.float32),
        input_output_aliases={3: 0},
        compiler_params=pltpu.CompilerParams(vmem_limit_bytes=VMEM_LIMIT),
        cost_estimate=pl.CostEstimate(
            flops=2 * len(pieces) * len(blocks) * count * rows * width * panel_width,
            bytes_accessed=2 * sum(x.size for x in (*blocks, *flat)),
            transcendentals=0,
        ),
        name="ladder",
    )(tile, row, parts, acc, *blocks, *flat)


def few_kernel(
    counts, at_ref, tile_ref, row_ref, count_ref, part_ref, acc_in_ref, x_ref, *refs
):
    piece_refs, (acc_ref, block_ref, panel_ref, sem) = refs[:-4], refs[-4:]
    parts, _, width, _ = panel_ref.shape
    count = count_ref[0]

    def start(i, carry):
        pltpu.make_async_copy(x_ref.at[at_ref[i]], block_ref.at[i], sem.at[parts, i]).start()
        tile = tile_ref[i]
        for r in range(parts):
            first = 0
            for j, length in enumerate(counts):

                @pl.when(jnp.logical_and(tile >= first, tile < first + length))
                def _(r=r, j=j, first=first):
                    pltpu.make_async_copy(
                        piece_refs[r * len(counts) + j].at[tile - first],
                        panel_ref.at[r, i],
                        sem.at[r, i],
                    ).start()

                first += length
        return carry

    def step(i, carry):
        pltpu.make_async_copy(x_ref.at[0], block_ref.at[i], sem.at[parts, i]).wait()
        row = row_ref[i]
        value = acc_ref[row]
        for r in range(parts):
            pltpu.make_async_copy(piece_refs[0].at[0], panel_ref.at[r, i], sem.at[r, i]).wait()
            first = pl.multiple_of(part_ref[r] * width, width)
            value = value + jnp.dot(
                block_ref[i, :, pl.ds(first, width)],
                panel_ref[r, i],
                preferred_element_type=jnp.float32,
            )
        acc_ref[row] = value
        return carry

    lax.fori_loop(0, count, start, 0)
    acc_ref[...] = acc_in_ref[...]
    lax.fori_loop(0, count, step, 0)


def ladder_few(lists, acc, blocks, parts, pieces):
    at, tile, row, count = lists
    length, rows, across = blocks.shape
    counts = tuple(x.shape[0] for x in pieces[0])
    _, width, panel_width = pieces[0][0].shape
    flat = [x for piece in pieces for x in piece]
    whole = pl.BlockSpec(acc.shape, lambda i, *_: (0, 0, 0))
    return pl.pallas_call(
        functools.partial(few_kernel, counts),
        grid_spec=pltpu.PrefetchScalarGridSpec(
            num_scalar_prefetch=5,
            grid=(1,),
            in_specs=[whole] + [pl.BlockSpec(memory_space=pl.ANY)] * (1 + len(flat)),
            out_specs=whole,
            scratch_shapes=[
                pltpu.VMEM((length, rows, across), blocks.dtype),
                pltpu.VMEM((len(pieces), length, width, panel_width), blocks.dtype),
                pltpu.SemaphoreType.DMA((len(pieces) + 1, length)),
            ],
        ),
        out_shape=jax.ShapeDtypeStruct(acc.shape, jnp.float32),
        input_output_aliases={5: 0},
        compiler_params=pltpu.CompilerParams(vmem_limit_bytes=VMEM_LIMIT),
        name="ladder_few",
    )(at, tile, row, count, parts, acc, blocks, *flat)


def squeeze(tile, row):
    length = tile.shape[0]
    at = jnp.arange(length, dtype=jnp.int32)
    valid = tile >= 0
    ahead = jnp.cumsum(valid.astype(jnp.int32))
    count = ahead[-1]
    wanted = jnp.minimum(at, jnp.maximum(count - 1, 0))
    chosen = (valid[None, :] & (ahead[None, :] - 1 == wanted[:, None])).astype(jnp.int32)
    return [jnp.sum(chosen * c[None, :], axis=1) for c in (at, tile, row)] + [count.reshape(1)]


def residual_kernel(
    owner_ref,
    local_ref,
    count_ref,
    map_ref,
    amp_ref,
    weight_ref,
    left_ref,
    right_ref,
    out_ref,
    diag_ref,
    rows_ref,
    turned_ref,
):
    slots = owner_ref.shape[1]
    i = pl.program_id(0)
    used = i % slots < count_ref[i // slots]
    _, _, rows, size = amp_ref.shape
    vt = left_ref.shape[1]
    half = vt // 2
    lanes = 2 * vt
    pieces = size // lanes
    wide = diag_ref.shape[0]

    @pl.when(i == 0)
    def _():
        diag_ref[...] = jnp.zeros_like(diag_ref)

    @pl.when(jnp.logical_not(used))
    def _():
        out_ref[...] = jnp.zeros_like(out_ref)

    @pl.when(used)
    def _():
        for k in range(wide // vt):
            diag_ref[k * vt : (k + 1) * vt, k * vt : (k + 1) * vt] = right_ref[0]
        low = lax.broadcasted_iota(jnp.int32, (half, lanes), 1) < vt
        for k in range(pieces):
            rows_ref[pl.ds(k, rows, stride=pieces), :] = amp_ref[
                0, 0, :, k * lanes : (k + 1) * lanes
            ].astype(jnp.float32)
        for j in range(rows // 2):
            even = rows_ref[(2 * j) * pieces : (2 * j + 1) * pieces, :]
            odd = rows_ref[(2 * j + 1) * pieces : (2 * j + 2) * pieces, :]
            top = jnp.where(low, even, pltpu.roll(odd, vt, 1))
            bottom = jnp.where(low, pltpu.roll(even, vt, 1), odd)
            turned_ref[:, j * lanes : (j + 1) * lanes] = jnp.concatenate([top, bottom], 0).astype(
                jnp.bfloat16
            )
        for j in range(rows // 2):
            both = jnp.dot(
                left_ref[0],
                turned_ref[:, j * lanes : (j + 1) * lanes],
                preferred_element_type=jnp.float32,
            )
            top, bottom = both[:half], both[half:]
            rows_ref[(2 * j) * pieces : (2 * j + 1) * pieces, :] = jnp.where(
                low, top, pltpu.roll(bottom, vt, 1)
            )
            rows_ref[(2 * j + 1) * pieces : (2 * j + 2) * pieces, :] = jnp.where(
                low, pltpu.roll(top, vt, 1), bottom
            )
        for j in range(size // wide):
            at = slice(j * wide, (j + 1) * wide)
            block = amp_ref[0, 0, :, at]
            total = jnp.dot(weight_ref[0], block, preferred_element_type=jnp.float32)
            total = total + jnp.dot(block, diag_ref[...], preferred_element_type=jnp.float32)
            for k in range(wide // lanes):
                piece = j * (wide // lanes) + k
                left = rows_ref[pl.ds(piece, rows, stride=pieces), :]
                out_ref[0, 0, :, piece * lanes : (piece + 1) * lanes] = (
                    total[:, k * lanes : (k + 1) * lanes] + left
                ).astype(jnp.bfloat16)


def residual(tile_owner, tile_local, tile_counts, pair_map, amplitudes, hole_weight, fock_tiles, per_owner):
    tiles, slots, rows, size = amplitudes.shape
    tile_count, vt, _ = fock_tiles.shape
    left = fock_tiles.reshape(tile_count, vt // 2, 2, vt // 2, 2).transpose(0, 2, 1, 4, 3)
    left = left.reshape(tile_count, vt, vt)
    wide = 4 * vt

    def ident(i, owner, local, pairs):
        t, s = i // slots, i % slots
        return pairs[owner[t, s] * per_owner + local[t, s]]

    return pl.pallas_call(
        residual_kernel,
        grid_spec=pltpu.PrefetchScalarGridSpec(
            num_scalar_prefetch=4,
            grid=(tiles * slots,),
            in_specs=[
                pl.BlockSpec((1, 1, rows, size), lambda i, *_: (i // slots, i % slots, 0, 0)),
                pl.BlockSpec((1, rows, rows), lambda i, *_: (i // slots, 0, 0)),
                pl.BlockSpec(
                    (1, vt, vt), lambda i, o, l, c, m: (ident(i, o, l, m) // tile_count, 0, 0)
                ),
                pl.BlockSpec(
                    (1, vt, vt), lambda i, o, l, c, m: (ident(i, o, l, m) % tile_count, 0, 0)
                ),
            ],
            out_specs=pl.BlockSpec((1, 1, rows, size), lambda i, *_: (i // slots, i % slots, 0, 0)),
            scratch_shapes=[
                pltpu.VMEM((wide, wide), jnp.bfloat16),
                pltpu.VMEM((rows * size // (2 * vt), 2 * vt), jnp.float32),
                pltpu.VMEM((vt, rows * vt), jnp.bfloat16),
            ],
        ),
        out_shape=jax.ShapeDtypeStruct(amplitudes.shape, jnp.bfloat16),
        compiler_params=pltpu.CompilerParams(vmem_limit_bytes=VMEM_LIMIT),
        cost_estimate=pl.CostEstimate(
            flops=40 * amplitudes.size * vt, bytes_accessed=4 * amplitudes.size, transcendentals=0
        ),
        name="residual",
    )(tile_owner, tile_local, tile_counts, pair_map, amplitudes, hole_weight, left, fock_tiles)


def per_device(
    amplitudes,
    tile_counts,
    tile_owner,
    tile_local,
    pair_map,
    hole_weight,
    fock_tiles,
    ladder_panels,
):
    owners, parts = lax.axis_size("occ"), lax.axis_size("vir")
    per_owner, part_rows, panel_width = ladder_panels.shape
    tiles, slots, pair_rows, tile_size = amplitudes.shape
    groups = owners // GROUP
    width = part_rows // GROUP
    across = parts * width
    me = lax.axis_index("occ")
    place = me % GROUP
    slot_at = jnp.arange(slots, dtype=jnp.int32)
    group_at = jnp.arange(groups, dtype=jnp.int32)

    named = (slot_at < tile_counts[:, None])[None] & (tile_owner // GROUP == group_at[:, None, None])
    named = named.reshape(groups, tiles * slots)
    own_turn = jnp.cumsum(named.astype(jnp.int32), axis=1) - named
    entry_at = jnp.arange(tiles * slots, dtype=jnp.int32)

    def entries(first, length):
        at = first + jnp.arange(length, dtype=jnp.int32)
        chosen = named[:, None, :] & (own_turn[:, None, :] == at[None, :, None])
        return jnp.sum(jnp.where(chosen, entry_at + 1, 0), axis=2).astype(jnp.int32) - 1

    def send(packed):
        packed = packed.reshape((owners,) + packed.shape[2:])
        return lax.all_to_all(packed, "occ", split_axis=0, concat_axis=0, tiled=True)

    most = tiles * GROUP

    def columns(k, first, count):
        start = (jnp.int32(first), (place ^ k) * width, jnp.int32(0))
        return lax.dynamic_slice(ladder_panels, start, (count, width, panel_width))

    def swap(k, x):
        return lax.ppermute(x, "occ", [(o, o ^ k) for o in range(owners)])

    main = pack(entries(0, FIRST), amplitudes, parts)
    mine = jnp.concatenate([tile_owner, tile_local, tile_counts[:, None]], axis=1)
    main, mine, late = lax.optimization_barrier((main, mine, amplitudes))
    main = send(main)
    table = lax.all_gather(mine, AXES, axis=0, tiled=True).reshape(
        owners * parts, tiles, 2 * slots + 1
    )
    shared = [columns(0, 0, per_owner)] + [swap(k, columns(k, 0, per_owner)) for k in (1, 2)]
    second = pack(entries(FIRST, MAIN - FIRST), late, parts)
    extras = [pack(entries(MAIN, length), late, parts) for length in (1, 2)]
    local_residual = residual(
        tile_owner, tile_local, tile_counts, pair_map, late, hole_weight, fock_tiles, per_owner
    )
    main, second, shared, table, ladder_panels = lax.optimization_barrier(
        (main, second, shared, table, ladder_panels)
    )
    second = send(second)
    shared += [swap(k, columns(k, 0, per_owner)) for k in range(3, GROUP)]

    used = slot_at < table[:, :, 2 * slots :]
    owner, local = table[:, :, :slots], table[:, :, slots : 2 * slots]
    of_group = used[..., None] & ((owner // GROUP)[..., None] == group_at)
    longest = jnp.max(jnp.sum(of_group, axis=(1, 2)))

    def of_core(x):
        x = x.reshape(owners, parts, tiles, slots)
        x = lax.dynamic_index_in_dim(x, lax.axis_index("vir"), axis=1, keepdims=False)
        return x.reshape(owners, tiles * slots)

    hit = of_core(used & (owner // GROUP == me // GROUP))
    turn = jnp.cumsum(hit.astype(jnp.int32), axis=1) - hit
    tile = of_core(((owner % GROUP) ^ place) * per_owner + local)
    row = jnp.arange(owners, dtype=jnp.int32)[:, None] * tiles + entry_at // slots

    def lists(first, length):
        at = first + jnp.arange(length, dtype=jnp.int32)
        chosen = hit[:, None, :] & (turn[:, None, :] == at[None, :, None])
        tiles_of = jnp.sum(jnp.where(chosen, tile[:, None, :] + 1, 0), axis=2) - 1
        rows_of = jnp.sum(jnp.where(chosen, row[:, None, :], 0), axis=2)
        return tiles_of.reshape(-1), rows_of.reshape(-1)

    main, second, extras, local_residual, shared = lax.optimization_barrier(
        (main, second, extras, local_residual, shared)
    )
    empty = jnp.zeros((owners * tiles, pair_rows, panel_width), jnp.float32)
    main_lists = [lists(0, FIRST), lists(FIRST, MAIN - FIRST)]
    extra_lists = [squeeze(*lists(MAIN, length)) for length in range(1, most - MAIN + 1)]
    extra_entries = [entries(MAIN, length) for length in range(3, most - MAIN + 1)]
    core_parts = (lax.axis_index("vir") + jnp.arange(parts, dtype=jnp.int32)) % parts

    def some(length, main, second, shared, main_lists, extra_lists, extras, extra_entries, amplitudes):
        if length > len(extras):
            packed = pack(extra_entries[length - 1 - len(extras)], amplitudes, parts)
        elif length > 0:
            packed = extras[length - 1]
        if length > 0:
            blocks = send(packed).reshape(-1, pair_rows, across)
        panels = [shared]
        for r in range(1, parts):
            back = [(v, (v - r) % parts) for v in range(parts)]
            panels.append([lax.ppermute(x, "vir", back) for x in shared])
        main = [x.reshape(-1, pair_rows, across) for x in (main, second)]
        acc = ladder(main_lists, empty, main, core_parts[:1], panels[:1])
        if parts > 1:
            acc = ladder(main_lists, acc, main, core_parts[1:], panels[1:])
        if length > 0:
            acc = ladder_few(extra_lists[length - 1], acc, blocks, core_parts, panels)
        return acc

    acc = lax.switch(
        jnp.maximum(longest - MAIN, 0),
        [functools.partial(some, length) for length in range(most - MAIN + 1)],
        main,
        second,
        shared,
        main_lists,
        extra_lists,
        extras,
        extra_entries,
        amplitudes,
    )
    acc = acc.reshape(owners, tiles, pair_rows, panel_width)
    acc = lax.all_to_all(acc, "occ", split_axis=0, concat_axis=0, tiled=True)
    ladder_panel = jnp.sum(acc, axis=0).astype(jnp.bfloat16)
    return (local_residual, ladder_panel)


def solution(mesh):
    in_specs = (
        P(("occ", "vir"), None, None, None),
        P(("occ", "vir")),
        P(("occ", "vir"), None),
        P(("occ", "vir"), None),
        P(),
        P(("occ", "vir"), None, None),
        P(),
        P("occ", "vir", None),
    )
    out_specs = (P(("occ", "vir"), None, None, None), P(("occ", "vir"), None, None))
    return jax.shard_map(
        per_device, mesh=mesh, in_specs=in_specs, out_specs=out_specs, check_vma=False
    )
```

```python
import functools

import jax
import jax.numpy as jnp
from jax import lax
from jax.experimental import pallas as pl
from jax.experimental.pallas import tpu as pltpu
from jax.sharding import PartitionSpec as P

AXES = ("occ", "vir")
GROUP = 4
MAIN = 4
VMEM_LIMIT = 48 * 1024 * 1024


def pack_kernel(parts, entry_ref, place_ref, amp_ref, *refs):
    out_refs, (block_ref, in_sem, out_sem) = refs[:-3], refs[-3:]
    length, _, across = out_refs[0].shape
    group = GROUP
    groups = len(out_refs) // group
    slots = amp_ref.shape[1]
    width = across // parts

    def fetch(i):
        entry = jnp.maximum(entry_ref[i], 0)
        source = amp_ref.at[entry // slots, entry % slots]
        return pltpu.make_async_copy(source, block_ref.at[i], in_sem.at[i])

    def leave(z, k):
        i = z * length + k
        return [
            pltpu.make_async_copy(
                block_ref.at[
                    i,
                    :,
                    pl.ds(pl.multiple_of((v * group + (place_ref[0] ^ j)) * width, width), width),
                ],
                out_refs[z * group + j].at[k, :, pl.ds(v * width, width)],
                out_sem.at[i],
            )
            for j in range(group)
            for v in range(parts)
        ]

    def each(act):
        for z in range(groups):

            def step(k, carry, z=z):
                pl.when(entry_ref[z * length + k] >= 0)(lambda: act(z, k))
                return carry

            lax.fori_loop(0, length, step, 0)

    def turn(z, k):
        fetch(z * length + k).wait()
        for copy in leave(z, k):
            copy.start()

    def finish(z, k):
        for copy in leave(z, k):
            copy.wait()

    each(lambda z, k: fetch(z * length + k).start())
    each(turn)
    each(finish)


def pack(entries, place, amplitudes, parts):
    _, slots, rows, size = amplitudes.shape
    groups, length = entries.shape
    across = size // GROUP
    return pl.pallas_call(
        functools.partial(pack_kernel, parts),
        grid_spec=pltpu.PrefetchScalarGridSpec(
            num_scalar_prefetch=2,
            grid=(1,),
            in_specs=[pl.BlockSpec(memory_space=pl.ANY)],
            out_specs=[pl.BlockSpec(memory_space=pl.ANY)] * (groups * GROUP),
            scratch_shapes=[
                pltpu.VMEM((groups * length, rows, size), amplitudes.dtype),
                pltpu.SemaphoreType.DMA((groups * length,)),
                pltpu.SemaphoreType.DMA((groups * length,)),
            ],
        ),
        out_shape=[jax.ShapeDtypeStruct((length, rows, across), amplitudes.dtype)]
        * (groups * GROUP),
        compiler_params=pltpu.CompilerParams(vmem_limit_bytes=VMEM_LIMIT),
        cost_estimate=pl.CostEstimate(
            flops=0, bytes_accessed=4 * groups * length * rows * size, transcendentals=0
        ),
        name="pack",
    )(entries.reshape(-1), place.reshape(1), amplitudes)


def pack_all_kernel(parts, entry_ref, amp_ref, out_ref, block_ref, in_sem, out_sem):
    groups, group, length, _, across = out_ref.shape
    slots = amp_ref.shape[1]
    width = across // parts

    def fetch(i):
        entry = jnp.maximum(entry_ref[i], 0)
        source = amp_ref.at[entry // slots, entry % slots]
        return pltpu.make_async_copy(source, block_ref.at[i], in_sem.at[i])

    def leave(i):
        return [
            pltpu.make_async_copy(
                block_ref.at[i, :, pl.ds((v * group + j) * width, width)],
                out_ref.at[i // length, j, i % length, :, pl.ds(v * width, width)],
                out_sem.at[i],
            )
            for j in range(group)
            for v in range(parts)
        ]

    def each(act):
        def step(i, carry):
            pl.when(entry_ref[i] >= 0)(lambda: act(i))
            return carry

        lax.fori_loop(0, groups * length, step, 0)

    def turn(i):
        fetch(i).wait()
        for copy in leave(i):
            copy.start()

    def finish(i):
        for copy in leave(i):
            copy.wait()

    each(lambda i: fetch(i).start())
    each(turn)
    each(finish)


def pack_all(entries, amplitudes, parts):
    _, slots, rows, size = amplitudes.shape
    groups, length = entries.shape
    across = size // GROUP
    return pl.pallas_call(
        functools.partial(pack_all_kernel, parts),
        grid_spec=pltpu.PrefetchScalarGridSpec(
            num_scalar_prefetch=1,
            grid=(1,),
            in_specs=[pl.BlockSpec(memory_space=pl.ANY)],
            out_specs=pl.BlockSpec(memory_space=pl.ANY),
            scratch_shapes=[
                pltpu.VMEM((groups * length, rows, size), amplitudes.dtype),
                pltpu.SemaphoreType.DMA((groups * length,)),
                pltpu.SemaphoreType.DMA((groups * length,)),
            ],
        ),
        out_shape=jax.ShapeDtypeStruct((groups, GROUP, length, rows, across), amplitudes.dtype),
        compiler_params=pltpu.CompilerParams(vmem_limit_bytes=VMEM_LIMIT),
        cost_estimate=pl.CostEstimate(
            flops=0, bytes_accessed=4 * groups * length * rows * size, transcendentals=0
        ),
        name="pack_all",
    )(entries.reshape(-1), amplitudes)


def ladder_kernel(counts, arrays, tile_ref, row_ref, part_ref, acc_in_ref, *refs):
    x_refs, piece_refs = refs[:arrays], refs[arrays:-5]
    acc_ref, block_ref, panel_ref, block_sem, panel_sem = refs[-5:]
    parts, _, width, _ = panel_ref.shape
    length = block_ref.shape[1]
    copies = []
    for r in range(parts):
        first = 0
        for i, count in enumerate(counts):
            copies.append(
                pltpu.make_async_copy(
                    piece_refs[r * len(counts) + i],
                    panel_ref.at[r, pl.ds(first, count)],
                    panel_sem.at[r, i],
                )
            )
            first += count
    blocks = [
        pltpu.make_async_copy(x_ref, block_ref.at[a], block_sem.at[a])
        for a, x_ref in enumerate(x_refs)
    ]
    for copy in copies + blocks:
        copy.start()
    acc_ref[...] = acc_in_ref[...]
    for copy in copies:
        copy.wait()
    for a, copy in enumerate(blocks):
        copy.wait()

        def step(k, carry, a=a):
            tile = tile_ref[a * length + k]

            @pl.when(tile >= 0)
            def _():
                row = row_ref[a * length + k]
                value = acc_ref[row]
                for r in range(parts):
                    first = pl.multiple_of(part_ref[r] * width, width)
                    value = value + jnp.dot(
                        block_ref[a, k, :, pl.ds(first, width)],
                        panel_ref[r, tile],
                        preferred_element_type=jnp.float32,
                    )
                acc_ref[row] = value

            return carry

        lax.fori_loop(0, length, step, 0)


def ladder(lists, acc, blocks, parts, pieces):
    tile, row = lists
    length, rows, across = blocks[0].shape
    counts = tuple(x.shape[0] for x in pieces[0])
    _, width, panel_width = pieces[0][0].shape
    flat = [x for piece in pieces for x in piece]
    whole = pl.BlockSpec(acc.shape, lambda i, *_: (0, 0, 0))
    return pl.pallas_call(
        functools.partial(ladder_kernel, counts, len(blocks)),
        grid_spec=pltpu.PrefetchScalarGridSpec(
            num_scalar_prefetch=3,
            grid=(1,),
            in_specs=[whole] + [pl.BlockSpec(memory_space=pl.ANY)] * (len(blocks) + len(flat)),
            out_specs=whole,
            scratch_shapes=[
                pltpu.VMEM((len(blocks), length, rows, across), blocks[0].dtype),
                pltpu.VMEM((len(pieces), sum(counts), width, panel_width), blocks[0].dtype),
                pltpu.SemaphoreType.DMA((len(blocks),)),
                pltpu.SemaphoreType.DMA((len(pieces), len(counts))),
            ],
        ),
        out_shape=jax.ShapeDtypeStruct(acc.shape, jnp.float32),
        input_output_aliases={3: 0},
        compiler_params=pltpu.CompilerParams(vmem_limit_bytes=VMEM_LIMIT),
        cost_estimate=pl.CostEstimate(
            flops=2 * len(pieces) * len(blocks) * length * rows * width * panel_width,
            bytes_accessed=2 * sum(x.size for x in (*blocks, *flat)),
            transcendentals=0,
        ),
        name="ladder",
    )(tile, row, parts, acc, *blocks, *flat)


def few_kernel(
    counts, at_ref, tile_ref, row_ref, count_ref, part_ref, acc_in_ref, x_ref, *refs
):
    piece_refs, (acc_ref, block_ref, panel_ref, sem) = refs[:-4], refs[-4:]
    parts, _, width, _ = panel_ref.shape
    count = count_ref[0]

    def start(i, carry):
        pltpu.make_async_copy(x_ref.at[at_ref[i]], block_ref.at[i], sem.at[parts, i]).start()
        tile = tile_ref[i]
        for r in range(parts):
            first = 0
            for j, length in enumerate(counts):

                @pl.when(jnp.logical_and(tile >= first, tile < first + length))
                def _(r=r, j=j, first=first):
                    pltpu.make_async_copy(
                        piece_refs[r * len(counts) + j].at[tile - first],
                        panel_ref.at[r, i],
                        sem.at[r, i],
                    ).start()

                first += length
        return carry

    def step(i, carry):
        pltpu.make_async_copy(x_ref.at[0], block_ref.at[i], sem.at[parts, i]).wait()
        row = row_ref[i]
        value = acc_ref[row]
        for r in range(parts):
            pltpu.make_async_copy(piece_refs[0].at[0], panel_ref.at[r, i], sem.at[r, i]).wait()
            first = pl.multiple_of(part_ref[r] * width, width)
            value = value + jnp.dot(
                block_ref[i, :, pl.ds(first, width)],
                panel_ref[r, i],
                preferred_element_type=jnp.float32,
            )
        acc_ref[row] = value
        return carry

    lax.fori_loop(0, count, start, 0)
    acc_ref[...] = acc_in_ref[...]
    lax.fori_loop(0, count, step, 0)


def ladder_few(lists, acc, blocks, parts, pieces):
    at, tile, row, count = lists
    length, rows, across = blocks.shape
    counts = tuple(x.shape[0] for x in pieces[0])
    _, width, panel_width = pieces[0][0].shape
    flat = [x for piece in pieces for x in piece]
    whole = pl.BlockSpec(acc.shape, lambda i, *_: (0, 0, 0))
    return pl.pallas_call(
        functools.partial(few_kernel, counts),
        grid_spec=pltpu.PrefetchScalarGridSpec(
            num_scalar_prefetch=5,
            grid=(1,),
            in_specs=[whole] + [pl.BlockSpec(memory_space=pl.ANY)] * (1 + len(flat)),
            out_specs=whole,
            scratch_shapes=[
                pltpu.VMEM((length, rows, across), blocks.dtype),
                pltpu.VMEM((len(pieces), length, width, panel_width), blocks.dtype),
                pltpu.SemaphoreType.DMA((len(pieces) + 1, length)),
            ],
        ),
        out_shape=jax.ShapeDtypeStruct(acc.shape, jnp.float32),
        input_output_aliases={5: 0},
        compiler_params=pltpu.CompilerParams(vmem_limit_bytes=VMEM_LIMIT),
        name="ladder_few",
    )(at, tile, row, count, parts, acc, blocks, *flat)


def squeeze(tile, row):
    length = tile.shape[0]
    at = jnp.arange(length, dtype=jnp.int32)
    valid = tile >= 0
    ahead = jnp.cumsum(valid.astype(jnp.int32))
    count = ahead[-1]
    wanted = jnp.minimum(at, jnp.maximum(count - 1, 0))
    chosen = (valid[None, :] & (ahead[None, :] - 1 == wanted[:, None])).astype(jnp.int32)
    return [jnp.sum(chosen * c[None, :], axis=1) for c in (at, tile, row)] + [count.reshape(1)]


def residual_kernel(
    owner_ref,
    local_ref,
    count_ref,
    map_ref,
    amp_ref,
    weight_ref,
    left_ref,
    right_ref,
    out_ref,
    diag_ref,
    rows_ref,
    turned_ref,
):
    slots = owner_ref.shape[1]
    i = pl.program_id(0)
    used = i % slots < count_ref[i // slots]
    _, _, rows, size = amp_ref.shape
    vt = left_ref.shape[1]
    half = vt // 2
    lanes = 2 * vt
    pieces = size // lanes
    wide = diag_ref.shape[0]

    @pl.when(i == 0)
    def _():
        diag_ref[...] = jnp.zeros_like(diag_ref)

    @pl.when(jnp.logical_not(used))
    def _():
        out_ref[...] = jnp.zeros_like(out_ref)

    @pl.when(used)
    def _():
        for k in range(wide // vt):
            diag_ref[k * vt : (k + 1) * vt, k * vt : (k + 1) * vt] = right_ref[0]
        low = lax.broadcasted_iota(jnp.int32, (half, lanes), 1) < vt
        for k in range(pieces):
            rows_ref[pl.ds(k, rows, stride=pieces), :] = amp_ref[
                0, 0, :, k * lanes : (k + 1) * lanes
            ].astype(jnp.float32)
        for j in range(rows // 2):
            even = rows_ref[(2 * j) * pieces : (2 * j + 1) * pieces, :]
            odd = rows_ref[(2 * j + 1) * pieces : (2 * j + 2) * pieces, :]
            top = jnp.where(low, even, pltpu.roll(odd, vt, 1))
            bottom = jnp.where(low, pltpu.roll(even, vt, 1), odd)
            turned_ref[:, j * lanes : (j + 1) * lanes] = jnp.concatenate([top, bottom], 0).astype(
                jnp.bfloat16
            )
        for j in range(rows // 2):
            both = jnp.dot(
                left_ref[0],
                turned_ref[:, j * lanes : (j + 1) * lanes],
                preferred_element_type=jnp.float32,
            )
            top, bottom = both[:half], both[half:]
            rows_ref[(2 * j) * pieces : (2 * j + 1) * pieces, :] = jnp.where(
                low, top, pltpu.roll(bottom, vt, 1)
            )
            rows_ref[(2 * j + 1) * pieces : (2 * j + 2) * pieces, :] = jnp.where(
                low, pltpu.roll(top, vt, 1), bottom
            )
        for j in range(size // wide):
            at = slice(j * wide, (j + 1) * wide)
            block = amp_ref[0, 0, :, at]
            total = jnp.dot(weight_ref[0], block, preferred_element_type=jnp.float32)
            total = total + jnp.dot(block, diag_ref[...], preferred_element_type=jnp.float32)
            for k in range(wide // lanes):
                piece = j * (wide // lanes) + k
                left = rows_ref[pl.ds(piece, rows, stride=pieces), :]
                out_ref[0, 0, :, piece * lanes : (piece + 1) * lanes] = (
                    total[:, k * lanes : (k + 1) * lanes] + left
                ).astype(jnp.bfloat16)


def residual(tile_owner, tile_local, tile_counts, pair_map, amplitudes, hole_weight, fock_tiles, per_owner):
    tiles, slots, rows, size = amplitudes.shape
    tile_count, vt, _ = fock_tiles.shape
    left = fock_tiles.reshape(tile_count, vt // 2, 2, vt // 2, 2).transpose(0, 2, 1, 4, 3)
    left = left.reshape(tile_count, vt, vt)
    wide = 4 * vt

    def ident(i, owner, local, pairs):
        t, s = i // slots, i % slots
        return pairs[owner[t, s] * per_owner + local[t, s]]

    return pl.pallas_call(
        residual_kernel,
        grid_spec=pltpu.PrefetchScalarGridSpec(
            num_scalar_prefetch=4,
            grid=(tiles * slots,),
            in_specs=[
                pl.BlockSpec((1, 1, rows, size), lambda i, *_: (i // slots, i % slots, 0, 0)),
                pl.BlockSpec((1, rows, rows), lambda i, *_: (i // slots, 0, 0)),
                pl.BlockSpec(
                    (1, vt, vt), lambda i, o, l, c, m: (ident(i, o, l, m) // tile_count, 0, 0)
                ),
                pl.BlockSpec(
                    (1, vt, vt), lambda i, o, l, c, m: (ident(i, o, l, m) % tile_count, 0, 0)
                ),
            ],
            out_specs=pl.BlockSpec((1, 1, rows, size), lambda i, *_: (i // slots, i % slots, 0, 0)),
            scratch_shapes=[
                pltpu.VMEM((wide, wide), jnp.bfloat16),
                pltpu.VMEM((rows * size // (2 * vt), 2 * vt), jnp.float32),
                pltpu.VMEM((vt, rows * vt), jnp.bfloat16),
            ],
        ),
        out_shape=jax.ShapeDtypeStruct(amplitudes.shape, jnp.bfloat16),
        compiler_params=pltpu.CompilerParams(vmem_limit_bytes=VMEM_LIMIT),
        cost_estimate=pl.CostEstimate(
            flops=40 * amplitudes.size * vt, bytes_accessed=4 * amplitudes.size, transcendentals=0
        ),
        name="residual",
    )(tile_owner, tile_local, tile_counts, pair_map, amplitudes, hole_weight, left, fock_tiles)


def per_device(
    amplitudes,
    tile_counts,
    tile_owner,
    tile_local,
    pair_map,
    hole_weight,
    fock_tiles,
    ladder_panels,
):
    owners, parts = lax.axis_size("occ"), lax.axis_size("vir")
    per_owner, part_rows, panel_width = ladder_panels.shape
    tiles, slots, pair_rows, tile_size = amplitudes.shape
    groups = owners // GROUP
    width = part_rows // GROUP
    across = parts * width
    me = lax.axis_index("occ")
    place = me % GROUP
    slot_at = jnp.arange(slots, dtype=jnp.int32)
    group_at = jnp.arange(groups, dtype=jnp.int32)

    named = (slot_at < tile_counts[:, None])[None] & (tile_owner // GROUP == group_at[:, None, None])
    named = named.reshape(groups, tiles * slots)
    own_turn = jnp.cumsum(named.astype(jnp.int32), axis=1) - named
    entry_at = jnp.arange(tiles * slots, dtype=jnp.int32)

    def entries(first, length):
        at = first + jnp.arange(length, dtype=jnp.int32)
        chosen = named[:, None, :] & (own_turn[:, None, :] == at[None, :, None])
        return jnp.sum(jnp.where(chosen, entry_at + 1, 0), axis=2).astype(jnp.int32) - 1

    def send(packed):
        packed = packed.reshape((owners,) + packed.shape[2:])
        return lax.all_to_all(packed, "occ", split_axis=0, concat_axis=0, tiled=True)

    most = tiles * GROUP

    def columns(k, first, count):
        start = (jnp.int32(first), (place ^ k) * width, jnp.int32(0))
        return lax.dynamic_slice(ladder_panels, start, (count, width, panel_width))

    def swap(k, x):
        return lax.ppermute(x, "occ", [(o, o ^ k) for o in range(owners)])

    beside = me ^ jnp.arange(owners, dtype=jnp.int32)
    near = (me // GROUP) ^ group_at
    chosen = (near[:, None] == group_at[None, :]).astype(jnp.int32)
    wanted = jnp.sum(chosen[:, :, None] * entries(0, MAIN)[None], axis=1)
    main = pack(wanted, place, amplitudes, parts)
    mine = jnp.concatenate([tile_owner, tile_local, tile_counts[:, None]], axis=1)
    main, mine, late = lax.optimization_barrier((main, mine, amplitudes))
    near_far = [r ^ h for r in range(owners // 2) for h in (owners // 2, 0)]
    moved = {r: swap(r, main[r]) for r in near_far if r}
    main = [main[0]] + [moved[r] for r in range(1, owners)]
    table = lax.all_gather(mine, AXES, axis=0, tiled=True).reshape(
        owners * parts, tiles, 2 * slots + 1
    )
    shared = [columns(0, 0, per_owner)]
    shared += [swap(k, columns(k, 0, per_owner)) for k in range(1, GROUP)]

    local_residual = residual(
        tile_owner, tile_local, tile_counts, pair_map, late, hole_weight, fock_tiles, per_owner
    )
    extras = [pack_all(entries(MAIN, length), late, parts) for length in (1, 2)]

    used = slot_at < table[:, :, 2 * slots :]
    owner, local = table[:, :, :slots], table[:, :, slots : 2 * slots]
    of_group = used[..., None] & ((owner // GROUP)[..., None] == group_at)
    longest = jnp.max(jnp.sum(of_group, axis=(1, 2)))

    def of_core(x):
        x = x.reshape(owners, parts, tiles, slots)
        x = lax.dynamic_index_in_dim(x, lax.axis_index("vir"), axis=1, keepdims=False)
        return x.reshape(owners, tiles * slots)

    hit = of_core(used & (owner // GROUP == me // GROUP))
    turn = jnp.cumsum(hit.astype(jnp.int32), axis=1) - hit
    tile = of_core(((owner % GROUP) ^ place) * per_owner + local)
    row = jnp.arange(owners, dtype=jnp.int32)[:, None] * tiles + entry_at // slots

    def lists(first, length, order=None):
        at = first + jnp.arange(length, dtype=jnp.int32)
        chosen = hit[:, None, :] & (turn[:, None, :] == at[None, :, None])
        tiles_of = jnp.sum(jnp.where(chosen, tile[:, None, :] + 1, 0), axis=2) - 1
        rows_of = jnp.sum(jnp.where(chosen, row[:, None, :], 0), axis=2)
        if order is not None:
            source = (order[:, None] == jnp.arange(owners, dtype=jnp.int32)).astype(jnp.int32)
            tiles_of = jnp.sum(source[:, :, None] * tiles_of[None], axis=1)
            rows_of = jnp.sum(source[:, :, None] * rows_of[None], axis=1)
        return tiles_of.reshape(-1), rows_of.reshape(-1)

    main, extras, local_residual, shared = lax.optimization_barrier(
        (main, extras, local_residual, shared)
    )
    empty = jnp.zeros((owners * tiles, pair_rows, panel_width), jnp.float32)
    main_lists = lists(0, MAIN, beside)
    extra_lists = [squeeze(*lists(MAIN, length)) for length in range(1, most - MAIN + 1)]
    extra_entries = [entries(MAIN, length) for length in range(3, most - MAIN + 1)]
    core_parts = (lax.axis_index("vir") + jnp.arange(parts, dtype=jnp.int32)) % parts

    def some(length, main, shared, main_lists, extra_lists, extras, extra_entries, amplitudes):
        if length > len(extras):
            packed = pack_all(extra_entries[length - 1 - len(extras)], amplitudes, parts)
        elif length > 0:
            packed = extras[length - 1]
        if length > 0:
            blocks = send(packed).reshape(-1, pair_rows, across)
        panels = [shared]
        for r in range(1, parts):
            back = [(v, (v - r) % parts) for v in range(parts)]
            panels.append([lax.ppermute(x, "vir", back) for x in shared])
        acc = ladder(main_lists, empty, main, core_parts[:1], panels[:1])
        if parts > 1:
            acc = ladder(main_lists, acc, main, core_parts[1:], panels[1:])
        if length > 0:
            acc = ladder_few(extra_lists[length - 1], acc, blocks, core_parts, panels)
        return acc

    acc = lax.switch(
        jnp.maximum(longest - MAIN, 0),
        [functools.partial(some, length) for length in range(most - MAIN + 1)],
        main,
        shared,
        main_lists,
        extra_lists,
        extras,
        extra_entries,
        amplitudes,
    )
    acc = acc.reshape(owners, tiles, pair_rows, panel_width)
    acc = lax.all_to_all(acc, "occ", split_axis=0, concat_axis=0, tiled=True)
    ladder_panel = jnp.sum(acc, axis=0).astype(jnp.bfloat16)
    return (local_residual, ladder_panel)


def solution(mesh):
    in_specs = (
        P(("occ", "vir"), None, None, None),
        P(("occ", "vir")),
        P(("occ", "vir"), None),
        P(("occ", "vir"), None),
        P(),
        P(("occ", "vir"), None, None),
        P(),
        P("occ", "vir", None),
    )
    out_specs = (P(("occ", "vir"), None, None, None), P(("occ", "vir"), None, None))
    return jax.shard_map(
        per_device, mesh=mesh, in_specs=in_specs, out_specs=out_specs, check_vma=False
    )
```

```python
import functools

import jax
import jax.numpy as jnp
from jax import lax
from jax.experimental import pallas as pl
from jax.experimental.pallas import tpu as pltpu
from jax.sharding import PartitionSpec as P

AXES = ("occ", "vir")
GROUP = 4
MAIN = 4
VMEM_LIMIT = 48 * 1024 * 1024


def pack_kernel(parts, entry_ref, amp_ref, out_ref, block_ref, in_sem, out_sem):
    groups, group, length, _, across = out_ref.shape
    slots = amp_ref.shape[1]
    width = across // parts

    def fetch(i):
        entry = jnp.maximum(entry_ref[i], 0)
        source = amp_ref.at[entry // slots, entry % slots]
        return pltpu.make_async_copy(source, block_ref.at[i], in_sem.at[i])

    def leave(i):
        return [
            pltpu.make_async_copy(
                block_ref.at[i, :, pl.ds((v * group + j) * width, width)],
                out_ref.at[i // length, j, i % length, :, pl.ds(v * width, width)],
                out_sem.at[i],
            )
            for j in range(group)
            for v in range(parts)
        ]

    def each(act):
        def step(i, carry):
            pl.when(entry_ref[i] >= 0)(lambda: act(i))
            return carry

        lax.fori_loop(0, groups * length, step, 0)

    def turn(i):
        fetch(i).wait()
        for copy in leave(i):
            copy.start()

    def finish(i):
        for copy in leave(i):
            copy.wait()

    each(lambda i: fetch(i).start())
    each(turn)
    each(finish)


def pack(entries, amplitudes, parts):
    _, slots, rows, size = amplitudes.shape
    groups, length = entries.shape
    across = size // GROUP
    return pl.pallas_call(
        functools.partial(pack_kernel, parts),
        grid_spec=pltpu.PrefetchScalarGridSpec(
            num_scalar_prefetch=1,
            grid=(1,),
            in_specs=[pl.BlockSpec(memory_space=pl.ANY)],
            out_specs=pl.BlockSpec(memory_space=pl.ANY),
            scratch_shapes=[
                pltpu.VMEM((groups * length, rows, size), amplitudes.dtype),
                pltpu.SemaphoreType.DMA((groups * length,)),
                pltpu.SemaphoreType.DMA((groups * length,)),
            ],
        ),
        out_shape=jax.ShapeDtypeStruct((groups, GROUP, length, rows, across), amplitudes.dtype),
        compiler_params=pltpu.CompilerParams(vmem_limit_bytes=VMEM_LIMIT),
        cost_estimate=pl.CostEstimate(
            flops=0, bytes_accessed=4 * groups * length * rows * size, transcendentals=0
        ),
        name="pack",
    )(entries.reshape(-1), amplitudes)


def ladder_kernel(counts, tile_ref, row_ref, part_ref, acc_in_ref, x_ref, *refs):
    piece_refs, (acc_ref, panel_ref, sem) = refs[:-3], refs[-3:]
    g = pl.program_id(0)
    here = x_ref.shape[0]
    parts, _, width, _ = panel_ref.shape

    @pl.when(g == 0)
    def _():
        copies = []
        for r in range(parts):
            first = 0
            for i, count in enumerate(counts):
                copies.append(
                    pltpu.make_async_copy(
                        piece_refs[r * len(counts) + i],
                        panel_ref.at[r, pl.ds(first, count)],
                        sem.at[r, i],
                    )
                )
                first += count
        for copy in copies:
            copy.start()
        acc_ref[...] = acc_in_ref[...]
        for copy in copies:
            copy.wait()

    def step(i, carry):
        at = g * here + i
        tile = tile_ref[at]

        @pl.when(tile >= 0)
        def _():
            row = row_ref[at]
            value = acc_ref[row]
            for r in range(parts):
                first = pl.multiple_of(part_ref[r] * width, width)
                value = value + jnp.dot(
                    x_ref[i, :, pl.ds(first, width)],
                    panel_ref[r, tile],
                    preferred_element_type=jnp.float32,
                )
            acc_ref[row] = value

        return carry

    lax.fori_loop(0, here, step, 0)


def ladder(lists, acc, blocks, parts, pieces):
    tile, row = lists
    count, rows, across = blocks.shape
    counts = tuple(x.shape[0] for x in pieces[0])
    _, width, panel_width = pieces[0][0].shape
    flat = [x for piece in pieces for x in piece]
    steps = 4
    whole = pl.BlockSpec(acc.shape, lambda i, *_: (0, 0, 0))
    return pl.pallas_call(
        functools.partial(ladder_kernel, counts),
        grid_spec=pltpu.PrefetchScalarGridSpec(
            num_scalar_prefetch=3,
            grid=(steps,),
            in_specs=[whole, pl.BlockSpec((count // steps, rows, across), lambda i, *_: (i, 0, 0))]
            + [pl.BlockSpec(memory_space=pl.ANY)] * len(flat),
            out_specs=whole,
            scratch_shapes=[
                pltpu.VMEM((len(pieces), sum(counts), width, panel_width), blocks.dtype),
                pltpu.SemaphoreType.DMA((len(pieces), len(counts))),
            ],
        ),
        out_shape=jax.ShapeDtypeStruct(acc.shape, jnp.float32),
        input_output_aliases={3: 0},
        compiler_params=pltpu.CompilerParams(vmem_limit_bytes=VMEM_LIMIT),
        cost_estimate=pl.CostEstimate(
            flops=2 * len(pieces) * count * rows * width * panel_width,
            bytes_accessed=2 * (blocks.size + sum(x.size for x in flat)),
            transcendentals=0,
        ),
        name="ladder",
    )(tile, row, parts, acc, blocks, *flat)


def few_kernel(
    counts, at_ref, tile_ref, row_ref, count_ref, part_ref, acc_in_ref, x_ref, *refs
):
    piece_refs, (acc_ref, block_ref, panel_ref, sem) = refs[:-4], refs[-4:]
    parts, _, width, _ = panel_ref.shape
    count = count_ref[0]

    def start(i, carry):
        pltpu.make_async_copy(x_ref.at[at_ref[i]], block_ref.at[i], sem.at[parts, i]).start()
        tile = tile_ref[i]
        for r in range(parts):
            first = 0
            for j, length in enumerate(counts):

                @pl.when(jnp.logical_and(tile >= first, tile < first + length))
                def _(r=r, j=j, first=first):
                    pltpu.make_async_copy(
                        piece_refs[r * len(counts) + j].at[tile - first],
                        panel_ref.at[r, i],
                        sem.at[r, i],
                    ).start()

                first += length
        return carry

    def step(i, carry):
        pltpu.make_async_copy(x_ref.at[0], block_ref.at[i], sem.at[parts, i]).wait()
        row = row_ref[i]
        value = acc_ref[row]
        for r in range(parts):
            pltpu.make_async_copy(piece_refs[0].at[0], panel_ref.at[r, i], sem.at[r, i]).wait()
            first = pl.multiple_of(part_ref[r] * width, width)
            value = value + jnp.dot(
                block_ref[i, :, pl.ds(first, width)],
                panel_ref[r, i],
                preferred_element_type=jnp.float32,
            )
        acc_ref[row] = value
        return carry

    lax.fori_loop(0, count, start, 0)
    acc_ref[...] = acc_in_ref[...]
    lax.fori_loop(0, count, step, 0)


def ladder_few(lists, acc, blocks, parts, pieces):
    at, tile, row, count = lists
    length, rows, across = blocks.shape
    counts = tuple(x.shape[0] for x in pieces[0])
    _, width, panel_width = pieces[0][0].shape
    flat = [x for piece in pieces for x in piece]
    whole = pl.BlockSpec(acc.shape, lambda i, *_: (0, 0, 0))
    return pl.pallas_call(
        functools.partial(few_kernel, counts),
        grid_spec=pltpu.PrefetchScalarGridSpec(
            num_scalar_prefetch=5,
            grid=(1,),
            in_specs=[whole] + [pl.BlockSpec(memory_space=pl.ANY)] * (1 + len(flat)),
            out_specs=whole,
            scratch_shapes=[
                pltpu.VMEM((length, rows, across), blocks.dtype),
                pltpu.VMEM((len(pieces), length, width, panel_width), blocks.dtype),
                pltpu.SemaphoreType.DMA((len(pieces) + 1, length)),
            ],
        ),
        out_shape=jax.ShapeDtypeStruct(acc.shape, jnp.float32),
        input_output_aliases={5: 0},
        compiler_params=pltpu.CompilerParams(vmem_limit_bytes=VMEM_LIMIT),
        name="ladder_few",
    )(at, tile, row, count, parts, acc, blocks, *flat)


def squeeze(tile, row):
    length = tile.shape[0]
    at = jnp.arange(length, dtype=jnp.int32)
    valid = tile >= 0
    ahead = jnp.cumsum(valid.astype(jnp.int32))
    count = ahead[-1]
    wanted = jnp.minimum(at, jnp.maximum(count - 1, 0))
    chosen = (valid[None, :] & (ahead[None, :] - 1 == wanted[:, None])).astype(jnp.int32)
    return [jnp.sum(chosen * c[None, :], axis=1) for c in (at, tile, row)] + [count.reshape(1)]


def residual_kernel(
    owner_ref,
    local_ref,
    count_ref,
    map_ref,
    amp_ref,
    weight_ref,
    left_ref,
    right_ref,
    out_ref,
    diag_ref,
    rows_ref,
    turned_ref,
):
    slots = owner_ref.shape[1]
    i = pl.program_id(0)
    used = i % slots < count_ref[i // slots]
    _, _, rows, size = amp_ref.shape
    vt = left_ref.shape[1]
    half = vt // 2
    lanes = 2 * vt
    pieces = size // lanes
    wide = diag_ref.shape[0]

    @pl.when(i == 0)
    def _():
        diag_ref[...] = jnp.zeros_like(diag_ref)

    @pl.when(jnp.logical_not(used))
    def _():
        out_ref[...] = jnp.zeros_like(out_ref)

    @pl.when(used)
    def _():
        for k in range(wide // vt):
            diag_ref[k * vt : (k + 1) * vt, k * vt : (k + 1) * vt] = right_ref[0]
        low = lax.broadcasted_iota(jnp.int32, (half, lanes), 1) < vt
        for k in range(pieces):
            rows_ref[pl.ds(k, rows, stride=pieces), :] = amp_ref[
                0, 0, :, k * lanes : (k + 1) * lanes
            ].astype(jnp.float32)
        for j in range(rows // 2):
            even = rows_ref[(2 * j) * pieces : (2 * j + 1) * pieces, :]
            odd = rows_ref[(2 * j + 1) * pieces : (2 * j + 2) * pieces, :]
            top = jnp.where(low, even, pltpu.roll(odd, vt, 1))
            bottom = jnp.where(low, pltpu.roll(even, vt, 1), odd)
            turned_ref[:, j * lanes : (j + 1) * lanes] = jnp.concatenate([top, bottom], 0).astype(
                jnp.bfloat16
            )
        for j in range(rows // 2):
            both = jnp.dot(
                left_ref[0],
                turned_ref[:, j * lanes : (j + 1) * lanes],
                preferred_element_type=jnp.float32,
            )
            top, bottom = both[:half], both[half:]
            rows_ref[(2 * j) * pieces : (2 * j + 1) * pieces, :] = jnp.where(
                low, top, pltpu.roll(bottom, vt, 1)
            )
            rows_ref[(2 * j + 1) * pieces : (2 * j + 2) * pieces, :] = jnp.where(
                low, pltpu.roll(top, vt, 1), bottom
            )
        for j in range(size // wide):
            at = slice(j * wide, (j + 1) * wide)
            block = amp_ref[0, 0, :, at]
            total = jnp.dot(weight_ref[0], block, preferred_element_type=jnp.float32)
            total = total + jnp.dot(block, diag_ref[...], preferred_element_type=jnp.float32)
            for k in range(wide // lanes):
                piece = j * (wide // lanes) + k
                left = rows_ref[pl.ds(piece, rows, stride=pieces), :]
                out_ref[0, 0, :, piece * lanes : (piece + 1) * lanes] = (
                    total[:, k * lanes : (k + 1) * lanes] + left
                ).astype(jnp.bfloat16)


def residual(tile_owner, tile_local, tile_counts, pair_map, amplitudes, hole_weight, fock_tiles, per_owner):
    tiles, slots, rows, size = amplitudes.shape
    tile_count, vt, _ = fock_tiles.shape
    left = fock_tiles.reshape(tile_count, vt // 2, 2, vt // 2, 2).transpose(0, 2, 1, 4, 3)
    left = left.reshape(tile_count, vt, vt)
    wide = 4 * vt

    def ident(i, owner, local, pairs):
        t, s = i // slots, i % slots
        return pairs[owner[t, s] * per_owner + local[t, s]]

    return pl.pallas_call(
        residual_kernel,
        grid_spec=pltpu.PrefetchScalarGridSpec(
            num_scalar_prefetch=4,
            grid=(tiles * slots,),
            in_specs=[
                pl.BlockSpec((1, 1, rows, size), lambda i, *_: (i // slots, i % slots, 0, 0)),
                pl.BlockSpec((1, rows, rows), lambda i, *_: (i // slots, 0, 0)),
                pl.BlockSpec(
                    (1, vt, vt), lambda i, o, l, c, m: (ident(i, o, l, m) // tile_count, 0, 0)
                ),
                pl.BlockSpec(
                    (1, vt, vt), lambda i, o, l, c, m: (ident(i, o, l, m) % tile_count, 0, 0)
                ),
            ],
            out_specs=pl.BlockSpec((1, 1, rows, size), lambda i, *_: (i // slots, i % slots, 0, 0)),
            scratch_shapes=[
                pltpu.VMEM((wide, wide), jnp.bfloat16),
                pltpu.VMEM((rows * size // (2 * vt), 2 * vt), jnp.float32),
                pltpu.VMEM((vt, rows * vt), jnp.bfloat16),
            ],
        ),
        out_shape=jax.ShapeDtypeStruct(amplitudes.shape, jnp.bfloat16),
        compiler_params=pltpu.CompilerParams(vmem_limit_bytes=VMEM_LIMIT),
        cost_estimate=pl.CostEstimate(
            flops=40 * amplitudes.size * vt, bytes_accessed=4 * amplitudes.size, transcendentals=0
        ),
        name="residual",
    )(tile_owner, tile_local, tile_counts, pair_map, amplitudes, hole_weight, left, fock_tiles)


def per_device(
    amplitudes,
    tile_counts,
    tile_owner,
    tile_local,
    pair_map,
    hole_weight,
    fock_tiles,
    ladder_panels,
):
    owners, parts = lax.axis_size("occ"), lax.axis_size("vir")
    per_owner, part_rows, panel_width = ladder_panels.shape
    tiles, slots, pair_rows, tile_size = amplitudes.shape
    groups = owners // GROUP
    width = part_rows // GROUP
    across = parts * width
    me = lax.axis_index("occ")
    place = me % GROUP
    slot_at = jnp.arange(slots, dtype=jnp.int32)
    group_at = jnp.arange(groups, dtype=jnp.int32)

    named = (slot_at < tile_counts[:, None])[None] & (tile_owner // GROUP == group_at[:, None, None])
    named = named.reshape(groups, tiles * slots)
    own_turn = jnp.cumsum(named.astype(jnp.int32), axis=1) - named
    entry_at = jnp.arange(tiles * slots, dtype=jnp.int32)

    def entries(first, length):
        at = first + jnp.arange(length, dtype=jnp.int32)
        chosen = named[:, None, :] & (own_turn[:, None, :] == at[None, :, None])
        return jnp.sum(jnp.where(chosen, entry_at + 1, 0), axis=2).astype(jnp.int32) - 1

    def send(packed):
        packed = packed.reshape((owners,) + packed.shape[2:])
        return lax.all_to_all(packed, "occ", split_axis=0, concat_axis=0, tiled=True)

    most = tiles * GROUP

    def columns(k, first, count):
        start = (jnp.int32(first), (place ^ k) * width, jnp.int32(0))
        return lax.dynamic_slice(ladder_panels, start, (count, width, panel_width))

    def swap(k, x):
        return lax.ppermute(x, "occ", [(o, o ^ k) for o in range(owners)])

    main = pack(entries(0, MAIN), amplitudes, parts)
    mine = jnp.concatenate([tile_owner, tile_local, tile_counts[:, None]], axis=1)
    main, mine, late = lax.optimization_barrier((main, mine, amplitudes))
    main = send(main)
    table = lax.all_gather(mine, AXES, axis=0, tiled=True).reshape(
        owners * parts, tiles, 2 * slots + 1
    )
    shared = [columns(0, 0, per_owner)]
    shared += [swap(k, columns(k, 0, per_owner)) for k in range(1, GROUP)]

    local_residual = residual(
        tile_owner, tile_local, tile_counts, pair_map, late, hole_weight, fock_tiles, per_owner
    )
    extras = [pack(entries(MAIN, length), late, parts) for length in (1, 2)]

    used = slot_at < table[:, :, 2 * slots :]
    owner, local = table[:, :, :slots], table[:, :, slots : 2 * slots]
    of_group = used[..., None] & ((owner // GROUP)[..., None] == group_at)
    longest = jnp.max(jnp.sum(of_group, axis=(1, 2)))

    def of_core(x):
        x = x.reshape(owners, parts, tiles, slots)
        x = lax.dynamic_index_in_dim(x, lax.axis_index("vir"), axis=1, keepdims=False)
        return x.reshape(owners, tiles * slots)

    hit = of_core(used & (owner // GROUP == me // GROUP))
    turn = jnp.cumsum(hit.astype(jnp.int32), axis=1) - hit
    tile = of_core(((owner % GROUP) ^ place) * per_owner + local)
    source = jnp.arange(owners, dtype=jnp.int32)
    source = ((source % GROUP) ^ place) * groups + ((source // GROUP) ^ (me // GROUP))
    row = source[:, None] * tiles + entry_at // slots

    def lists(first, length):
        at = first + jnp.arange(length, dtype=jnp.int32)
        chosen = hit[:, None, :] & (turn[:, None, :] == at[None, :, None])
        tiles_of = jnp.sum(jnp.where(chosen, tile[:, None, :] + 1, 0), axis=2) - 1
        rows_of = jnp.sum(jnp.where(chosen, row[:, None, :], 0), axis=2)
        return tiles_of.reshape(-1), rows_of.reshape(-1)

    main, extras, local_residual, shared = lax.optimization_barrier(
        (main, extras, local_residual, shared)
    )
    empty = jnp.zeros((owners * tiles, pair_rows, panel_width), jnp.float32)
    main_lists = lists(0, MAIN)
    extra_lists = [squeeze(*lists(MAIN, length)) for length in range(1, most - MAIN + 1)]
    extra_entries = [entries(MAIN, length) for length in range(3, most - MAIN + 1)]
    core_parts = (lax.axis_index("vir") + jnp.arange(parts, dtype=jnp.int32)) % parts

    def some(length, main, shared, main_lists, extra_lists, extras, extra_entries, amplitudes):
        if length > len(extras):
            packed = pack(extra_entries[length - 1 - len(extras)], amplitudes, parts)
        elif length > 0:
            packed = extras[length - 1]
        if length > 0:
            blocks = send(packed).reshape(-1, pair_rows, across)
        panels = [shared]
        for r in range(1, parts):
            back = [(v, (v - r) % parts) for v in range(parts)]
            panels.append([lax.ppermute(x, "vir", back) for x in shared])
        main = main.reshape(-1, pair_rows, across)
        acc = ladder(main_lists, empty, main, core_parts[:1], panels[:1])
        if parts > 1:
            acc = ladder(main_lists, acc, main, core_parts[1:], panels[1:])
        if length > 0:
            acc = ladder_few(extra_lists[length - 1], acc, blocks, core_parts, panels)
        return acc

    acc = lax.switch(
        jnp.maximum(longest - MAIN, 0),
        [functools.partial(some, length) for length in range(most - MAIN + 1)],
        main,
        shared,
        main_lists,
        extra_lists,
        extras,
        extra_entries,
        amplitudes,
    )
    acc = acc.reshape(GROUP, groups, tiles, pair_rows, panel_width)
    acc = sum([swap(k, acc[k]) for k in range(1, GROUP)], acc[0])
    acc = sum([swap(q * GROUP, acc[q]) for q in range(1, groups)], acc[0])
    return (local_residual, acc.astype(jnp.bfloat16))


def solution(mesh):
    in_specs = (
        P(("occ", "vir"), None, None, None),
        P(("occ", "vir")),
        P(("occ", "vir"), None),
        P(("occ", "vir"), None),
        P(),
        P(("occ", "vir"), None, None),
        P(),
        P("occ", "vir", None),
    )
    out_specs = (P(("occ", "vir"), None, None, None), P(("occ", "vir"), None, None))
    return jax.shard_map(
        per_device, mesh=mesh, in_specs=in_specs, out_specs=out_specs, check_vma=False
    )
```

```python
import functools

import jax
import jax.numpy as jnp
from jax import lax
from jax.experimental import pallas as pl
from jax.experimental.pallas import tpu as pltpu
from jax.sharding import PartitionSpec as P

AXES = ("occ", "vir")
GROUP = 4
MAIN = 4
VMEM_LIMIT = 48 * 1024 * 1024


def pack_kernel(parts, entry_ref, amp_ref, out_ref, block_ref, in_sem, out_sem):
    groups, group, length, _, across = out_ref.shape
    slots = amp_ref.shape[1]
    width = across // parts

    def fetch(i):
        entry = jnp.maximum(entry_ref[i], 0)
        source = amp_ref.at[entry // slots, entry % slots]
        return pltpu.make_async_copy(source, block_ref.at[i], in_sem.at[i])

    def leave(i):
        return [
            pltpu.make_async_copy(
                block_ref.at[i, :, pl.ds((v * group + j) * width, width)],
                out_ref.at[i // length, j, i % length, :, pl.ds(v * width, width)],
                out_sem.at[i],
            )
            for j in range(group)
            for v in range(parts)
        ]

    def each(act):
        def step(i, carry):
            pl.when(entry_ref[i] >= 0)(lambda: act(i))
            return carry

        lax.fori_loop(0, groups * length, step, 0)

    def turn(i):
        fetch(i).wait()
        for copy in leave(i):
            copy.start()

    def finish(i):
        for copy in leave(i):
            copy.wait()

    each(lambda i: fetch(i).start())
    each(turn)
    each(finish)


def pack(entries, amplitudes, parts):
    _, slots, rows, size = amplitudes.shape
    groups, length = entries.shape
    across = size // GROUP
    return pl.pallas_call(
        functools.partial(pack_kernel, parts),
        grid_spec=pltpu.PrefetchScalarGridSpec(
            num_scalar_prefetch=1,
            grid=(1,),
            in_specs=[pl.BlockSpec(memory_space=pl.ANY)],
            out_specs=pl.BlockSpec(memory_space=pl.ANY),
            scratch_shapes=[
                pltpu.VMEM((groups * length, rows, size), amplitudes.dtype),
                pltpu.SemaphoreType.DMA((groups * length,)),
                pltpu.SemaphoreType.DMA((groups * length,)),
            ],
        ),
        out_shape=jax.ShapeDtypeStruct((groups, GROUP, length, rows, across), amplitudes.dtype),
        compiler_params=pltpu.CompilerParams(vmem_limit_bytes=VMEM_LIMIT),
        cost_estimate=pl.CostEstimate(
            flops=0, bytes_accessed=4 * groups * length * rows * size, transcendentals=0
        ),
        name="pack",
    )(entries.reshape(-1), amplitudes)


def ladder_kernel(counts, tile_ref, row_ref, part_ref, acc_in_ref, x_ref, *refs):
    piece_refs, (acc_ref, panel_ref, sem) = refs[:-3], refs[-3:]
    g = pl.program_id(0)
    here = x_ref.shape[0]
    parts, _, width, _ = panel_ref.shape

    @pl.when(g == 0)
    def _():
        copies = []
        for r in range(parts):
            first = 0
            for i, count in enumerate(counts):
                copies.append(
                    pltpu.make_async_copy(
                        piece_refs[r * len(counts) + i],
                        panel_ref.at[r, pl.ds(first, count)],
                        sem.at[r, i],
                    )
                )
                first += count
        for copy in copies:
            copy.start()
        acc_ref[...] = acc_in_ref[...]
        for copy in copies:
            copy.wait()

    def step(i, carry):
        at = g * here + i
        tile = tile_ref[at]

        @pl.when(tile >= 0)
        def _():
            row = row_ref[at]
            value = acc_ref[row]
            for r in range(parts):
                first = pl.multiple_of(part_ref[r] * width, width)
                value = value + jnp.dot(
                    x_ref[i, :, pl.ds(first, width)],
                    panel_ref[r, tile],
                    preferred_element_type=jnp.float32,
                )
            acc_ref[row] = value

        return carry

    lax.fori_loop(0, here, step, 0)


def ladder(lists, acc, blocks, parts, pieces):
    tile, row = lists
    count, rows, across = blocks.shape
    counts = tuple(x.shape[0] for x in pieces[0])
    _, width, panel_width = pieces[0][0].shape
    flat = [x for piece in pieces for x in piece]
    steps = 4
    whole = pl.BlockSpec(acc.shape, lambda i, *_: (0, 0, 0))
    return pl.pallas_call(
        functools.partial(ladder_kernel, counts),
        grid_spec=pltpu.PrefetchScalarGridSpec(
            num_scalar_prefetch=3,
            grid=(steps,),
            in_specs=[whole, pl.BlockSpec((count // steps, rows, across), lambda i, *_: (i, 0, 0))]
            + [pl.BlockSpec(memory_space=pl.ANY)] * len(flat),
            out_specs=whole,
            scratch_shapes=[
                pltpu.VMEM((len(pieces), sum(counts), width, panel_width), blocks.dtype),
                pltpu.SemaphoreType.DMA((len(pieces), len(counts))),
            ],
        ),
        out_shape=jax.ShapeDtypeStruct(acc.shape, jnp.float32),
        input_output_aliases={3: 0},
        compiler_params=pltpu.CompilerParams(vmem_limit_bytes=VMEM_LIMIT),
        cost_estimate=pl.CostEstimate(
            flops=2 * len(pieces) * count * rows * width * panel_width,
            bytes_accessed=2 * (blocks.size + sum(x.size for x in flat)),
            transcendentals=0,
        ),
        name="ladder",
    )(tile, row, parts, acc, blocks, *flat)


def few_kernel(
    counts, at_ref, tile_ref, row_ref, count_ref, part_ref, acc_in_ref, x_ref, *refs
):
    piece_refs, (acc_ref, block_ref, panel_ref, sem) = refs[:-4], refs[-4:]
    parts, _, width, _ = panel_ref.shape
    count = count_ref[0]

    def start(i, carry):
        pltpu.make_async_copy(x_ref.at[at_ref[i]], block_ref.at[i], sem.at[parts, i]).start()
        tile = tile_ref[i]
        for r in range(parts):
            first = 0
            for j, length in enumerate(counts):

                @pl.when(jnp.logical_and(tile >= first, tile < first + length))
                def _(r=r, j=j, first=first):
                    pltpu.make_async_copy(
                        piece_refs[r * len(counts) + j].at[tile - first],
                        panel_ref.at[r, i],
                        sem.at[r, i],
                    ).start()

                first += length
        return carry

    def step(i, carry):
        pltpu.make_async_copy(x_ref.at[0], block_ref.at[i], sem.at[parts, i]).wait()
        row = row_ref[i]
        value = acc_ref[row]
        for r in range(parts):
            pltpu.make_async_copy(piece_refs[0].at[0], panel_ref.at[r, i], sem.at[r, i]).wait()
            first = pl.multiple_of(part_ref[r] * width, width)
            value = value + jnp.dot(
                block_ref[i, :, pl.ds(first, width)],
                panel_ref[r, i],
                preferred_element_type=jnp.float32,
            )
        acc_ref[row] = value
        return carry

    lax.fori_loop(0, count, start, 0)
    acc_ref[...] = acc_in_ref[...]
    lax.fori_loop(0, count, step, 0)


def ladder_few(lists, acc, blocks, parts, pieces):
    at, tile, row, count = lists
    length, rows, across = blocks.shape
    counts = tuple(x.shape[0] for x in pieces[0])
    _, width, panel_width = pieces[0][0].shape
    flat = [x for piece in pieces for x in piece]
    whole = pl.BlockSpec(acc.shape, lambda i, *_: (0, 0, 0))
    return pl.pallas_call(
        functools.partial(few_kernel, counts),
        grid_spec=pltpu.PrefetchScalarGridSpec(
            num_scalar_prefetch=5,
            grid=(1,),
            in_specs=[whole] + [pl.BlockSpec(memory_space=pl.ANY)] * (1 + len(flat)),
            out_specs=whole,
            scratch_shapes=[
                pltpu.VMEM((length, rows, across), blocks.dtype),
                pltpu.VMEM((len(pieces), length, width, panel_width), blocks.dtype),
                pltpu.SemaphoreType.DMA((len(pieces) + 1, length)),
            ],
        ),
        out_shape=jax.ShapeDtypeStruct(acc.shape, jnp.float32),
        input_output_aliases={5: 0},
        compiler_params=pltpu.CompilerParams(vmem_limit_bytes=VMEM_LIMIT),
        name="ladder_few",
    )(at, tile, row, count, parts, acc, blocks, *flat)


def squeeze(tile, row):
    length = tile.shape[0]
    at = jnp.arange(length, dtype=jnp.int32)
    valid = tile >= 0
    ahead = jnp.cumsum(valid.astype(jnp.int32))
    count = ahead[-1]
    wanted = jnp.minimum(at, jnp.maximum(count - 1, 0))
    chosen = (valid[None, :] & (ahead[None, :] - 1 == wanted[:, None])).astype(jnp.int32)
    return [jnp.sum(chosen * c[None, :], axis=1) for c in (at, tile, row)] + [count.reshape(1)]


def residual_kernel(
    owner_ref,
    local_ref,
    count_ref,
    map_ref,
    amp_ref,
    weight_ref,
    left_ref,
    right_ref,
    out_ref,
    diag_ref,
    rows_ref,
    turned_ref,
):
    slots = owner_ref.shape[1]
    i = pl.program_id(0)
    used = i % slots < count_ref[i // slots]
    _, _, rows, size = amp_ref.shape
    vt = left_ref.shape[1]
    half = vt // 2
    lanes = 2 * vt
    pieces = size // lanes
    wide = diag_ref.shape[0]

    @pl.when(i == 0)
    def _():
        diag_ref[...] = jnp.zeros_like(diag_ref)

    @pl.when(jnp.logical_not(used))
    def _():
        out_ref[...] = jnp.zeros_like(out_ref)

    @pl.when(used)
    def _():
        for k in range(wide // vt):
            diag_ref[k * vt : (k + 1) * vt, k * vt : (k + 1) * vt] = right_ref[0]
        low = lax.broadcasted_iota(jnp.int32, (half, lanes), 1) < vt
        for k in range(pieces):
            rows_ref[pl.ds(k, rows, stride=pieces), :] = amp_ref[
                0, 0, :, k * lanes : (k + 1) * lanes
            ].astype(jnp.float32)
        for j in range(rows // 2):
            even = rows_ref[(2 * j) * pieces : (2 * j + 1) * pieces, :]
            odd = rows_ref[(2 * j + 1) * pieces : (2 * j + 2) * pieces, :]
            top = jnp.where(low, even, pltpu.roll(odd, vt, 1))
            bottom = jnp.where(low, pltpu.roll(even, vt, 1), odd)
            turned_ref[:, j * lanes : (j + 1) * lanes] = jnp.concatenate([top, bottom], 0).astype(
                jnp.bfloat16
            )
        for j in range(rows // 2):
            both = jnp.dot(
                left_ref[0],
                turned_ref[:, j * lanes : (j + 1) * lanes],
                preferred_element_type=jnp.float32,
            )
            top, bottom = both[:half], both[half:]
            rows_ref[(2 * j) * pieces : (2 * j + 1) * pieces, :] = jnp.where(
                low, top, pltpu.roll(bottom, vt, 1)
            )
            rows_ref[(2 * j + 1) * pieces : (2 * j + 2) * pieces, :] = jnp.where(
                low, pltpu.roll(top, vt, 1), bottom
            )
        for j in range(size // wide):
            at = slice(j * wide, (j + 1) * wide)
            block = amp_ref[0, 0, :, at]
            total = jnp.dot(weight_ref[0], block, preferred_element_type=jnp.float32)
            total = total + jnp.dot(block, diag_ref[...], preferred_element_type=jnp.float32)
            for k in range(wide // lanes):
                piece = j * (wide // lanes) + k
                left = rows_ref[pl.ds(piece, rows, stride=pieces), :]
                out_ref[0, 0, :, piece * lanes : (piece + 1) * lanes] = (
                    total[:, k * lanes : (k + 1) * lanes] + left
                ).astype(jnp.bfloat16)


def residual(tile_owner, tile_local, tile_counts, pair_map, amplitudes, hole_weight, fock_tiles, per_owner):
    tiles, slots, rows, size = amplitudes.shape
    tile_count, vt, _ = fock_tiles.shape
    left = fock_tiles.reshape(tile_count, vt // 2, 2, vt // 2, 2).transpose(0, 2, 1, 4, 3)
    left = left.reshape(tile_count, vt, vt)
    wide = 4 * vt

    def ident(i, owner, local, pairs):
        t, s = i // slots, i % slots
        return pairs[owner[t, s] * per_owner + local[t, s]]

    return pl.pallas_call(
        residual_kernel,
        grid_spec=pltpu.PrefetchScalarGridSpec(
            num_scalar_prefetch=4,
            grid=(tiles * slots,),
            in_specs=[
                pl.BlockSpec((1, 1, rows, size), lambda i, *_: (i // slots, i % slots, 0, 0)),
                pl.BlockSpec((1, rows, rows), lambda i, *_: (i // slots, 0, 0)),
                pl.BlockSpec(
                    (1, vt, vt), lambda i, o, l, c, m: (ident(i, o, l, m) // tile_count, 0, 0)
                ),
                pl.BlockSpec(
                    (1, vt, vt), lambda i, o, l, c, m: (ident(i, o, l, m) % tile_count, 0, 0)
                ),
            ],
            out_specs=pl.BlockSpec((1, 1, rows, size), lambda i, *_: (i // slots, i % slots, 0, 0)),
            scratch_shapes=[
                pltpu.VMEM((wide, wide), jnp.bfloat16),
                pltpu.VMEM((rows * size // (2 * vt), 2 * vt), jnp.float32),
                pltpu.VMEM((vt, rows * vt), jnp.bfloat16),
            ],
        ),
        out_shape=jax.ShapeDtypeStruct(amplitudes.shape, jnp.bfloat16),
        compiler_params=pltpu.CompilerParams(vmem_limit_bytes=VMEM_LIMIT),
        cost_estimate=pl.CostEstimate(
            flops=40 * amplitudes.size * vt, bytes_accessed=4 * amplitudes.size, transcendentals=0
        ),
        name="residual",
    )(tile_owner, tile_local, tile_counts, pair_map, amplitudes, hole_weight, left, fock_tiles)


def per_device(
    amplitudes,
    tile_counts,
    tile_owner,
    tile_local,
    pair_map,
    hole_weight,
    fock_tiles,
    ladder_panels,
):
    owners, parts = lax.axis_size("occ"), lax.axis_size("vir")
    per_owner, part_rows, panel_width = ladder_panels.shape
    tiles, slots, pair_rows, tile_size = amplitudes.shape
    groups = owners // GROUP
    width = part_rows // GROUP
    across = parts * width
    me = lax.axis_index("occ")
    place = me % GROUP
    slot_at = jnp.arange(slots, dtype=jnp.int32)
    group_at = jnp.arange(groups, dtype=jnp.int32)

    named = (slot_at < tile_counts[:, None])[None] & (tile_owner // GROUP == group_at[:, None, None])
    named = named.reshape(groups, tiles * slots)
    own_turn = jnp.cumsum(named.astype(jnp.int32), axis=1) - named
    entry_at = jnp.arange(tiles * slots, dtype=jnp.int32)

    def entries(first, length):
        at = first + jnp.arange(length, dtype=jnp.int32)
        chosen = named[:, None, :] & (own_turn[:, None, :] == at[None, :, None])
        return jnp.sum(jnp.where(chosen, entry_at + 1, 0), axis=2).astype(jnp.int32) - 1

    def send(packed):
        packed = packed.reshape((owners,) + packed.shape[2:])
        return lax.all_to_all(packed, "occ", split_axis=0, concat_axis=0, tiled=True)

    most = tiles * GROUP

    def columns(k, first, count):
        start = (jnp.int32(first), (place ^ k) * width, jnp.int32(0))
        return lax.dynamic_slice(ladder_panels, start, (count, width, panel_width))

    def swap(k, x):
        return lax.ppermute(x, "occ", [(o, o ^ k) for o in range(owners)])

    main = pack(entries(0, MAIN), amplitudes, parts)
    mine = jnp.concatenate([tile_owner, tile_local, tile_counts[:, None]], axis=1)
    table = lax.all_to_all(
        jnp.broadcast_to(mine, (owners * parts,) + mine.shape), AXES, 0, 0, tiled=True
    )
    main, table, late = lax.optimization_barrier((main, table, amplitudes))
    main = send(main)
    shared = [columns(0, 0, per_owner)]
    shared += [swap(k, columns(k, 0, per_owner)) for k in range(1, GROUP)]

    local_residual = residual(
        tile_owner, tile_local, tile_counts, pair_map, late, hole_weight, fock_tiles, per_owner
    )
    extras = [pack(entries(MAIN, length), late, parts) for length in (1, 2)]

    used = slot_at < table[:, :, 2 * slots :]
    owner, local = table[:, :, :slots], table[:, :, slots : 2 * slots]
    of_group = used[..., None] & ((owner // GROUP)[..., None] == group_at)
    longest = jnp.max(jnp.sum(of_group, axis=(1, 2)))

    def of_core(x):
        x = x.reshape(owners, parts, tiles, slots)
        x = lax.dynamic_index_in_dim(x, lax.axis_index("vir"), axis=1, keepdims=False)
        return x.reshape(owners, tiles * slots)

    hit = of_core(used & (owner // GROUP == me // GROUP))
    turn = jnp.cumsum(hit.astype(jnp.int32), axis=1) - hit
    tile = of_core(((owner % GROUP) ^ place) * per_owner + local)
    source = jnp.arange(owners, dtype=jnp.int32)
    source = ((source % GROUP) ^ place) * groups + ((source // GROUP) ^ (me // GROUP))
    row = source[:, None] * tiles + entry_at // slots

    def lists(first, length):
        at = first + jnp.arange(length, dtype=jnp.int32)
        chosen = hit[:, None, :] & (turn[:, None, :] == at[None, :, None])
        tiles_of = jnp.sum(jnp.where(chosen, tile[:, None, :] + 1, 0), axis=2) - 1
        rows_of = jnp.sum(jnp.where(chosen, row[:, None, :], 0), axis=2)
        return tiles_of.reshape(-1), rows_of.reshape(-1)

    main, extras, local_residual, shared = lax.optimization_barrier(
        (main, extras, local_residual, shared)
    )
    empty = jnp.zeros((owners * tiles, pair_rows, panel_width), jnp.float32)
    main_lists = lists(0, MAIN)
    extra_lists = [squeeze(*lists(MAIN, length)) for length in range(1, most - MAIN + 1)]
    extra_entries = [entries(MAIN, length) for length in range(3, most - MAIN + 1)]
    core_parts = (lax.axis_index("vir") + jnp.arange(parts, dtype=jnp.int32)) % parts

    def some(length, main, shared, main_lists, extra_lists, extras, extra_entries, amplitudes):
        if length > len(extras):
            packed = pack(extra_entries[length - 1 - len(extras)], amplitudes, parts)
        elif length > 0:
            packed = extras[length - 1]
        if length > 0:
            blocks = send(packed).reshape(-1, pair_rows, across)
        panels = [shared]
        for r in range(1, parts):
            back = [(v, (v - r) % parts) for v in range(parts)]
            panels.append([lax.ppermute(x, "vir", back) for x in shared])
        main = main.reshape(-1, pair_rows, across)
        acc = ladder(main_lists, empty, main, core_parts[:1], panels[:1])
        if parts > 1:
            acc = ladder(main_lists, acc, main, core_parts[1:], panels[1:])
        if length > 0:
            acc = ladder_few(extra_lists[length - 1], acc, blocks, core_parts, panels)
        return acc

    acc = lax.switch(
        jnp.maximum(longest - MAIN, 0),
        [functools.partial(some, length) for length in range(most - MAIN + 1)],
        main,
        shared,
        main_lists,
        extra_lists,
        extras,
        extra_entries,
        amplitudes,
    )
    acc = acc.reshape(GROUP, groups, tiles, pair_rows, panel_width)
    acc = sum([swap(k, acc[k]) for k in range(1, GROUP)], acc[0])
    acc = sum([swap(q * GROUP, acc[q]) for q in range(1, groups)], acc[0])
    return (local_residual, acc.astype(jnp.bfloat16))


def solution(mesh):
    in_specs = (
        P(("occ", "vir"), None, None, None),
        P(("occ", "vir")),
        P(("occ", "vir"), None),
        P(("occ", "vir"), None),
        P(),
        P(("occ", "vir"), None, None),
        P(),
        P("occ", "vir", None),
    )
    out_specs = (P(("occ", "vir"), None, None, None), P(("occ", "vir"), None, None))
    return jax.shard_map(
        per_device, mesh=mesh, in_specs=in_specs, out_specs=out_specs, check_vma=False
    )
```

```python
import functools

import jax
import jax.numpy as jnp
from jax import lax
from jax.experimental import pallas as pl
from jax.experimental.pallas import tpu as pltpu
from jax.sharding import PartitionSpec as P

AXES = ("occ", "vir")
GROUP = 4
MAIN = 4
VMEM_LIMIT = 48 * 1024 * 1024


def pack_kernel(parts, entry_ref, amp_ref, out_ref, block_ref, in_sem, out_sem):
    groups, group, length, _, across = out_ref.shape
    slots = amp_ref.shape[1]
    width = across // parts

    def fetch(i):
        entry = jnp.maximum(entry_ref[i], 0)
        source = amp_ref.at[entry // slots, entry % slots]
        return pltpu.make_async_copy(source, block_ref.at[i], in_sem.at[i])

    def leave(i):
        return [
            pltpu.make_async_copy(
                block_ref.at[i, :, pl.ds((v * group + j) * width, width)],
                out_ref.at[i // length, j, i % length, :, pl.ds(v * width, width)],
                out_sem.at[i],
            )
            for j in range(group)
            for v in range(parts)
        ]

    def each(act):
        def step(i, carry):
            pl.when(entry_ref[i] >= 0)(lambda: act(i))
            return carry

        lax.fori_loop(0, groups * length, step, 0)

    def turn(i):
        fetch(i).wait()
        for copy in leave(i):
            copy.start()

    def finish(i):
        for copy in leave(i):
            copy.wait()

    each(lambda i: fetch(i).start())
    each(turn)
    each(finish)


def pack(entries, amplitudes, parts):
    _, slots, rows, size = amplitudes.shape
    groups, length = entries.shape
    across = size // GROUP
    return pl.pallas_call(
        functools.partial(pack_kernel, parts),
        grid_spec=pltpu.PrefetchScalarGridSpec(
            num_scalar_prefetch=1,
            grid=(1,),
            in_specs=[pl.BlockSpec(memory_space=pl.ANY)],
            out_specs=pl.BlockSpec(memory_space=pl.ANY),
            scratch_shapes=[
                pltpu.VMEM((groups * length, rows, size), amplitudes.dtype),
                pltpu.SemaphoreType.DMA((groups * length,)),
                pltpu.SemaphoreType.DMA((groups * length,)),
            ],
        ),
        out_shape=jax.ShapeDtypeStruct((groups, GROUP, length, rows, across), amplitudes.dtype),
        compiler_params=pltpu.CompilerParams(vmem_limit_bytes=VMEM_LIMIT),
        cost_estimate=pl.CostEstimate(
            flops=0, bytes_accessed=4 * groups * length * rows * size, transcendentals=0
        ),
        name="pack",
    )(entries.reshape(-1), amplitudes)


def ladder_kernel(counts, tile_ref, row_ref, part_ref, acc_in_ref, x_ref, *refs):
    piece_refs, (acc_ref, panel_ref, sem) = refs[:-3], refs[-3:]
    g = pl.program_id(0)
    here = x_ref.shape[0]
    parts, _, width, _ = panel_ref.shape

    @pl.when(g == 0)
    def _():
        copies = []
        for r in range(parts):
            first = 0
            for i, count in enumerate(counts):
                copies.append(
                    pltpu.make_async_copy(
                        piece_refs[r * len(counts) + i],
                        panel_ref.at[r, pl.ds(first, count)],
                        sem.at[r, i],
                    )
                )
                first += count
        for copy in copies:
            copy.start()
        acc_ref[...] = acc_in_ref[...]
        for copy in copies:
            copy.wait()

    def step(i, carry):
        at = g * here + i
        tile = tile_ref[at]

        @pl.when(tile >= 0)
        def _():
            row = row_ref[at]
            value = acc_ref[row]
            for r in range(parts):
                first = pl.multiple_of(part_ref[r] * width, width)
                value = value + jnp.dot(
                    x_ref[i, :, pl.ds(first, width)],
                    panel_ref[r, tile],
                    preferred_element_type=jnp.float32,
                )
            acc_ref[row] = value

        return carry

    lax.fori_loop(0, here, step, 0)


def ladder(lists, acc, blocks, parts, pieces):
    tile, row = lists
    count, rows, across = blocks.shape
    counts = tuple(x.shape[0] for x in pieces[0])
    _, width, panel_width = pieces[0][0].shape
    flat = [x for piece in pieces for x in piece]
    steps = 4
    whole = pl.BlockSpec(acc.shape, lambda i, *_: (0, 0, 0))
    return pl.pallas_call(
        functools.partial(ladder_kernel, counts),
        grid_spec=pltpu.PrefetchScalarGridSpec(
            num_scalar_prefetch=3,
            grid=(steps,),
            in_specs=[whole, pl.BlockSpec((count // steps, rows, across), lambda i, *_: (i, 0, 0))]
            + [pl.BlockSpec(memory_space=pl.ANY)] * len(flat),
            out_specs=whole,
            scratch_shapes=[
                pltpu.VMEM((len(pieces), sum(counts), width, panel_width), blocks.dtype),
                pltpu.SemaphoreType.DMA((len(pieces), len(counts))),
            ],
        ),
        out_shape=jax.ShapeDtypeStruct(acc.shape, jnp.float32),
        input_output_aliases={3: 0},
        compiler_params=pltpu.CompilerParams(vmem_limit_bytes=VMEM_LIMIT),
        cost_estimate=pl.CostEstimate(
            flops=2 * len(pieces) * count * rows * width * panel_width,
            bytes_accessed=2 * (blocks.size + sum(x.size for x in flat)),
            transcendentals=0,
        ),
        name="ladder",
    )(tile, row, parts, acc, blocks, *flat)


def few_kernel(
    counts, at_ref, tile_ref, row_ref, count_ref, part_ref, acc_in_ref, x_ref, *refs
):
    piece_refs, (acc_ref, block_ref, panel_ref, sem) = refs[:-4], refs[-4:]
    parts, _, width, _ = panel_ref.shape
    count = count_ref[0]

    def start(i, carry):
        pltpu.make_async_copy(x_ref.at[at_ref[i]], block_ref.at[i], sem.at[parts, i]).start()
        tile = tile_ref[i]
        for r in range(parts):
            first = 0
            for j, length in enumerate(counts):

                @pl.when(jnp.logical_and(tile >= first, tile < first + length))
                def _(r=r, j=j, first=first):
                    pltpu.make_async_copy(
                        piece_refs[r * len(counts) + j].at[tile - first],
                        panel_ref.at[r, i],
                        sem.at[r, i],
                    ).start()

                first += length
        return carry

    def step(i, carry):
        pltpu.make_async_copy(x_ref.at[0], block_ref.at[i], sem.at[parts, i]).wait()
        row = row_ref[i]
        value = acc_ref[row]
        for r in range(parts):
            pltpu.make_async_copy(piece_refs[0].at[0], panel_ref.at[r, i], sem.at[r, i]).wait()
            first = pl.multiple_of(part_ref[r] * width, width)
            value = value + jnp.dot(
                block_ref[i, :, pl.ds(first, width)],
                panel_ref[r, i],
                preferred_element_type=jnp.float32,
            )
        acc_ref[row] = value
        return carry

    lax.fori_loop(0, count, start, 0)
    acc_ref[...] = acc_in_ref[...]
    lax.fori_loop(0, count, step, 0)


def ladder_few(lists, acc, blocks, parts, pieces):
    at, tile, row, count = lists
    length, rows, across = blocks.shape
    counts = tuple(x.shape[0] for x in pieces[0])
    _, width, panel_width = pieces[0][0].shape
    flat = [x for piece in pieces for x in piece]
    whole = pl.BlockSpec(acc.shape, lambda i, *_: (0, 0, 0))
    return pl.pallas_call(
        functools.partial(few_kernel, counts),
        grid_spec=pltpu.PrefetchScalarGridSpec(
            num_scalar_prefetch=5,
            grid=(1,),
            in_specs=[whole] + [pl.BlockSpec(memory_space=pl.ANY)] * (1 + len(flat)),
            out_specs=whole,
            scratch_shapes=[
                pltpu.VMEM((length, rows, across), blocks.dtype),
                pltpu.VMEM((len(pieces), length, width, panel_width), blocks.dtype),
                pltpu.SemaphoreType.DMA((len(pieces) + 1, length)),
            ],
        ),
        out_shape=jax.ShapeDtypeStruct(acc.shape, jnp.float32),
        input_output_aliases={5: 0},
        compiler_params=pltpu.CompilerParams(vmem_limit_bytes=VMEM_LIMIT),
        name="ladder_few",
    )(at, tile, row, count, parts, acc, blocks, *flat)


def squeeze(tile, row):
    length = tile.shape[0]
    at = jnp.arange(length, dtype=jnp.int32)
    valid = tile >= 0
    ahead = jnp.cumsum(valid.astype(jnp.int32))
    count = ahead[-1]
    wanted = jnp.minimum(at, jnp.maximum(count - 1, 0))
    chosen = (valid[None, :] & (ahead[None, :] - 1 == wanted[:, None])).astype(jnp.int32)
    return [jnp.sum(chosen * c[None, :], axis=1) for c in (at, tile, row)] + [count.reshape(1)]


def residual_kernel(
    owner_ref,
    local_ref,
    count_ref,
    map_ref,
    amp_ref,
    weight_ref,
    left_ref,
    right_ref,
    out_ref,
    diag_ref,
    rows_ref,
    turned_ref,
):
    slots = owner_ref.shape[1]
    i = pl.program_id(0)
    used = i % slots < count_ref[i // slots]
    _, _, rows, size = amp_ref.shape
    vt = left_ref.shape[1]
    half = vt // 2
    lanes = 2 * vt
    pieces = size // lanes
    wide = diag_ref.shape[0]

    @pl.when(i == 0)
    def _():
        diag_ref[...] = jnp.zeros_like(diag_ref)

    @pl.when(jnp.logical_not(used))
    def _():
        out_ref[...] = jnp.zeros_like(out_ref)

    @pl.when(used)
    def _():
        for k in range(wide // vt):
            diag_ref[k * vt : (k + 1) * vt, k * vt : (k + 1) * vt] = right_ref[0]
        low = lax.broadcasted_iota(jnp.int32, (half, lanes), 1) < vt
        for k in range(pieces):
            rows_ref[pl.ds(k, rows, stride=pieces), :] = amp_ref[
                0, 0, :, k * lanes : (k + 1) * lanes
            ].astype(jnp.float32)
        for j in range(rows // 2):
            even = rows_ref[(2 * j) * pieces : (2 * j + 1) * pieces, :]
            odd = rows_ref[(2 * j + 1) * pieces : (2 * j + 2) * pieces, :]
            top = jnp.where(low, even, pltpu.roll(odd, vt, 1))
            bottom = jnp.where(low, pltpu.roll(even, vt, 1), odd)
            turned_ref[:, j * lanes : (j + 1) * lanes] = jnp.concatenate([top, bottom], 0).astype(
                jnp.bfloat16
            )
        for j in range(rows // 2):
            both = jnp.dot(
                left_ref[0],
                turned_ref[:, j * lanes : (j + 1) * lanes],
                preferred_element_type=jnp.float32,
            )
            top, bottom = both[:half], both[half:]
            rows_ref[(2 * j) * pieces : (2 * j + 1) * pieces, :] = jnp.where(
                low, top, pltpu.roll(bottom, vt, 1)
            )
            rows_ref[(2 * j + 1) * pieces : (2 * j + 2) * pieces, :] = jnp.where(
                low, pltpu.roll(top, vt, 1), bottom
            )
        for j in range(size // wide):
            at = slice(j * wide, (j + 1) * wide)
            block = amp_ref[0, 0, :, at]
            total = jnp.dot(weight_ref[0], block, preferred_element_type=jnp.float32)
            total = total + jnp.dot(block, diag_ref[...], preferred_element_type=jnp.float32)
            for k in range(wide // lanes):
                piece = j * (wide // lanes) + k
                left = rows_ref[pl.ds(piece, rows, stride=pieces), :]
                out_ref[0, 0, :, piece * lanes : (piece + 1) * lanes] = (
                    total[:, k * lanes : (k + 1) * lanes] + left
                ).astype(jnp.bfloat16)


def residual(tile_owner, tile_local, tile_counts, pair_map, amplitudes, hole_weight, fock_tiles, per_owner):
    tiles, slots, rows, size = amplitudes.shape
    tile_count, vt, _ = fock_tiles.shape
    left = fock_tiles.reshape(tile_count, vt // 2, 2, vt // 2, 2).transpose(0, 2, 1, 4, 3)
    left = left.reshape(tile_count, vt, vt)
    wide = 4 * vt

    def ident(i, owner, local, pairs):
        t, s = i // slots, i % slots
        return pairs[owner[t, s] * per_owner + local[t, s]]

    return pl.pallas_call(
        residual_kernel,
        grid_spec=pltpu.PrefetchScalarGridSpec(
            num_scalar_prefetch=4,
            grid=(tiles * slots,),
            in_specs=[
                pl.BlockSpec((1, 1, rows, size), lambda i, *_: (i // slots, i % slots, 0, 0)),
                pl.BlockSpec((1, rows, rows), lambda i, *_: (i // slots, 0, 0)),
                pl.BlockSpec(
                    (1, vt, vt), lambda i, o, l, c, m: (ident(i, o, l, m) // tile_count, 0, 0)
                ),
                pl.BlockSpec(
                    (1, vt, vt), lambda i, o, l, c, m: (ident(i, o, l, m) % tile_count, 0, 0)
                ),
            ],
            out_specs=pl.BlockSpec((1, 1, rows, size), lambda i, *_: (i // slots, i % slots, 0, 0)),
            scratch_shapes=[
                pltpu.VMEM((wide, wide), jnp.bfloat16),
                pltpu.VMEM((rows * size // (2 * vt), 2 * vt), jnp.float32),
                pltpu.VMEM((vt, rows * vt), jnp.bfloat16),
            ],
        ),
        out_shape=jax.ShapeDtypeStruct(amplitudes.shape, jnp.bfloat16),
        compiler_params=pltpu.CompilerParams(vmem_limit_bytes=VMEM_LIMIT),
        cost_estimate=pl.CostEstimate(
            flops=40 * amplitudes.size * vt, bytes_accessed=4 * amplitudes.size, transcendentals=0
        ),
        name="residual",
    )(tile_owner, tile_local, tile_counts, pair_map, amplitudes, hole_weight, left, fock_tiles)


def per_device(
    amplitudes,
    tile_counts,
    tile_owner,
    tile_local,
    pair_map,
    hole_weight,
    fock_tiles,
    ladder_panels,
):
    owners, parts = lax.axis_size("occ"), lax.axis_size("vir")
    per_owner, part_rows, panel_width = ladder_panels.shape
    tiles, slots, pair_rows, tile_size = amplitudes.shape
    groups = owners // GROUP
    width = part_rows // GROUP
    across = parts * width
    me = lax.axis_index("occ")
    place = me % GROUP
    slot_at = jnp.arange(slots, dtype=jnp.int32)
    group_at = jnp.arange(groups, dtype=jnp.int32)

    named = (slot_at < tile_counts[:, None])[None] & (tile_owner // GROUP == group_at[:, None, None])
    named = named.reshape(groups, tiles * slots)
    own_turn = jnp.cumsum(named.astype(jnp.int32), axis=1) - named
    entry_at = jnp.arange(tiles * slots, dtype=jnp.int32)

    def entries(first, length):
        at = first + jnp.arange(length, dtype=jnp.int32)
        chosen = named[:, None, :] & (own_turn[:, None, :] == at[None, :, None])
        return jnp.sum(jnp.where(chosen, entry_at + 1, 0), axis=2).astype(jnp.int32) - 1

    def send(packed):
        packed = packed.reshape((owners,) + packed.shape[2:])
        return lax.all_to_all(packed, "occ", split_axis=0, concat_axis=0, tiled=True)

    most = tiles * GROUP

    def columns(k, first, count):
        start = (jnp.int32(first), (place ^ k) * width, jnp.int32(0))
        return lax.dynamic_slice(ladder_panels, start, (count, width, panel_width))

    def swap(k, x):
        return lax.ppermute(x, "occ", [(o, o ^ k) for o in range(owners)])

    early = per_owner // 4
    mine = jnp.concatenate([tile_owner, tile_local, tile_counts[:, None]], axis=1)
    soon = [columns(k, 0, early) for k in (1, 2)]
    soon, mine = lax.optimization_barrier((soon, mine))
    soon = [swap(k, x) for k, x in zip((1, 2), soon)]
    main = pack(entries(0, MAIN), amplitudes, parts)
    table = lax.all_to_all(
        jnp.broadcast_to(mine, (owners * parts,) + mine.shape), AXES, 0, 0, tiled=True
    )
    main, table, late, soon = lax.optimization_barrier((main, table, amplitudes, soon))
    main = send(main)
    shared = [columns(0, 0, per_owner)]
    shared += [swap(k, columns(k, early, per_owner - early)) for k in (1, 2)]
    shared += [swap(k, columns(k, 0, per_owner)) for k in range(3, GROUP)]

    local_residual = residual(
        tile_owner, tile_local, tile_counts, pair_map, late, hole_weight, fock_tiles, per_owner
    )
    extras = [pack(entries(MAIN, length), late, parts) for length in (1, 2)]

    used = slot_at < table[:, :, 2 * slots :]
    owner, local = table[:, :, :slots], table[:, :, slots : 2 * slots]
    of_group = used[..., None] & ((owner // GROUP)[..., None] == group_at)
    longest = jnp.max(jnp.sum(of_group, axis=(1, 2)))

    def of_core(x):
        x = x.reshape(owners, parts, tiles, slots)
        x = lax.dynamic_index_in_dim(x, lax.axis_index("vir"), axis=1, keepdims=False)
        return x.reshape(owners, tiles * slots)

    hit = of_core(used & (owner // GROUP == me // GROUP))
    turn = jnp.cumsum(hit.astype(jnp.int32), axis=1) - hit
    tile = of_core(((owner % GROUP) ^ place) * per_owner + local)
    source = jnp.arange(owners, dtype=jnp.int32)
    source = ((source % GROUP) ^ place) * groups + ((source // GROUP) ^ (me // GROUP))
    row = source[:, None] * tiles + entry_at // slots

    def lists(first, length):
        at = first + jnp.arange(length, dtype=jnp.int32)
        chosen = hit[:, None, :] & (turn[:, None, :] == at[None, :, None])
        tiles_of = jnp.sum(jnp.where(chosen, tile[:, None, :] + 1, 0), axis=2) - 1
        rows_of = jnp.sum(jnp.where(chosen, row[:, None, :], 0), axis=2)
        return tiles_of.reshape(-1), rows_of.reshape(-1)

    main, extras, local_residual, shared = lax.optimization_barrier(
        (main, extras, local_residual, shared)
    )
    shared = [shared[0], soon[0], shared[1], soon[1], shared[2]] + list(shared[3:])
    empty = jnp.zeros((owners * tiles, pair_rows, panel_width), jnp.float32)
    main_lists = lists(0, MAIN)
    extra_lists = [squeeze(*lists(MAIN, length)) for length in range(1, most - MAIN + 1)]
    extra_entries = [entries(MAIN, length) for length in range(3, most - MAIN + 1)]
    core_parts = (lax.axis_index("vir") + jnp.arange(parts, dtype=jnp.int32)) % parts

    def some(length, main, shared, main_lists, extra_lists, extras, extra_entries, amplitudes):
        if length > len(extras):
            packed = pack(extra_entries[length - 1 - len(extras)], amplitudes, parts)
        elif length > 0:
            packed = extras[length - 1]
        if length > 0:
            blocks = send(packed).reshape(-1, pair_rows, across)
        panels = [shared]
        for r in range(1, parts):
            back = [(v, (v - r) % parts) for v in range(parts)]
            panels.append([lax.ppermute(x, "vir", back) for x in shared])
        main = main.reshape(-1, pair_rows, across)
        acc = ladder(main_lists, empty, main, core_parts[:1], panels[:1])
        if parts > 1:
            acc = ladder(main_lists, acc, main, core_parts[1:], panels[1:])
        if length > 0:
            acc = ladder_few(extra_lists[length - 1], acc, blocks, core_parts, panels)
        return acc

    acc = lax.switch(
        jnp.maximum(longest - MAIN, 0),
        [functools.partial(some, length) for length in range(most - MAIN + 1)],
        main,
        shared,
        main_lists,
        extra_lists,
        extras,
        extra_entries,
        amplitudes,
    )
    acc = acc.reshape(GROUP, groups, tiles, pair_rows, panel_width)
    acc = sum([swap(k, acc[k]) for k in range(1, GROUP)], acc[0])
    acc = sum([swap(q * GROUP, acc[q]) for q in range(1, groups)], acc[0])
    return (local_residual, acc.astype(jnp.bfloat16))


def solution(mesh):
    in_specs = (
        P(("occ", "vir"), None, None, None),
        P(("occ", "vir")),
        P(("occ", "vir"), None),
        P(("occ", "vir"), None),
        P(),
        P(("occ", "vir"), None, None),
        P(),
        P("occ", "vir", None),
    )
    out_specs = (P(("occ", "vir"), None, None, None), P(("occ", "vir"), None, None))
    return jax.shard_map(
        per_device, mesh=mesh, in_specs=in_specs, out_specs=out_specs, check_vma=False
    )
```

```python
import functools

import jax
import jax.numpy as jnp
from jax import lax
from jax.experimental import pallas as pl
from jax.experimental.pallas import tpu as pltpu
from jax.sharding import PartitionSpec as P

AXES = ("occ", "vir")
GROUP = 4
MAIN = 4
VMEM_LIMIT = 48 * 1024 * 1024


def pack_kernel(parts, entry_ref, amp_ref, out_ref, block_ref, in_sem, out_sem):
    groups, group, length, _, across = out_ref.shape
    slots = amp_ref.shape[1]
    width = across // parts

    def fetch(i):
        entry = jnp.maximum(entry_ref[i], 0)
        source = amp_ref.at[entry // slots, entry % slots]
        return pltpu.make_async_copy(source, block_ref.at[i], in_sem.at[i])

    def leave(i):
        return [
            pltpu.make_async_copy(
                block_ref.at[i, :, pl.ds((v * group + j) * width, width)],
                out_ref.at[i // length, j, i % length, :, pl.ds(v * width, width)],
                out_sem.at[i],
            )
            for j in range(group)
            for v in range(parts)
        ]

    def each(act):
        def step(i, carry):
            pl.when(entry_ref[i] >= 0)(lambda: act(i))
            return carry

        lax.fori_loop(0, groups * length, step, 0)

    def turn(i):
        fetch(i).wait()
        for copy in leave(i):
            copy.start()

    def finish(i):
        for copy in leave(i):
            copy.wait()

    each(lambda i: fetch(i).start())
    each(turn)
    each(finish)


def pack(entries, amplitudes, parts):
    _, slots, rows, size = amplitudes.shape
    groups, length = entries.shape
    across = size // GROUP
    return pl.pallas_call(
        functools.partial(pack_kernel, parts),
        grid_spec=pltpu.PrefetchScalarGridSpec(
            num_scalar_prefetch=1,
            grid=(1,),
            in_specs=[pl.BlockSpec(memory_space=pl.ANY)],
            out_specs=pl.BlockSpec(memory_space=pl.ANY),
            scratch_shapes=[
                pltpu.VMEM((groups * length, rows, size), amplitudes.dtype),
                pltpu.SemaphoreType.DMA((groups * length,)),
                pltpu.SemaphoreType.DMA((groups * length,)),
            ],
        ),
        out_shape=jax.ShapeDtypeStruct((groups, GROUP, length, rows, across), amplitudes.dtype),
        compiler_params=pltpu.CompilerParams(vmem_limit_bytes=VMEM_LIMIT),
        cost_estimate=pl.CostEstimate(
            flops=0, bytes_accessed=4 * groups * length * rows * size, transcendentals=0
        ),
        name="pack",
    )(entries.reshape(-1), amplitudes)


def ladder_kernel(counts, tile_ref, row_ref, part_ref, acc_in_ref, x_ref, *refs):
    piece_refs, (acc_ref, panel_ref, sem) = refs[:-3], refs[-3:]
    g = pl.program_id(0)
    here = x_ref.shape[0]
    parts, _, width, _ = panel_ref.shape

    @pl.when(g == 0)
    def _():
        copies = []
        for r in range(parts):
            first = 0
            for i, count in enumerate(counts):
                copies.append(
                    pltpu.make_async_copy(
                        piece_refs[r * len(counts) + i],
                        panel_ref.at[r, pl.ds(first, count)],
                        sem.at[r, i],
                    )
                )
                first += count
        for copy in copies:
            copy.start()
        acc_ref[...] = acc_in_ref[...]
        for copy in copies:
            copy.wait()

    def step(i, carry):
        at = g * here + i
        tile = tile_ref[at]

        @pl.when(tile >= 0)
        def _():
            row = row_ref[at]
            value = acc_ref[row]
            for r in range(parts):
                first = pl.multiple_of(part_ref[r] * width, width)
                value = value + jnp.dot(
                    x_ref[i, :, pl.ds(first, width)],
                    panel_ref[r, tile],
                    preferred_element_type=jnp.float32,
                )
            acc_ref[row] = value

        return carry

    lax.fori_loop(0, here, step, 0)


def ladder(lists, acc, blocks, parts, pieces):
    tile, row = lists
    count, rows, across = blocks.shape
    counts = tuple(x.shape[0] for x in pieces[0])
    _, width, panel_width = pieces[0][0].shape
    flat = [x for piece in pieces for x in piece]
    steps = 4
    whole = pl.BlockSpec(acc.shape, lambda i, *_: (0, 0, 0))
    return pl.pallas_call(
        functools.partial(ladder_kernel, counts),
        grid_spec=pltpu.PrefetchScalarGridSpec(
            num_scalar_prefetch=3,
            grid=(steps,),
            in_specs=[whole, pl.BlockSpec((count // steps, rows, across), lambda i, *_: (i, 0, 0))]
            + [pl.BlockSpec(memory_space=pl.ANY)] * len(flat),
            out_specs=whole,
            scratch_shapes=[
                pltpu.VMEM((len(pieces), sum(counts), width, panel_width), blocks.dtype),
                pltpu.SemaphoreType.DMA((len(pieces), len(counts))),
            ],
        ),
        out_shape=jax.ShapeDtypeStruct(acc.shape, jnp.float32),
        input_output_aliases={3: 0},
        compiler_params=pltpu.CompilerParams(vmem_limit_bytes=VMEM_LIMIT),
        cost_estimate=pl.CostEstimate(
            flops=2 * len(pieces) * count * rows * width * panel_width,
            bytes_accessed=2 * (blocks.size + sum(x.size for x in flat)),
            transcendentals=0,
        ),
        name="ladder",
    )(tile, row, parts, acc, blocks, *flat)


def few_kernel(counts, at_ref, tile_ref, row_ref, count_ref, part_ref, x_ref, *refs):
    piece_refs, (acc_ref, block_ref, panel_ref, sem) = refs[:-4], refs[-4:]
    parts, _, width, _ = panel_ref.shape
    count = count_ref[0]
    pairs = (count + 1) // 2

    def start(i, carry):
        pltpu.make_async_copy(x_ref.at[at_ref[i]], block_ref.at[i], sem.at[parts, i]).start()
        tile = tile_ref[i]
        for r in range(parts):
            first = 0
            for j, length in enumerate(counts):

                @pl.when(jnp.logical_and(tile >= first, tile < first + length))
                def _(r=r, j=j, first=first):
                    pltpu.make_async_copy(
                        piece_refs[r * len(counts) + j].at[tile - first],
                        panel_ref.at[r, i],
                        sem.at[r, i],
                    ).start()

                first += length
        return carry

    def value(i):
        pltpu.make_async_copy(x_ref.at[0], block_ref.at[i], sem.at[parts, i]).wait()
        for r in range(parts):
            pltpu.make_async_copy(piece_refs[0].at[0], panel_ref.at[r, i], sem.at[r, i]).wait()
        return sum(
            jnp.dot(
                block_ref[i, :, pl.ds(pl.multiple_of(part_ref[r] * width, width), width)],
                panel_ref[r, i],
                preferred_element_type=jnp.float32,
            )
            for r in range(parts)
        )

    def step(p, carry):
        i = 2 * p
        one, two = value(i), value(i + 1)
        acc_ref[row_ref[i]] = acc_ref[row_ref[i]] + one
        two = jnp.where(i + 1 < count, two, 0.0)
        acc_ref[row_ref[i + 1]] = acc_ref[row_ref[i + 1]] + two
        return carry

    lax.fori_loop(0, 2 * pairs, start, 0)
    acc_ref[...] = jnp.zeros_like(acc_ref)
    lax.fori_loop(0, pairs, step, 0)


def ladder_few(lists, acc_rows, blocks, parts, pieces):
    at, tile, row, count = lists
    length, rows, across = blocks.shape
    counts = tuple(x.shape[0] for x in pieces[0])
    _, width, panel_width = pieces[0][0].shape
    flat = [x for piece in pieces for x in piece]
    shape = (acc_rows, rows, panel_width)
    return pl.pallas_call(
        functools.partial(few_kernel, counts),
        grid_spec=pltpu.PrefetchScalarGridSpec(
            num_scalar_prefetch=5,
            grid=(1,),
            in_specs=[pl.BlockSpec(memory_space=pl.ANY)] * (1 + len(flat)),
            out_specs=pl.BlockSpec(shape, lambda i, *_: (0, 0, 0)),
            scratch_shapes=[
                pltpu.VMEM((length, rows, across), blocks.dtype),
                pltpu.VMEM((len(pieces), length, width, panel_width), blocks.dtype),
                pltpu.SemaphoreType.DMA((len(pieces) + 1, length)),
            ],
        ),
        out_shape=jax.ShapeDtypeStruct(shape, jnp.float32),
        compiler_params=pltpu.CompilerParams(vmem_limit_bytes=VMEM_LIMIT),
        name="ladder_few",
    )(at, tile, row, count, parts, blocks, *flat)


def squeeze(tile, row):
    length = tile.shape[0]
    at = jnp.arange(length, dtype=jnp.int32)
    valid = tile >= 0
    ahead = jnp.cumsum(valid.astype(jnp.int32))
    count = ahead[-1]
    wanted = jnp.minimum(at, jnp.maximum(count - 1, 0))
    chosen = (valid[None, :] & (ahead[None, :] - 1 == wanted[:, None])).astype(jnp.int32)
    return [jnp.sum(chosen * c[None, :], axis=1) for c in (at, tile, row)] + [count.reshape(1)]


def residual_kernel(
    owner_ref,
    local_ref,
    count_ref,
    map_ref,
    amp_ref,
    weight_ref,
    left_ref,
    right_ref,
    out_ref,
    diag_ref,
    rows_ref,
    turned_ref,
):
    slots = owner_ref.shape[1]
    i = pl.program_id(0)
    used = i % slots < count_ref[i // slots]
    _, _, rows, size = amp_ref.shape
    vt = left_ref.shape[1]
    half = vt // 2
    lanes = 2 * vt
    pieces = size // lanes
    wide = diag_ref.shape[0]

    @pl.when(i == 0)
    def _():
        diag_ref[...] = jnp.zeros_like(diag_ref)

    @pl.when(jnp.logical_not(used))
    def _():
        out_ref[...] = jnp.zeros_like(out_ref)

    @pl.when(used)
    def _():
        for k in range(wide // vt):
            diag_ref[k * vt : (k + 1) * vt, k * vt : (k + 1) * vt] = right_ref[0]
        low = lax.broadcasted_iota(jnp.int32, (half, lanes), 1) < vt
        for k in range(pieces):
            rows_ref[pl.ds(k, rows, stride=pieces), :] = amp_ref[
                0, 0, :, k * lanes : (k + 1) * lanes
            ].astype(jnp.float32)
        for j in range(rows // 2):
            even = rows_ref[(2 * j) * pieces : (2 * j + 1) * pieces, :]
            odd = rows_ref[(2 * j + 1) * pieces : (2 * j + 2) * pieces, :]
            top = jnp.where(low, even, pltpu.roll(odd, vt, 1))
            bottom = jnp.where(low, pltpu.roll(even, vt, 1), odd)
            turned_ref[:, j * lanes : (j + 1) * lanes] = jnp.concatenate([top, bottom], 0).astype(
                jnp.bfloat16
            )
        for j in range(rows // 2):
            both = jnp.dot(
                left_ref[0],
                turned_ref[:, j * lanes : (j + 1) * lanes],
                preferred_element_type=jnp.float32,
            )
            top, bottom = both[:half], both[half:]
            rows_ref[(2 * j) * pieces : (2 * j + 1) * pieces, :] = jnp.where(
                low, top, pltpu.roll(bottom, vt, 1)
            )
            rows_ref[(2 * j + 1) * pieces : (2 * j + 2) * pieces, :] = jnp.where(
                low, pltpu.roll(top, vt, 1), bottom
            )
        for j in range(size // wide):
            at = slice(j * wide, (j + 1) * wide)
            block = amp_ref[0, 0, :, at]
            total = jnp.dot(weight_ref[0], block, preferred_element_type=jnp.float32)
            total = total + jnp.dot(block, diag_ref[...], preferred_element_type=jnp.float32)
            for k in range(wide // lanes):
                piece = j * (wide // lanes) + k
                left = rows_ref[pl.ds(piece, rows, stride=pieces), :]
                out_ref[0, 0, :, piece * lanes : (piece + 1) * lanes] = (
                    total[:, k * lanes : (k + 1) * lanes] + left
                ).astype(jnp.bfloat16)


def residual(tile_owner, tile_local, tile_counts, pair_map, amplitudes, hole_weight, fock_tiles, per_owner):
    tiles, slots, rows, size = amplitudes.shape
    tile_count, vt, _ = fock_tiles.shape
    left = fock_tiles.reshape(tile_count, vt // 2, 2, vt // 2, 2).transpose(0, 2, 1, 4, 3)
    left = left.reshape(tile_count, vt, vt)
    wide = 4 * vt

    def ident(i, owner, local, pairs):
        t, s = i // slots, i % slots
        return pairs[owner[t, s] * per_owner + local[t, s]]

    return pl.pallas_call(
        residual_kernel,
        grid_spec=pltpu.PrefetchScalarGridSpec(
            num_scalar_prefetch=4,
            grid=(tiles * slots,),
            in_specs=[
                pl.BlockSpec((1, 1, rows, size), lambda i, *_: (i // slots, i % slots, 0, 0)),
                pl.BlockSpec((1, rows, rows), lambda i, *_: (i // slots, 0, 0)),
                pl.BlockSpec(
                    (1, vt, vt), lambda i, o, l, c, m: (ident(i, o, l, m) // tile_count, 0, 0)
                ),
                pl.BlockSpec(
                    (1, vt, vt), lambda i, o, l, c, m: (ident(i, o, l, m) % tile_count, 0, 0)
                ),
            ],
            out_specs=pl.BlockSpec((1, 1, rows, size), lambda i, *_: (i // slots, i % slots, 0, 0)),
            scratch_shapes=[
                pltpu.VMEM((wide, wide), jnp.bfloat16),
                pltpu.VMEM((rows * size // (2 * vt), 2 * vt), jnp.float32),
                pltpu.VMEM((vt, rows * vt), jnp.bfloat16),
            ],
        ),
        out_shape=jax.ShapeDtypeStruct(amplitudes.shape, jnp.bfloat16),
        compiler_params=pltpu.CompilerParams(vmem_limit_bytes=VMEM_LIMIT),
        cost_estimate=pl.CostEstimate(
            flops=40 * amplitudes.size * vt, bytes_accessed=4 * amplitudes.size, transcendentals=0
        ),
        name="residual",
    )(tile_owner, tile_local, tile_counts, pair_map, amplitudes, hole_weight, left, fock_tiles)


def per_device(
    amplitudes,
    tile_counts,
    tile_owner,
    tile_local,
    pair_map,
    hole_weight,
    fock_tiles,
    ladder_panels,
):
    owners, parts = lax.axis_size("occ"), lax.axis_size("vir")
    per_owner, part_rows, panel_width = ladder_panels.shape
    tiles, slots, pair_rows, tile_size = amplitudes.shape
    groups = owners // GROUP
    width = part_rows // GROUP
    across = parts * width
    me = lax.axis_index("occ")
    place = me % GROUP
    slot_at = jnp.arange(slots, dtype=jnp.int32)
    group_at = jnp.arange(groups, dtype=jnp.int32)

    named = (slot_at < tile_counts[:, None])[None] & (tile_owner // GROUP == group_at[:, None, None])
    named = named.reshape(groups, tiles * slots)
    own_turn = jnp.cumsum(named.astype(jnp.int32), axis=1) - named
    entry_at = jnp.arange(tiles * slots, dtype=jnp.int32)

    def entries(first, length):
        at = first + jnp.arange(length, dtype=jnp.int32)
        chosen = named[:, None, :] & (own_turn[:, None, :] == at[None, :, None])
        return jnp.sum(jnp.where(chosen, entry_at + 1, 0), axis=2).astype(jnp.int32) - 1

    def send(packed):
        packed = packed.reshape((owners,) + packed.shape[2:])
        return lax.all_to_all(packed, "occ", split_axis=0, concat_axis=0, tiled=True)

    most = tiles * GROUP

    def columns(k, first, count):
        start = (jnp.int32(first), (place ^ k) * width, jnp.int32(0))
        return lax.dynamic_slice(ladder_panels, start, (count, width, panel_width))

    def swap(k, x):
        return lax.ppermute(x, "occ", [(o, o ^ k) for o in range(owners)])

    early = per_owner // 4
    mine = jnp.concatenate([tile_owner, tile_local, tile_counts[:, None]], axis=1)
    soon = [columns(k, 0, early) for k in (1, 2)]
    soon, mine = lax.optimization_barrier((soon, mine))
    soon = [swap(k, x) for k, x in zip((1, 2), soon)]
    main = pack(entries(0, MAIN), amplitudes, parts)
    table = lax.all_to_all(
        jnp.broadcast_to(mine, (owners * parts,) + mine.shape), AXES, 0, 0, tiled=True
    )
    main, table, late, soon = lax.optimization_barrier((main, table, amplitudes, soon))
    main = send(main)
    shared = [columns(0, 0, per_owner)]
    shared += [swap(k, columns(k, early, per_owner - early)) for k in (1, 2)]
    shared += [swap(k, columns(k, 0, per_owner)) for k in range(3, GROUP)]

    local_residual = residual(
        tile_owner, tile_local, tile_counts, pair_map, late, hole_weight, fock_tiles, per_owner
    )
    extras = [pack(entries(MAIN, length), late, parts) for length in (1, 2)]

    used = slot_at < table[:, :, 2 * slots :]
    owner, local = table[:, :, :slots], table[:, :, slots : 2 * slots]
    of_group = used[..., None] & ((owner // GROUP)[..., None] == group_at)
    longest = jnp.max(jnp.sum(of_group, axis=(1, 2)))

    def of_core(x):
        x = x.reshape(owners, parts, tiles, slots)
        x = lax.dynamic_index_in_dim(x, lax.axis_index("vir"), axis=1, keepdims=False)
        return x.reshape(owners, tiles * slots)

    hit = of_core(used & (owner // GROUP == me // GROUP))
    turn = jnp.cumsum(hit.astype(jnp.int32), axis=1) - hit
    tile = of_core(((owner % GROUP) ^ place) * per_owner + local)
    source = jnp.arange(owners, dtype=jnp.int32)
    source = ((source % GROUP) ^ place) * groups + ((source // GROUP) ^ (me // GROUP))
    row = source[:, None] * tiles + entry_at // slots

    def lists(first, length):
        at = first + jnp.arange(length, dtype=jnp.int32)
        chosen = hit[:, None, :] & (turn[:, None, :] == at[None, :, None])
        tiles_of = jnp.sum(jnp.where(chosen, tile[:, None, :] + 1, 0), axis=2) - 1
        rows_of = jnp.sum(jnp.where(chosen, row[:, None, :], 0), axis=2)
        return tiles_of.reshape(-1), rows_of.reshape(-1)

    main_lists = lists(0, MAIN)
    extra_lists = [lists(MAIN, length) for length in range(1, most - MAIN + 1)]
    here = source[None, :] == group_at[:, None]
    extra_tile = jnp.sum(jnp.where(here, extra_lists[0][1] % tiles, 0), axis=1)
    extra_lists[0] = (extra_lists[0][0], extra_lists[0][1] // tiles)
    extra_lists = [squeeze(*x) for x in extra_lists]
    extra_entries = [entries(MAIN, length) for length in range(3, most - MAIN + 1)]
    known = (main_lists, extra_lists, extra_tile, extra_entries)
    core_parts = (lax.axis_index("vir") + jnp.arange(parts, dtype=jnp.int32)) % parts
    empty = jnp.zeros((owners * tiles, pair_rows, panel_width), jnp.float32)
    main, extras, local_residual, shared, known, core_parts, empty = lax.optimization_barrier(
        (main, extras, local_residual, shared, known, core_parts, empty)
    )
    shared = [shared[0], soon[0], shared[1], soon[1], shared[2]] + list(shared[3:])

    def group_sum(acc):
        acc = acc.reshape((GROUP, acc.shape[0] // GROUP) + acc.shape[1:])
        return sum([swap(k, acc[k]) for k in range(1, GROUP)], acc[0])

    def some(length, main, shared, known, extras, amplitudes, core_parts, empty):
        main_lists, extra_lists, extra_tile, extra_entries = known
        if length > len(extras):
            packed = pack(extra_entries[length - 1 - len(extras)], amplitudes, parts)
        elif length > 0:
            packed = extras[length - 1]
        if length > 0:
            blocks = send(packed).reshape(-1, pair_rows, across)
        panels = [shared]
        for r in range(1, parts):
            back = [(v, (v - r) % parts) for v in range(parts)]
            panels.append([lax.ppermute(x, "vir", back) for x in shared])
        main = main.reshape(-1, pair_rows, across)
        acc = ladder(main_lists, empty, main, core_parts[:1], panels[:1])
        if parts > 1:
            acc = ladder(main_lists, acc, main, core_parts[1:], panels[1:])
        acc = group_sum(acc).reshape(groups, tiles, pair_rows, panel_width)
        if length == 0:
            return acc
        rows = owners if length == 1 else owners * tiles
        few = group_sum(ladder_few(extra_lists[length - 1], rows, blocks, core_parts, panels))
        if length == 1:
            at = jnp.arange(tiles, dtype=jnp.int32)
            chosen = (extra_tile[:, None] == at[None, :])[:, :, None, None]
            return acc + jnp.where(chosen, few[:, None], 0.0)
        return acc + few.reshape(acc.shape)

    acc = lax.switch(
        jnp.maximum(longest - MAIN, 0),
        [functools.partial(some, length) for length in range(most - MAIN + 1)],
        main,
        shared,
        known,
        extras,
        amplitudes,
        core_parts,
        empty,
    )
    acc = sum([swap(q * GROUP, acc[q]) for q in range(1, groups)], acc[0])
    return (local_residual, acc.astype(jnp.bfloat16))


def solution(mesh):
    in_specs = (
        P(("occ", "vir"), None, None, None),
        P(("occ", "vir")),
        P(("occ", "vir"), None),
        P(("occ", "vir"), None),
        P(),
        P(("occ", "vir"), None, None),
        P(),
        P("occ", "vir", None),
    )
    out_specs = (P(("occ", "vir"), None, None, None), P(("occ", "vir"), None, None))
    return jax.shard_map(
        per_device, mesh=mesh, in_specs=in_specs, out_specs=out_specs, check_vma=False
    )
```

```python
import functools

import jax
import jax.numpy as jnp
from jax import lax
from jax.experimental import pallas as pl
from jax.experimental.pallas import tpu as pltpu
from jax.sharding import PartitionSpec as P

AXES = ("occ", "vir")
GROUP = 4
MAIN = 4
VMEM_LIMIT = 56 * 1024 * 1024


def pack_kernel(parts, entry_ref, amp_ref, out_ref, block_ref, in_sem, out_sem):
    groups, group, length, _, across = out_ref.shape
    slots = amp_ref.shape[1]
    width = across // parts

    def fetch(i):
        entry = jnp.maximum(entry_ref[i], 0)
        source = amp_ref.at[entry // slots, entry % slots]
        return pltpu.make_async_copy(source, block_ref.at[i], in_sem.at[i])

    def leave(i):
        return [
            pltpu.make_async_copy(
                block_ref.at[i, :, pl.ds((v * group + j) * width, width)],
                out_ref.at[i // length, j, i % length, :, pl.ds(v * width, width)],
                out_sem.at[i],
            )
            for j in range(group)
            for v in range(parts)
        ]

    def each(act):
        def step(i, carry):
            pl.when(entry_ref[i] >= 0)(lambda: act(i))
            return carry

        lax.fori_loop(0, groups * length, step, 0)

    def turn(i):
        fetch(i).wait()
        for copy in leave(i):
            copy.start()

    def finish(i):
        for copy in leave(i):
            copy.wait()

    each(lambda i: fetch(i).start())
    each(turn)
    each(finish)


def pack(entries, amplitudes, parts):
    _, slots, rows, size = amplitudes.shape
    groups, length = entries.shape
    across = size // GROUP
    return pl.pallas_call(
        functools.partial(pack_kernel, parts),
        grid_spec=pltpu.PrefetchScalarGridSpec(
            num_scalar_prefetch=1,
            grid=(1,),
            in_specs=[pl.BlockSpec(memory_space=pl.ANY)],
            out_specs=pl.BlockSpec(memory_space=pl.ANY),
            scratch_shapes=[
                pltpu.VMEM((groups * length, rows, size), amplitudes.dtype),
                pltpu.SemaphoreType.DMA((groups * length,)),
                pltpu.SemaphoreType.DMA((groups * length,)),
            ],
        ),
        out_shape=jax.ShapeDtypeStruct((groups, GROUP, length, rows, across), amplitudes.dtype),
        compiler_params=pltpu.CompilerParams(vmem_limit_bytes=VMEM_LIMIT),
        cost_estimate=pl.CostEstimate(
            flops=0, bytes_accessed=4 * groups * length * rows * size, transcendentals=0
        ),
        name="pack",
    )(entries.reshape(-1), amplitudes)


def ladder_kernel(counts, tile_ref, row_ref, part_ref, x_ref, *refs):
    refs, (acc_ref, panel_ref, sem) = refs[:-3], refs[-3:]
    pieces = panel_ref.shape[0] * len(counts)
    piece_refs, acc_in_refs = refs[:pieces], refs[pieces:]
    g = pl.program_id(0)
    here = x_ref.shape[0]
    parts, _, width, _ = panel_ref.shape

    @pl.when(g == 0)
    def _():
        copies = []
        for r in range(parts):
            first = 0
            for i, count in enumerate(counts):
                copies.append(
                    pltpu.make_async_copy(
                        piece_refs[r * len(counts) + i],
                        panel_ref.at[r, pl.ds(first, count)],
                        sem.at[r, i],
                    )
                )
                first += count
        for copy in copies:
            copy.start()
        acc_ref[...] = acc_in_refs[0][...] if acc_in_refs else jnp.zeros_like(acc_ref)
        for copy in copies:
            copy.wait()

    def step(i, carry):
        at = g * here + i
        tile = tile_ref[at]

        @pl.when(tile >= 0)
        def _():
            row = row_ref[at]
            value = acc_ref[row]
            for r in range(parts):
                first = pl.multiple_of(part_ref[r] * width, width)
                value = value + jnp.dot(
                    x_ref[i, :, pl.ds(first, width)],
                    panel_ref[r, tile],
                    preferred_element_type=jnp.float32,
                )
            acc_ref[row] = value

        return carry

    lax.fori_loop(0, here, step, 0)


def ladder(lists, acc, blocks, parts, pieces):
    tile, row = lists
    count, rows, across = blocks.shape
    counts = tuple(x.shape[0] for x in pieces[0])
    _, width, panel_width = pieces[0][0].shape
    flat = [x for piece in pieces for x in piece]
    steps = 4
    shape = acc if isinstance(acc, tuple) else acc.shape
    before = () if isinstance(acc, tuple) else (acc,)
    whole = pl.BlockSpec(shape, lambda i, *_: (0, 0, 0))
    return pl.pallas_call(
        functools.partial(ladder_kernel, counts),
        grid_spec=pltpu.PrefetchScalarGridSpec(
            num_scalar_prefetch=3,
            grid=(steps,),
            in_specs=[pl.BlockSpec((count // steps, rows, across), lambda i, *_: (i, 0, 0))]
            + [pl.BlockSpec(memory_space=pl.ANY)] * len(flat)
            + [whole] * len(before),
            out_specs=whole,
            scratch_shapes=[
                pltpu.VMEM((len(pieces), sum(counts), width, panel_width), blocks.dtype),
                pltpu.SemaphoreType.DMA((len(pieces), len(counts))),
            ],
        ),
        out_shape=jax.ShapeDtypeStruct(shape, jnp.float32),
        input_output_aliases={4 + len(flat): 0} if before else {},
        compiler_params=pltpu.CompilerParams(vmem_limit_bytes=VMEM_LIMIT),
        cost_estimate=pl.CostEstimate(
            flops=2 * len(pieces) * count * rows * width * panel_width,
            bytes_accessed=2 * (blocks.size + sum(x.size for x in flat)),
            transcendentals=0,
        ),
        name="ladder",
    )(tile, row, parts, blocks, *flat, *before)


def few_kernel(counts, at_ref, tile_ref, row_ref, count_ref, part_ref, x_ref, *refs):
    piece_refs, (acc_ref, block_ref, panel_ref, sem) = refs[:-4], refs[-4:]
    parts, _, width, _ = panel_ref.shape
    count = count_ref[0]
    pairs = (count + 1) // 2

    def start(i, carry):
        pltpu.make_async_copy(x_ref.at[at_ref[i]], block_ref.at[i], sem.at[parts, i]).start()
        tile = tile_ref[i]
        for r in range(parts):
            first = 0
            for j, length in enumerate(counts):

                @pl.when(jnp.logical_and(tile >= first, tile < first + length))
                def _(r=r, j=j, first=first):
                    pltpu.make_async_copy(
                        piece_refs[r * len(counts) + j].at[tile - first],
                        panel_ref.at[r, i],
                        sem.at[r, i],
                    ).start()

                first += length
        return carry

    def value(i):
        pltpu.make_async_copy(x_ref.at[0], block_ref.at[i], sem.at[parts, i]).wait()
        for r in range(parts):
            pltpu.make_async_copy(piece_refs[0].at[0], panel_ref.at[r, i], sem.at[r, i]).wait()
        return sum(
            jnp.dot(
                block_ref[i, :, pl.ds(pl.multiple_of(part_ref[r] * width, width), width)],
                panel_ref[r, i],
                preferred_element_type=jnp.float32,
            )
            for r in range(parts)
        )

    def step(p, carry):
        i = 2 * p
        one, two = value(i), value(i + 1)
        acc_ref[row_ref[i]] = acc_ref[row_ref[i]] + one
        two = jnp.where(i + 1 < count, two, 0.0)
        acc_ref[row_ref[i + 1]] = acc_ref[row_ref[i + 1]] + two
        return carry

    lax.fori_loop(0, 2 * pairs, start, 0)
    acc_ref[...] = jnp.zeros_like(acc_ref)
    lax.fori_loop(0, pairs, step, 0)


def ladder_few(lists, acc_rows, blocks, parts, pieces):
    at, tile, row, count = lists
    length, rows, across = blocks.shape
    counts = tuple(x.shape[0] for x in pieces[0])
    _, width, panel_width = pieces[0][0].shape
    flat = [x for piece in pieces for x in piece]
    shape = (acc_rows, rows, panel_width)
    return pl.pallas_call(
        functools.partial(few_kernel, counts),
        grid_spec=pltpu.PrefetchScalarGridSpec(
            num_scalar_prefetch=5,
            grid=(1,),
            in_specs=[pl.BlockSpec(memory_space=pl.ANY)] * (1 + len(flat)),
            out_specs=pl.BlockSpec(shape, lambda i, *_: (0, 0, 0)),
            scratch_shapes=[
                pltpu.VMEM((length, rows, across), blocks.dtype),
                pltpu.VMEM((len(pieces), length, width, panel_width), blocks.dtype),
                pltpu.SemaphoreType.DMA((len(pieces) + 1, length)),
            ],
        ),
        out_shape=jax.ShapeDtypeStruct(shape, jnp.float32),
        compiler_params=pltpu.CompilerParams(vmem_limit_bytes=VMEM_LIMIT),
        name="ladder_few",
    )(at, tile, row, count, parts, blocks, *flat)


def squeeze(tile, row):
    length = tile.shape[0]
    at = jnp.arange(length, dtype=jnp.int32)
    valid = tile >= 0
    ahead = jnp.cumsum(valid.astype(jnp.int32))
    count = ahead[-1]
    wanted = jnp.minimum(at, jnp.maximum(count - 1, 0))
    chosen = (valid[None, :] & (ahead[None, :] - 1 == wanted[:, None])).astype(jnp.int32)
    return [jnp.sum(chosen * c[None, :], axis=1) for c in (at, tile, row)] + [count.reshape(1)]


def residual_kernel(
    owner_ref,
    local_ref,
    count_ref,
    map_ref,
    amp_ref,
    weight_ref,
    left_ref,
    right_ref,
    out_ref,
    diag_ref,
    rows_ref,
    turned_ref,
):
    slots = owner_ref.shape[1]
    i = pl.program_id(0)
    used = i % slots < count_ref[i // slots]
    _, _, rows, size = amp_ref.shape
    vt = left_ref.shape[1]
    half = vt // 2
    lanes = 2 * vt
    pieces = size // lanes
    wide = diag_ref.shape[0]

    @pl.when(i == 0)
    def _():
        diag_ref[...] = jnp.zeros_like(diag_ref)

    @pl.when(jnp.logical_not(used))
    def _():
        out_ref[...] = jnp.zeros_like(out_ref)

    @pl.when(used)
    def _():
        for k in range(wide // vt):
            diag_ref[k * vt : (k + 1) * vt, k * vt : (k + 1) * vt] = right_ref[0]
        low = lax.broadcasted_iota(jnp.int32, (half, lanes), 1) < vt
        for k in range(pieces):
            rows_ref[pl.ds(k, rows, stride=pieces), :] = amp_ref[
                0, 0, :, k * lanes : (k + 1) * lanes
            ].astype(jnp.float32)
        for j in range(rows // 2):
            even = rows_ref[(2 * j) * pieces : (2 * j + 1) * pieces, :]
            odd = rows_ref[(2 * j + 1) * pieces : (2 * j + 2) * pieces, :]
            top = jnp.where(low, even, pltpu.roll(odd, vt, 1))
            bottom = jnp.where(low, pltpu.roll(even, vt, 1), odd)
            turned_ref[:, j * lanes : (j + 1) * lanes] = jnp.concatenate([top, bottom], 0).astype(
                jnp.bfloat16
            )
        for j in range(rows // 2):
            both = jnp.dot(
                left_ref[0],
                turned_ref[:, j * lanes : (j + 1) * lanes],
                preferred_element_type=jnp.float32,
            )
            top, bottom = both[:half], both[half:]
            rows_ref[(2 * j) * pieces : (2 * j + 1) * pieces, :] = jnp.where(
                low, top, pltpu.roll(bottom, vt, 1)
            )
            rows_ref[(2 * j + 1) * pieces : (2 * j + 2) * pieces, :] = jnp.where(
                low, pltpu.roll(top, vt, 1), bottom
            )
        for j in range(size // wide):
            at = slice(j * wide, (j + 1) * wide)
            block = amp_ref[0, 0, :, at]
            total = jnp.dot(weight_ref[0], block, preferred_element_type=jnp.float32)
            total = total + jnp.dot(block, diag_ref[...], preferred_element_type=jnp.float32)
            for k in range(wide // lanes):
                piece = j * (wide // lanes) + k
                left = rows_ref[pl.ds(piece, rows, stride=pieces), :]
                out_ref[0, 0, :, piece * lanes : (piece + 1) * lanes] = (
                    total[:, k * lanes : (k + 1) * lanes] + left
                ).astype(jnp.bfloat16)


def residual(tile_owner, tile_local, tile_counts, pair_map, amplitudes, hole_weight, fock_tiles, per_owner):
    tiles, slots, rows, size = amplitudes.shape
    tile_count, vt, _ = fock_tiles.shape
    left = fock_tiles.reshape(tile_count, vt // 2, 2, vt // 2, 2).transpose(0, 2, 1, 4, 3)
    left = left.reshape(tile_count, vt, vt)
    wide = 4 * vt

    def ident(i, owner, local, pairs):
        t, s = i // slots, i % slots
        return pairs[owner[t, s] * per_owner + local[t, s]]

    return pl.pallas_call(
        residual_kernel,
        grid_spec=pltpu.PrefetchScalarGridSpec(
            num_scalar_prefetch=4,
            grid=(tiles * slots,),
            in_specs=[
                pl.BlockSpec((1, 1, rows, size), lambda i, *_: (i // slots, i % slots, 0, 0)),
                pl.BlockSpec((1, rows, rows), lambda i, *_: (i // slots, 0, 0)),
                pl.BlockSpec(
                    (1, vt, vt), lambda i, o, l, c, m: (ident(i, o, l, m) // tile_count, 0, 0)
                ),
                pl.BlockSpec(
                    (1, vt, vt), lambda i, o, l, c, m: (ident(i, o, l, m) % tile_count, 0, 0)
                ),
            ],
            out_specs=pl.BlockSpec((1, 1, rows, size), lambda i, *_: (i // slots, i % slots, 0, 0)),
            scratch_shapes=[
                pltpu.VMEM((wide, wide), jnp.bfloat16),
                pltpu.VMEM((rows * size // (2 * vt), 2 * vt), jnp.float32),
                pltpu.VMEM((vt, rows * vt), jnp.bfloat16),
            ],
        ),
        out_shape=jax.ShapeDtypeStruct(amplitudes.shape, jnp.bfloat16),
        compiler_params=pltpu.CompilerParams(vmem_limit_bytes=VMEM_LIMIT),
        cost_estimate=pl.CostEstimate(
            flops=40 * amplitudes.size * vt, bytes_accessed=4 * amplitudes.size, transcendentals=0
        ),
        name="residual",
    )(tile_owner, tile_local, tile_counts, pair_map, amplitudes, hole_weight, left, fock_tiles)


def per_device(
    amplitudes,
    tile_counts,
    tile_owner,
    tile_local,
    pair_map,
    hole_weight,
    fock_tiles,
    ladder_panels,
):
    owners, parts = lax.axis_size("occ"), lax.axis_size("vir")
    per_owner, part_rows, panel_width = ladder_panels.shape
    tiles, slots, pair_rows, tile_size = amplitudes.shape
    groups = owners // GROUP
    width = part_rows // GROUP
    across = parts * width
    me = lax.axis_index("occ")
    place = me % GROUP
    slot_at = jnp.arange(slots, dtype=jnp.int32)
    group_at = jnp.arange(groups, dtype=jnp.int32)

    named = (slot_at < tile_counts[:, None])[None] & (tile_owner // GROUP == group_at[:, None, None])
    named = named.reshape(groups, tiles * slots)
    own_turn = jnp.cumsum(named.astype(jnp.int32), axis=1) - named
    entry_at = jnp.arange(tiles * slots, dtype=jnp.int32)

    def entries(first, length):
        at = first + jnp.arange(length, dtype=jnp.int32)
        chosen = named[:, None, :] & (own_turn[:, None, :] == at[None, :, None])
        return jnp.sum(jnp.where(chosen, entry_at + 1, 0), axis=2).astype(jnp.int32) - 1

    def send(packed):
        packed = packed.reshape((owners,) + packed.shape[2:])
        return lax.all_to_all(packed, "occ", split_axis=0, concat_axis=0, tiled=True)

    most = tiles * GROUP

    def columns(k, first, count):
        start = (jnp.int32(first), (place ^ k) * width, jnp.int32(0))
        return lax.dynamic_slice(ladder_panels, start, (count, width, panel_width))

    def swap(k, x):
        return lax.ppermute(x, "occ", [(o, o ^ k) for o in range(owners)])

    early = per_owner // 4
    mine = jnp.concatenate([tile_owner, tile_local, tile_counts[:, None]], axis=1)
    soon = [columns(k, 0, early) for k in (1, 2)]
    soon, mine = lax.optimization_barrier((soon, mine))
    soon = [swap(k, x) for k, x in zip((1, 2), soon)]
    main = pack(entries(0, MAIN), amplitudes, parts)
    table = lax.all_to_all(
        jnp.broadcast_to(mine, (owners * parts,) + mine.shape), AXES, 0, 0, tiled=True
    )
    main, table, late, soon = lax.optimization_barrier((main, table, amplitudes, soon))
    main = send(main)
    shared = [columns(0, 0, per_owner)]
    shared += [swap(k, columns(k, early, per_owner - early)) for k in (1, 2)]
    shared += [swap(k, columns(k, 0, per_owner)) for k in range(3, GROUP)]

    local_residual = residual(
        tile_owner, tile_local, tile_counts, pair_map, late, hole_weight, fock_tiles, per_owner
    )
    extras = [pack(entries(MAIN, length), late, parts) for length in (1, 2)]

    used = slot_at < table[:, :, 2 * slots :]
    owner, local = table[:, :, :slots], table[:, :, slots : 2 * slots]
    of_group = used[..., None] & ((owner // GROUP)[..., None] == group_at)
    longest = jnp.max(jnp.sum(of_group, axis=(1, 2)))

    def of_core(x):
        x = x.reshape(owners, parts, tiles, slots)
        x = lax.dynamic_index_in_dim(x, lax.axis_index("vir"), axis=1, keepdims=False)
        return x.reshape(owners, tiles * slots)

    hit = of_core(used & (owner // GROUP == me // GROUP))
    turn = jnp.cumsum(hit.astype(jnp.int32), axis=1) - hit
    tile = of_core(((owner % GROUP) ^ place) * per_owner + local)
    source = jnp.arange(owners, dtype=jnp.int32)
    source = ((source % GROUP) ^ place) * groups + ((source // GROUP) ^ (me // GROUP))
    row = source[:, None] * tiles + entry_at // slots

    def lists(first, length):
        at = first + jnp.arange(length, dtype=jnp.int32)
        chosen = hit[:, None, :] & (turn[:, None, :] == at[None, :, None])
        tiles_of = jnp.sum(jnp.where(chosen, tile[:, None, :] + 1, 0), axis=2) - 1
        rows_of = jnp.sum(jnp.where(chosen, row[:, None, :], 0), axis=2)
        return tiles_of.reshape(-1), rows_of.reshape(-1)

    main_lists = lists(0, MAIN)
    extra_lists = [lists(MAIN, length) for length in range(1, most - MAIN + 1)]
    here = source[None, :] == group_at[:, None]
    extra_tile = jnp.sum(jnp.where(here, extra_lists[0][1] % tiles, 0), axis=1)
    extra_lists[0] = (extra_lists[0][0], extra_lists[0][1] // tiles)
    extra_lists = [squeeze(*x) for x in extra_lists]
    extra_entries = [entries(MAIN, length) for length in range(3, most - MAIN + 1)]
    known = (main_lists, extra_lists, extra_tile, extra_entries)
    core_parts = (lax.axis_index("vir") + jnp.arange(parts, dtype=jnp.int32)) % parts
    shared = [shared[0], soon[0], shared[1], soon[1], shared[2]] + list(shared[3:])
    shared = jnp.concatenate(shared, axis=0)
    main, extras, local_residual, shared, known, core_parts = lax.optimization_barrier(
        (main, extras, local_residual, shared, known, core_parts)
    )

    def group_sum(acc):
        acc = acc.reshape((GROUP, acc.shape[0] // GROUP) + acc.shape[1:])
        return sum([swap(k, acc[k]) for k in range(1, GROUP)], acc[0])

    def some(length, main, shared, known, extras, amplitudes, core_parts):
        main_lists, extra_lists, extra_tile, extra_entries = known
        if length > len(extras):
            packed = pack(extra_entries[length - 1 - len(extras)], amplitudes, parts)
        elif length > 0:
            packed = extras[length - 1]
        if length > 0:
            blocks = send(packed).reshape(-1, pair_rows, across)
        panels = [[shared]]
        for r in range(1, parts):
            back = [(v, (v - r) % parts) for v in range(parts)]
            panels.append([lax.ppermute(shared, "vir", back)])
        main = main.reshape(-1, pair_rows, across)
        acc = (owners * tiles, pair_rows, panel_width)
        acc = ladder(main_lists, acc, main, core_parts[:1], panels[:1])
        if parts > 1:
            acc = ladder(main_lists, acc, main, core_parts[1:], panels[1:])
        acc = group_sum(acc).reshape(groups, tiles, pair_rows, panel_width)
        if length == 0:
            return acc
        rows = owners if length == 1 else owners * tiles
        few = group_sum(ladder_few(extra_lists[length - 1], rows, blocks, core_parts, panels))
        if length == 1:
            at = jnp.arange(tiles, dtype=jnp.int32)
            chosen = (extra_tile[:, None] == at[None, :])[:, :, None, None]
            return acc + jnp.where(chosen, few[:, None], 0.0)
        return acc + few.reshape(acc.shape)

    acc = lax.switch(
        jnp.maximum(longest - MAIN, 0),
        [functools.partial(some, length) for length in range(most - MAIN + 1)],
        main,
        shared,
        known,
        extras,
        amplitudes,
        core_parts,
    )
    acc = sum([swap(q * GROUP, acc[q]) for q in range(1, groups)], acc[0])
    return (local_residual, acc.astype(jnp.bfloat16))


def solution(mesh):
    in_specs = (
        P(("occ", "vir"), None, None, None),
        P(("occ", "vir")),
        P(("occ", "vir"), None),
        P(("occ", "vir"), None),
        P(),
        P(("occ", "vir"), None, None),
        P(),
        P("occ", "vir", None),
    )
    out_specs = (P(("occ", "vir"), None, None, None), P(("occ", "vir"), None, None))
    return jax.shard_map(
        per_device, mesh=mesh, in_specs=in_specs, out_specs=out_specs, check_vma=False
    )
```

```python
import functools

import jax
import jax.numpy as jnp
from jax import lax
from jax.experimental import pallas as pl
from jax.experimental.pallas import tpu as pltpu
from jax.sharding import PartitionSpec as P

AXES = ("occ", "vir")
GROUP = 4
MAIN = 4
VMEM_LIMIT = 56 * 1024 * 1024


def pack_kernel(parts, entry_ref, amp_ref, out_ref, block_ref, in_sem, out_sem):
    groups, group, length, _, across = out_ref.shape
    slots = amp_ref.shape[1]
    width = across // parts

    def fetch(i):
        entry = jnp.maximum(entry_ref[i], 0)
        source = amp_ref.at[entry // slots, entry % slots]
        return pltpu.make_async_copy(source, block_ref.at[i], in_sem.at[i])

    def leave(i):
        return [
            pltpu.make_async_copy(
                block_ref.at[i, :, pl.ds((v * group + j) * width, width)],
                out_ref.at[i // length, j, i % length, :, pl.ds(v * width, width)],
                out_sem.at[i],
            )
            for j in range(group)
            for v in range(parts)
        ]

    def each(act):
        def step(i, carry):
            pl.when(entry_ref[i] >= 0)(lambda: act(i))
            return carry

        lax.fori_loop(0, groups * length, step, 0)

    def turn(i):
        fetch(i).wait()
        for copy in leave(i):
            copy.start()

    def finish(i):
        for copy in leave(i):
            copy.wait()

    each(lambda i: fetch(i).start())
    each(turn)
    each(finish)


def pack(entries, amplitudes, parts):
    _, slots, rows, size = amplitudes.shape
    groups, length = entries.shape
    across = size // GROUP
    return pl.pallas_call(
        functools.partial(pack_kernel, parts),
        grid_spec=pltpu.PrefetchScalarGridSpec(
            num_scalar_prefetch=1,
            grid=(1,),
            in_specs=[pl.BlockSpec(memory_space=pl.ANY)],
            out_specs=pl.BlockSpec(memory_space=pl.ANY),
            scratch_shapes=[
                pltpu.VMEM((groups * length, rows, size), amplitudes.dtype),
                pltpu.SemaphoreType.DMA((groups * length,)),
                pltpu.SemaphoreType.DMA((groups * length,)),
            ],
        ),
        out_shape=jax.ShapeDtypeStruct((groups, GROUP, length, rows, across), amplitudes.dtype),
        compiler_params=pltpu.CompilerParams(vmem_limit_bytes=VMEM_LIMIT),
        cost_estimate=pl.CostEstimate(
            flops=0, bytes_accessed=4 * groups * length * rows * size, transcendentals=0
        ),
        name="pack",
    )(entries.reshape(-1), amplitudes)


def ladder_kernel(counts, tile_ref, row_ref, part_ref, x_ref, *refs):
    refs, (acc_ref, panel_ref, sem) = refs[:-3], refs[-3:]
    pieces = panel_ref.shape[0] * len(counts)
    piece_refs, acc_in_refs = refs[:pieces], refs[pieces:]
    g = pl.program_id(0)
    here = x_ref.shape[0]
    parts, _, width, _ = panel_ref.shape

    @pl.when(g == 0)
    def _():
        copies = []
        for r in range(parts):
            first = 0
            for i, count in enumerate(counts):
                copies.append(
                    pltpu.make_async_copy(
                        piece_refs[r * len(counts) + i],
                        panel_ref.at[r, pl.ds(first, count)],
                        sem.at[r, i],
                    )
                )
                first += count
        for copy in copies:
            copy.start()
        acc_ref[...] = acc_in_refs[0][...] if acc_in_refs else jnp.zeros_like(acc_ref)
        for copy in copies:
            copy.wait()

    def step(i, carry):
        at = g * here + i
        tile = tile_ref[at]

        @pl.when(tile >= 0)
        def _():
            row = row_ref[at]
            value = acc_ref[row]
            for r in range(parts):
                first = pl.multiple_of(part_ref[r] * width, width)
                value = value + jnp.dot(
                    x_ref[i, :, pl.ds(first, width)],
                    panel_ref[r, tile],
                    preferred_element_type=jnp.float32,
                )
            acc_ref[row] = value

        return carry

    lax.fori_loop(0, here, step, 0)


def ladder(lists, acc, blocks, parts, pieces):
    tile, row = lists
    count, rows, across = blocks.shape
    counts = tuple(x.shape[0] for x in pieces[0])
    _, width, panel_width = pieces[0][0].shape
    flat = [x for piece in pieces for x in piece]
    steps = 4
    shape = acc if isinstance(acc, tuple) else acc.shape
    before = () if isinstance(acc, tuple) else (acc,)
    whole = pl.BlockSpec(shape, lambda i, *_: (0, 0, 0))
    return pl.pallas_call(
        functools.partial(ladder_kernel, counts),
        grid_spec=pltpu.PrefetchScalarGridSpec(
            num_scalar_prefetch=3,
            grid=(steps,),
            in_specs=[pl.BlockSpec((count // steps, rows, across), lambda i, *_: (i, 0, 0))]
            + [pl.BlockSpec(memory_space=pl.ANY)] * len(flat)
            + [whole] * len(before),
            out_specs=whole,
            scratch_shapes=[
                pltpu.VMEM((len(pieces), sum(counts), width, panel_width), blocks.dtype),
                pltpu.SemaphoreType.DMA((len(pieces), len(counts))),
            ],
        ),
        out_shape=jax.ShapeDtypeStruct(shape, jnp.float32),
        input_output_aliases={4 + len(flat): 0} if before else {},
        compiler_params=pltpu.CompilerParams(vmem_limit_bytes=VMEM_LIMIT),
        cost_estimate=pl.CostEstimate(
            flops=2 * len(pieces) * count * rows * width * panel_width,
            bytes_accessed=2 * (blocks.size + sum(x.size for x in flat)),
            transcendentals=0,
        ),
        name="ladder",
    )(tile, row, parts, blocks, *flat, *before)


def few_kernel(counts, at_ref, tile_ref, row_ref, count_ref, part_ref, x_ref, *refs):
    piece_refs, (acc_ref, block_ref, panel_ref, sem) = refs[:-4], refs[-4:]
    parts, _, width, _ = panel_ref.shape
    count = count_ref[0]
    pairs = (count + 1) // 2

    def start(i, carry):
        pltpu.make_async_copy(x_ref.at[at_ref[i]], block_ref.at[i], sem.at[parts, i]).start()
        tile = tile_ref[i]
        for r in range(parts):
            first = 0
            for j, length in enumerate(counts):

                @pl.when(jnp.logical_and(tile >= first, tile < first + length))
                def _(r=r, j=j, first=first):
                    pltpu.make_async_copy(
                        piece_refs[r * len(counts) + j].at[tile - first],
                        panel_ref.at[r, i],
                        sem.at[r, i],
                    ).start()

                first += length
        return carry

    def value(i):
        pltpu.make_async_copy(x_ref.at[0], block_ref.at[i], sem.at[parts, i]).wait()
        for r in range(parts):
            pltpu.make_async_copy(piece_refs[0].at[0], panel_ref.at[r, i], sem.at[r, i]).wait()
        return sum(
            jnp.dot(
                block_ref[i, :, pl.ds(pl.multiple_of(part_ref[r] * width, width), width)],
                panel_ref[r, i],
                preferred_element_type=jnp.float32,
            )
            for r in range(parts)
        )

    def step(p, carry):
        i = 2 * p
        one, two = value(i), value(i + 1)
        acc_ref[row_ref[i]] = acc_ref[row_ref[i]] + one
        two = jnp.where(i + 1 < count, two, 0.0)
        acc_ref[row_ref[i + 1]] = acc_ref[row_ref[i + 1]] + two
        return carry

    lax.fori_loop(0, 2 * pairs, start, 0)
    acc_ref[...] = jnp.zeros_like(acc_ref)
    lax.fori_loop(0, pairs, step, 0)


def ladder_few(lists, acc_rows, blocks, parts, pieces):
    at, tile, row, count = lists
    length, rows, across = blocks.shape
    counts = tuple(x.shape[0] for x in pieces[0])
    _, width, panel_width = pieces[0][0].shape
    flat = [x for piece in pieces for x in piece]
    shape = (acc_rows, rows, panel_width)
    return pl.pallas_call(
        functools.partial(few_kernel, counts),
        grid_spec=pltpu.PrefetchScalarGridSpec(
            num_scalar_prefetch=5,
            grid=(1,),
            in_specs=[pl.BlockSpec(memory_space=pl.ANY)] * (1 + len(flat)),
            out_specs=pl.BlockSpec(shape, lambda i, *_: (0, 0, 0)),
            scratch_shapes=[
                pltpu.VMEM((length, rows, across), blocks.dtype),
                pltpu.VMEM((len(pieces), length, width, panel_width), blocks.dtype),
                pltpu.SemaphoreType.DMA((len(pieces) + 1, length)),
            ],
        ),
        out_shape=jax.ShapeDtypeStruct(shape, jnp.float32),
        compiler_params=pltpu.CompilerParams(vmem_limit_bytes=VMEM_LIMIT),
        name="ladder_few",
    )(at, tile, row, count, parts, blocks, *flat)


def squeeze(tile, row):
    length = tile.shape[0]
    at = jnp.arange(length, dtype=jnp.int32)
    valid = tile >= 0
    ahead = jnp.cumsum(valid.astype(jnp.int32))
    count = ahead[-1]
    wanted = jnp.minimum(at, jnp.maximum(count - 1, 0))
    chosen = (valid[None, :] & (ahead[None, :] - 1 == wanted[:, None])).astype(jnp.int32)
    return [jnp.sum(chosen * c[None, :], axis=1) for c in (at, tile, row)] + [count.reshape(1)]


def residual_kernel(
    owner_ref,
    local_ref,
    count_ref,
    map_ref,
    amp_ref,
    weight_ref,
    left_ref,
    right_ref,
    out_ref,
    diag_ref,
    rows_ref,
    turned_ref,
):
    slots = owner_ref.shape[1]
    i = pl.program_id(0)
    used = i % slots < count_ref[i // slots]
    _, _, rows, size = amp_ref.shape
    vt = left_ref.shape[1]
    half = vt // 2
    lanes = 2 * vt
    pieces = size // lanes
    wide = diag_ref.shape[0]

    @pl.when(i == 0)
    def _():
        diag_ref[...] = jnp.zeros_like(diag_ref)

    @pl.when(jnp.logical_not(used))
    def _():
        out_ref[...] = jnp.zeros_like(out_ref)

    @pl.when(used)
    def _():
        for k in range(wide // vt):
            diag_ref[k * vt : (k + 1) * vt, k * vt : (k + 1) * vt] = right_ref[0]
        low = lax.broadcasted_iota(jnp.int32, (half, lanes), 1) < vt
        for k in range(pieces):
            rows_ref[pl.ds(k, rows, stride=pieces), :] = amp_ref[
                0, 0, :, k * lanes : (k + 1) * lanes
            ].astype(jnp.float32)
        for j in range(rows // 2):
            even = rows_ref[(2 * j) * pieces : (2 * j + 1) * pieces, :]
            odd = rows_ref[(2 * j + 1) * pieces : (2 * j + 2) * pieces, :]
            top = jnp.where(low, even, pltpu.roll(odd, vt, 1))
            bottom = jnp.where(low, pltpu.roll(even, vt, 1), odd)
            turned_ref[:, j * lanes : (j + 1) * lanes] = jnp.concatenate([top, bottom], 0).astype(
                jnp.bfloat16
            )
        for j in range(rows // 2):
            both = jnp.dot(
                left_ref[0],
                turned_ref[:, j * lanes : (j + 1) * lanes],
                preferred_element_type=jnp.float32,
            )
            top, bottom = both[:half], both[half:]
            rows_ref[(2 * j) * pieces : (2 * j + 1) * pieces, :] = jnp.where(
                low, top, pltpu.roll(bottom, vt, 1)
            )
            rows_ref[(2 * j + 1) * pieces : (2 * j + 2) * pieces, :] = jnp.where(
                low, pltpu.roll(top, vt, 1), bottom
            )
        for j in range(size // wide):
            at = slice(j * wide, (j + 1) * wide)
            block = amp_ref[0, 0, :, at]
            total = jnp.dot(weight_ref[0], block, preferred_element_type=jnp.float32)
            total = total + jnp.dot(block, diag_ref[...], preferred_element_type=jnp.float32)
            for k in range(wide // lanes):
                piece = j * (wide // lanes) + k
                left = rows_ref[pl.ds(piece, rows, stride=pieces), :]
                out_ref[0, 0, :, piece * lanes : (piece + 1) * lanes] = (
                    total[:, k * lanes : (k + 1) * lanes] + left
                ).astype(jnp.bfloat16)


def residual(tile_owner, tile_local, tile_counts, pair_map, amplitudes, hole_weight, fock_tiles, per_owner):
    tiles, slots, rows, size = amplitudes.shape
    tile_count, vt, _ = fock_tiles.shape
    left = fock_tiles.reshape(tile_count, vt // 2, 2, vt // 2, 2).transpose(0, 2, 1, 4, 3)
    left = left.reshape(tile_count, vt, vt)
    wide = 4 * vt

    def ident(i, owner, local, pairs):
        t, s = i // slots, i % slots
        return pairs[owner[t, s] * per_owner + local[t, s]]

    return pl.pallas_call(
        residual_kernel,
        grid_spec=pltpu.PrefetchScalarGridSpec(
            num_scalar_prefetch=4,
            grid=(tiles * slots,),
            in_specs=[
                pl.BlockSpec((1, 1, rows, size), lambda i, *_: (i // slots, i % slots, 0, 0)),
                pl.BlockSpec((1, rows, rows), lambda i, *_: (i // slots, 0, 0)),
                pl.BlockSpec(
                    (1, vt, vt), lambda i, o, l, c, m: (ident(i, o, l, m) // tile_count, 0, 0)
                ),
                pl.BlockSpec(
                    (1, vt, vt), lambda i, o, l, c, m: (ident(i, o, l, m) % tile_count, 0, 0)
                ),
            ],
            out_specs=pl.BlockSpec((1, 1, rows, size), lambda i, *_: (i // slots, i % slots, 0, 0)),
            scratch_shapes=[
                pltpu.VMEM((wide, wide), jnp.bfloat16),
                pltpu.VMEM((rows * size // (2 * vt), 2 * vt), jnp.float32),
                pltpu.VMEM((vt, rows * vt), jnp.bfloat16),
            ],
        ),
        out_shape=jax.ShapeDtypeStruct(amplitudes.shape, jnp.bfloat16),
        compiler_params=pltpu.CompilerParams(vmem_limit_bytes=VMEM_LIMIT),
        cost_estimate=pl.CostEstimate(
            flops=40 * amplitudes.size * vt, bytes_accessed=4 * amplitudes.size, transcendentals=0
        ),
        name="residual",
    )(tile_owner, tile_local, tile_counts, pair_map, amplitudes, hole_weight, left, fock_tiles)


def per_device(
    amplitudes,
    tile_counts,
    tile_owner,
    tile_local,
    pair_map,
    hole_weight,
    fock_tiles,
    ladder_panels,
):
    owners, parts = lax.axis_size("occ"), lax.axis_size("vir")
    per_owner, part_rows, panel_width = ladder_panels.shape
    tiles, slots, pair_rows, tile_size = amplitudes.shape
    groups = owners // GROUP
    width = part_rows // GROUP
    across = parts * width
    me = lax.axis_index("occ")
    place = me % GROUP
    slot_at = jnp.arange(slots, dtype=jnp.int32)
    group_at = jnp.arange(groups, dtype=jnp.int32)

    named = (slot_at < tile_counts[:, None])[None] & (tile_owner // GROUP == group_at[:, None, None])
    named = named.reshape(groups, tiles * slots)
    own_turn = jnp.cumsum(named.astype(jnp.int32), axis=1) - named
    entry_at = jnp.arange(tiles * slots, dtype=jnp.int32)

    def entries(first, length):
        at = first + jnp.arange(length, dtype=jnp.int32)
        chosen = named[:, None, :] & (own_turn[:, None, :] == at[None, :, None])
        return jnp.sum(jnp.where(chosen, entry_at + 1, 0), axis=2).astype(jnp.int32) - 1

    def send(packed):
        packed = packed.reshape((owners,) + packed.shape[2:])
        return lax.all_to_all(packed, "occ", split_axis=0, concat_axis=0, tiled=True)

    most = tiles * GROUP

    def columns(k, first, count):
        start = (jnp.int32(first), (place ^ k) * width, jnp.int32(0))
        return lax.dynamic_slice(ladder_panels, start, (count, width, panel_width))

    def swap(k, x):
        return lax.ppermute(x, "occ", [(o, o ^ k) for o in range(owners)])

    early = per_owner // 4
    mine = jnp.concatenate([tile_owner, tile_local, tile_counts[:, None]], axis=1)
    soon = [columns(k, 0, early) for k in (1, 2)]
    soon, mine = lax.optimization_barrier((soon, mine))
    soon = [swap(k, x) for k, x in zip((1, 2), soon)]
    main = pack(entries(0, MAIN), amplitudes, parts)
    table = lax.all_to_all(
        jnp.broadcast_to(mine, (owners * parts,) + mine.shape), AXES, 0, 0, tiled=True
    )
    main, table, late, soon = lax.optimization_barrier((main, table, amplitudes, soon))
    main = send(main)
    shared = [columns(0, 0, per_owner)]
    shared += [swap(k, columns(k, early, per_owner - early)) for k in (1, 2)]
    shared += [swap(k, columns(k, 0, per_owner)) for k in range(3, GROUP)]

    local_residual = residual(
        tile_owner, tile_local, tile_counts, pair_map, late, hole_weight, fock_tiles, per_owner
    )
    extras = [pack(entries(MAIN, length), late, parts) for length in (1, 2)]

    used = slot_at < table[:, :, 2 * slots :]
    owner, local = table[:, :, :slots], table[:, :, slots : 2 * slots]
    of_group = used[..., None] & ((owner // GROUP)[..., None] == group_at)
    longest = jnp.max(jnp.sum(of_group, axis=(1, 2)))

    def of_core(x):
        x = x.reshape(owners, parts, tiles, slots)
        x = lax.dynamic_index_in_dim(x, lax.axis_index("vir"), axis=1, keepdims=False)
        return x.reshape(owners, tiles * slots)

    hit = of_core(used & (owner // GROUP == me // GROUP))
    turn = jnp.cumsum(hit.astype(jnp.int32), axis=1) - hit
    tile = of_core(((owner % GROUP) ^ place) * per_owner + local)
    source = jnp.arange(owners, dtype=jnp.int32)
    source = ((source % GROUP) ^ place) * groups + ((source // GROUP) ^ (me // GROUP))
    row = source[:, None] * tiles + entry_at // slots

    def lists(first, length):
        at = first + jnp.arange(length, dtype=jnp.int32)
        chosen = hit[:, None, :] & (turn[:, None, :] == at[None, :, None])
        tiles_of = jnp.sum(jnp.where(chosen, tile[:, None, :] + 1, 0), axis=2) - 1
        rows_of = jnp.sum(jnp.where(chosen, row[:, None, :], 0), axis=2)
        return tiles_of.reshape(-1), rows_of.reshape(-1)

    main_lists = lists(0, MAIN)
    extra_lists = [lists(MAIN, length) for length in range(1, most - MAIN + 1)]
    here = source[None, :] == group_at[:, None]
    extra_tile = jnp.sum(jnp.where(here, extra_lists[0][1] % tiles, 0), axis=1)
    extra_lists[0] = (extra_lists[0][0], extra_lists[0][1] // tiles)
    extra_lists = [squeeze(*x) for x in extra_lists]
    extra_entries = [entries(MAIN, length) for length in range(3, most - MAIN + 1)]
    known = (main_lists, extra_lists, extra_tile, extra_entries)
    core_parts = (lax.axis_index("vir") + jnp.arange(parts, dtype=jnp.int32)) % parts
    shared = [shared[0], soon[0], shared[1], soon[1], shared[2]] + list(shared[3:])
    shared = jnp.concatenate(shared, axis=0)
    main, extras, local_residual, shared, known, core_parts = lax.optimization_barrier(
        (main, extras, local_residual, shared, known, core_parts)
    )

    def group_sum(acc):
        acc = acc.reshape((GROUP, acc.shape[0] // GROUP) + acc.shape[1:])
        return sum([swap(k, acc[k]) for k in range(1, GROUP)], acc[0])

    def some(length, main, shared, known, extras, amplitudes, core_parts):
        main_lists, extra_lists, extra_tile, extra_entries = known
        if length > len(extras):
            packed = pack(extra_entries[length - 1 - len(extras)], amplitudes, parts)
        elif length > 0:
            packed = extras[length - 1]
        if length > 0:
            blocks = send(packed).reshape(-1, pair_rows, across)
        panels = [[shared]]
        for r in range(1, parts):
            back = [(v, (v - r) % parts) for v in range(parts)]
            panels.append([lax.ppermute(shared, "vir", back)])
        main = main.reshape(-1, pair_rows, across)
        acc = (owners * tiles, pair_rows, panel_width)
        acc = ladder(main_lists, acc, main, core_parts[:1], panels[:1])
        if parts > 1:
            acc = ladder(main_lists, acc, main, core_parts[1:], panels[1:])
        acc = group_sum(acc).reshape(groups, tiles, pair_rows, panel_width)
        if length == 0:
            return acc
        blocks, acc = lax.optimization_barrier((blocks, acc))
        rows = owners if length == 1 else owners * tiles
        few = group_sum(ladder_few(extra_lists[length - 1], rows, blocks, core_parts, panels))
        if length == 1:
            at = jnp.arange(tiles, dtype=jnp.int32)
            chosen = (extra_tile[:, None] == at[None, :])[:, :, None, None]
            return acc + jnp.where(chosen, few[:, None], 0.0)
        return acc + few.reshape(acc.shape)

    acc = lax.switch(
        jnp.maximum(longest - MAIN, 0),
        [functools.partial(some, length) for length in range(most - MAIN + 1)],
        main,
        shared,
        known,
        extras,
        amplitudes,
        core_parts,
    )
    acc = sum([swap(q * GROUP, acc[q]) for q in range(1, groups)], acc[0])
    return (local_residual, acc.astype(jnp.bfloat16))


def solution(mesh):
    in_specs = (
        P(("occ", "vir"), None, None, None),
        P(("occ", "vir")),
        P(("occ", "vir"), None),
        P(("occ", "vir"), None),
        P(),
        P(("occ", "vir"), None, None),
        P(),
        P("occ", "vir", None),
    )
    out_specs = (P(("occ", "vir"), None, None, None), P(("occ", "vir"), None, None))
    return jax.shard_map(
        per_device, mesh=mesh, in_specs=in_specs, out_specs=out_specs, check_vma=False
    )
```

```python
import functools

import jax
import jax.numpy as jnp
from jax import lax
from jax.experimental import pallas as pl
from jax.experimental.pallas import tpu as pltpu
from jax.sharding import PartitionSpec as P

AXES = ("occ", "vir")
GROUP = 4
MAIN = 4
VMEM_LIMIT = 56 * 1024 * 1024


def pack_kernel(parts, entry_ref, amp_ref, out_ref, block_ref, in_sem, out_sem):
    groups, group, length, _, across = out_ref.shape
    slots = amp_ref.shape[1]
    width = across // parts

    def fetch(i):
        entry = jnp.maximum(entry_ref[i], 0)
        source = amp_ref.at[entry // slots, entry % slots]
        return pltpu.make_async_copy(source, block_ref.at[i], in_sem.at[i])

    def leave(i):
        return [
            pltpu.make_async_copy(
                block_ref.at[i, :, pl.ds((v * group + j) * width, width)],
                out_ref.at[i // length, j, i % length, :, pl.ds(v * width, width)],
                out_sem.at[i],
            )
            for j in range(group)
            for v in range(parts)
        ]

    def each(act):
        def step(i, carry):
            pl.when(entry_ref[i] >= 0)(lambda: act(i))
            return carry

        lax.fori_loop(0, groups * length, step, 0)

    def turn(i):
        fetch(i).wait()
        for copy in leave(i):
            copy.start()

    def finish(i):
        for copy in leave(i):
            copy.wait()

    each(lambda i: fetch(i).start())
    each(turn)
    each(finish)


def pack(entries, amplitudes, parts):
    _, slots, rows, size = amplitudes.shape
    groups, length = entries.shape
    across = size // GROUP
    return pl.pallas_call(
        functools.partial(pack_kernel, parts),
        grid_spec=pltpu.PrefetchScalarGridSpec(
            num_scalar_prefetch=1,
            grid=(1,),
            in_specs=[pl.BlockSpec(memory_space=pl.ANY)],
            out_specs=pl.BlockSpec(memory_space=pl.ANY),
            scratch_shapes=[
                pltpu.VMEM((groups * length, rows, size), amplitudes.dtype),
                pltpu.SemaphoreType.DMA((groups * length,)),
                pltpu.SemaphoreType.DMA((groups * length,)),
            ],
        ),
        out_shape=jax.ShapeDtypeStruct((groups, GROUP, length, rows, across), amplitudes.dtype),
        compiler_params=pltpu.CompilerParams(vmem_limit_bytes=VMEM_LIMIT),
        cost_estimate=pl.CostEstimate(
            flops=0, bytes_accessed=4 * groups * length * rows * size, transcendentals=0
        ),
        name="pack",
    )(entries.reshape(-1), amplitudes)


def ladder_kernel(counts, tile_ref, row_ref, part_ref, x_ref, *refs):
    refs, (acc_ref, panel_ref, sem) = refs[:-3], refs[-3:]
    pieces = panel_ref.shape[0] * len(counts)
    piece_refs, acc_in_refs = refs[:pieces], refs[pieces:]
    g = pl.program_id(0)
    here = x_ref.shape[0]
    parts, _, width, _ = panel_ref.shape

    @pl.when(g == 0)
    def _():
        copies = []
        for r in range(parts):
            first = 0
            for i, count in enumerate(counts):
                copies.append(
                    pltpu.make_async_copy(
                        piece_refs[r * len(counts) + i],
                        panel_ref.at[r, pl.ds(first, count)],
                        sem.at[r, i],
                    )
                )
                first += count
        for copy in copies:
            copy.start()
        acc_ref[...] = acc_in_refs[0][...] if acc_in_refs else jnp.zeros_like(acc_ref)
        for copy in copies:
            copy.wait()

    def value(i, tile):
        total = sum(
            jnp.dot(
                x_ref[i, :, pl.ds(pl.multiple_of(part_ref[r] * width, width), width)],
                panel_ref[r, jnp.maximum(tile, 0)],
                preferred_element_type=jnp.float32,
            )
            for r in range(parts)
        )
        return jnp.where(tile >= 0, total, 0.0)

    def step(p, carry):
        at = g * here + 2 * p
        one, two = tile_ref[at], tile_ref[at + 1]

        @pl.when(jnp.logical_or(one >= 0, two >= 0))
        def _():
            first, second = value(2 * p, one), value(2 * p + 1, two)
            acc_ref[row_ref[at]] = acc_ref[row_ref[at]] + first
            acc_ref[row_ref[at + 1]] = acc_ref[row_ref[at + 1]] + second

        return carry

    lax.fori_loop(0, here // 2, step, 0)


def ladder(lists, acc, blocks, parts, pieces):
    tile, row = lists
    count, rows, across = blocks.shape
    counts = tuple(x.shape[0] for x in pieces[0])
    _, width, panel_width = pieces[0][0].shape
    flat = [x for piece in pieces for x in piece]
    steps = 4
    shape = acc if isinstance(acc, tuple) else acc.shape
    before = () if isinstance(acc, tuple) else (acc,)
    whole = pl.BlockSpec(shape, lambda i, *_: (0, 0, 0))
    return pl.pallas_call(
        functools.partial(ladder_kernel, counts),
        grid_spec=pltpu.PrefetchScalarGridSpec(
            num_scalar_prefetch=3,
            grid=(steps,),
            in_specs=[pl.BlockSpec((count // steps, rows, across), lambda i, *_: (i, 0, 0))]
            + [pl.BlockSpec(memory_space=pl.ANY)] * len(flat)
            + [whole] * len(before),
            out_specs=whole,
            scratch_shapes=[
                pltpu.VMEM((len(pieces), sum(counts), width, panel_width), blocks.dtype),
                pltpu.SemaphoreType.DMA((len(pieces), len(counts))),
            ],
        ),
        out_shape=jax.ShapeDtypeStruct(shape, jnp.float32),
        input_output_aliases={4 + len(flat): 0} if before else {},
        compiler_params=pltpu.CompilerParams(vmem_limit_bytes=VMEM_LIMIT),
        cost_estimate=pl.CostEstimate(
            flops=2 * len(pieces) * count * rows * width * panel_width,
            bytes_accessed=2 * (blocks.size + sum(x.size for x in flat)),
            transcendentals=0,
        ),
        name="ladder",
    )(tile, row, parts, blocks, *flat, *before)


def few_kernel(counts, at_ref, tile_ref, row_ref, count_ref, part_ref, x_ref, *refs):
    piece_refs, (acc_ref, block_ref, panel_ref, sem) = refs[:-4], refs[-4:]
    parts, _, width, _ = panel_ref.shape
    count = count_ref[0]
    pairs = (count + 1) // 2

    def start(i, carry):
        pltpu.make_async_copy(x_ref.at[at_ref[i]], block_ref.at[i], sem.at[parts, i]).start()
        tile = tile_ref[i]
        for r in range(parts):
            first = 0
            for j, length in enumerate(counts):

                @pl.when(jnp.logical_and(tile >= first, tile < first + length))
                def _(r=r, j=j, first=first):
                    pltpu.make_async_copy(
                        piece_refs[r * len(counts) + j].at[tile - first],
                        panel_ref.at[r, i],
                        sem.at[r, i],
                    ).start()

                first += length
        return carry

    def value(i):
        pltpu.make_async_copy(x_ref.at[0], block_ref.at[i], sem.at[parts, i]).wait()
        for r in range(parts):
            pltpu.make_async_copy(piece_refs[0].at[0], panel_ref.at[r, i], sem.at[r, i]).wait()
        return sum(
            jnp.dot(
                block_ref[i, :, pl.ds(pl.multiple_of(part_ref[r] * width, width), width)],
                panel_ref[r, i],
                preferred_element_type=jnp.float32,
            )
            for r in range(parts)
        )

    def step(p, carry):
        i = 2 * p
        one, two = value(i), value(i + 1)
        acc_ref[row_ref[i]] = acc_ref[row_ref[i]] + one
        two = jnp.where(i + 1 < count, two, 0.0)
        acc_ref[row_ref[i + 1]] = acc_ref[row_ref[i + 1]] + two
        return carry

    lax.fori_loop(0, 2 * pairs, start, 0)
    acc_ref[...] = jnp.zeros_like(acc_ref)
    lax.fori_loop(0, pairs, step, 0)


def ladder_few(lists, acc_rows, blocks, parts, pieces):
    at, tile, row, count = lists
    length, rows, across = blocks.shape
    counts = tuple(x.shape[0] for x in pieces[0])
    _, width, panel_width = pieces[0][0].shape
    flat = [x for piece in pieces for x in piece]
    shape = (acc_rows, rows, panel_width)
    return pl.pallas_call(
        functools.partial(few_kernel, counts),
        grid_spec=pltpu.PrefetchScalarGridSpec(
            num_scalar_prefetch=5,
            grid=(1,),
            in_specs=[pl.BlockSpec(memory_space=pl.ANY)] * (1 + len(flat)),
            out_specs=pl.BlockSpec(shape, lambda i, *_: (0, 0, 0)),
            scratch_shapes=[
                pltpu.VMEM((length, rows, across), blocks.dtype),
                pltpu.VMEM((len(pieces), length, width, panel_width), blocks.dtype),
                pltpu.SemaphoreType.DMA((len(pieces) + 1, length)),
            ],
        ),
        out_shape=jax.ShapeDtypeStruct(shape, jnp.float32),
        compiler_params=pltpu.CompilerParams(vmem_limit_bytes=VMEM_LIMIT),
        name="ladder_few",
    )(at, tile, row, count, parts, blocks, *flat)


def squeeze(tile, row):
    length = tile.shape[0]
    at = jnp.arange(length, dtype=jnp.int32)
    valid = tile >= 0
    ahead = jnp.cumsum(valid.astype(jnp.int32))
    count = ahead[-1]
    wanted = jnp.minimum(at, jnp.maximum(count - 1, 0))
    chosen = (valid[None, :] & (ahead[None, :] - 1 == wanted[:, None])).astype(jnp.int32)
    return [jnp.sum(chosen * c[None, :], axis=1) for c in (at, tile, row)] + [count.reshape(1)]


def residual_kernel(
    owner_ref,
    local_ref,
    count_ref,
    map_ref,
    amp_ref,
    weight_ref,
    left_ref,
    right_ref,
    out_ref,
    diag_ref,
    rows_ref,
    turned_ref,
):
    slots = owner_ref.shape[1]
    i = pl.program_id(0)
    used = i % slots < count_ref[i // slots]
    _, _, rows, size = amp_ref.shape
    vt = left_ref.shape[1]
    half = vt // 2
    lanes = 2 * vt
    pieces = size // lanes
    wide = diag_ref.shape[0]

    @pl.when(i == 0)
    def _():
        diag_ref[...] = jnp.zeros_like(diag_ref)

    @pl.when(jnp.logical_not(used))
    def _():
        out_ref[...] = jnp.zeros_like(out_ref)

    @pl.when(used)
    def _():
        for k in range(wide // vt):
            diag_ref[k * vt : (k + 1) * vt, k * vt : (k + 1) * vt] = right_ref[0]
        low = lax.broadcasted_iota(jnp.int32, (half, lanes), 1) < vt
        for k in range(pieces):
            rows_ref[pl.ds(k, rows, stride=pieces), :] = amp_ref[
                0, 0, :, k * lanes : (k + 1) * lanes
            ].astype(jnp.float32)
        for j in range(rows // 2):
            even = rows_ref[(2 * j) * pieces : (2 * j + 1) * pieces, :]
            odd = rows_ref[(2 * j + 1) * pieces : (2 * j + 2) * pieces, :]
            top = jnp.where(low, even, pltpu.roll(odd, vt, 1))
            bottom = jnp.where(low, pltpu.roll(even, vt, 1), odd)
            turned_ref[:, j * lanes : (j + 1) * lanes] = jnp.concatenate([top, bottom], 0).astype(
                jnp.bfloat16
            )
        for j in range(rows // 2):
            both = jnp.dot(
                left_ref[0],
                turned_ref[:, j * lanes : (j + 1) * lanes],
                preferred_element_type=jnp.float32,
            )
            top, bottom = both[:half], both[half:]
            rows_ref[(2 * j) * pieces : (2 * j + 1) * pieces, :] = jnp.where(
                low, top, pltpu.roll(bottom, vt, 1)
            )
            rows_ref[(2 * j + 1) * pieces : (2 * j + 2) * pieces, :] = jnp.where(
                low, pltpu.roll(top, vt, 1), bottom
            )
        for j in range(size // wide):
            at = slice(j * wide, (j + 1) * wide)
            block = amp_ref[0, 0, :, at]
            total = jnp.dot(weight_ref[0], block, preferred_element_type=jnp.float32)
            total = total + jnp.dot(block, diag_ref[...], preferred_element_type=jnp.float32)
            for k in range(wide // lanes):
                piece = j * (wide // lanes) + k
                left = rows_ref[pl.ds(piece, rows, stride=pieces), :]
                out_ref[0, 0, :, piece * lanes : (piece + 1) * lanes] = (
                    total[:, k * lanes : (k + 1) * lanes] + left
                ).astype(jnp.bfloat16)


def residual(tile_owner, tile_local, tile_counts, pair_map, amplitudes, hole_weight, fock_tiles, per_owner):
    tiles, slots, rows, size = amplitudes.shape
    tile_count, vt, _ = fock_tiles.shape
    left = fock_tiles.reshape(tile_count, vt // 2, 2, vt // 2, 2).transpose(0, 2, 1, 4, 3)
    left = left.reshape(tile_count, vt, vt)
    wide = 4 * vt

    def ident(i, owner, local, pairs):
        t, s = i // slots, i % slots
        return pairs[owner[t, s] * per_owner + local[t, s]]

    return pl.pallas_call(
        residual_kernel,
        grid_spec=pltpu.PrefetchScalarGridSpec(
            num_scalar_prefetch=4,
            grid=(tiles * slots,),
            in_specs=[
                pl.BlockSpec((1, 1, rows, size), lambda i, *_: (i // slots, i % slots, 0, 0)),
                pl.BlockSpec((1, rows, rows), lambda i, *_: (i // slots, 0, 0)),
                pl.BlockSpec(
                    (1, vt, vt), lambda i, o, l, c, m: (ident(i, o, l, m) // tile_count, 0, 0)
                ),
                pl.BlockSpec(
                    (1, vt, vt), lambda i, o, l, c, m: (ident(i, o, l, m) % tile_count, 0, 0)
                ),
            ],
            out_specs=pl.BlockSpec((1, 1, rows, size), lambda i, *_: (i // slots, i % slots, 0, 0)),
            scratch_shapes=[
                pltpu.VMEM((wide, wide), jnp.bfloat16),
                pltpu.VMEM((rows * size // (2 * vt), 2 * vt), jnp.float32),
                pltpu.VMEM((vt, rows * vt), jnp.bfloat16),
            ],
        ),
        out_shape=jax.ShapeDtypeStruct(amplitudes.shape, jnp.bfloat16),
        compiler_params=pltpu.CompilerParams(vmem_limit_bytes=VMEM_LIMIT),
        cost_estimate=pl.CostEstimate(
            flops=40 * amplitudes.size * vt, bytes_accessed=4 * amplitudes.size, transcendentals=0
        ),
        name="residual",
    )(tile_owner, tile_local, tile_counts, pair_map, amplitudes, hole_weight, left, fock_tiles)


def per_device(
    amplitudes,
    tile_counts,
    tile_owner,
    tile_local,
    pair_map,
    hole_weight,
    fock_tiles,
    ladder_panels,
):
    owners, parts = lax.axis_size("occ"), lax.axis_size("vir")
    per_owner, part_rows, panel_width = ladder_panels.shape
    tiles, slots, pair_rows, tile_size = amplitudes.shape
    groups = owners // GROUP
    width = part_rows // GROUP
    across = parts * width
    me = lax.axis_index("occ")
    place = me % GROUP
    slot_at = jnp.arange(slots, dtype=jnp.int32)
    group_at = jnp.arange(groups, dtype=jnp.int32)

    named = (slot_at < tile_counts[:, None])[None] & (tile_owner // GROUP == group_at[:, None, None])
    named = named.reshape(groups, tiles * slots)
    own_turn = jnp.cumsum(named.astype(jnp.int32), axis=1) - named
    entry_at = jnp.arange(tiles * slots, dtype=jnp.int32)

    def entries(first, length):
        at = first + jnp.arange(length, dtype=jnp.int32)
        chosen = named[:, None, :] & (own_turn[:, None, :] == at[None, :, None])
        return jnp.sum(jnp.where(chosen, entry_at + 1, 0), axis=2).astype(jnp.int32) - 1

    def send(packed):
        packed = packed.reshape((owners,) + packed.shape[2:])
        return lax.all_to_all(packed, "occ", split_axis=0, concat_axis=0, tiled=True)

    most = tiles * GROUP

    def columns(k, first, count):
        start = (jnp.int32(first), (place ^ k) * width, jnp.int32(0))
        return lax.dynamic_slice(ladder_panels, start, (count, width, panel_width))

    def swap(k, x):
        return lax.ppermute(x, "occ", [(o, o ^ k) for o in range(owners)])

    early = per_owner // 4
    mine = jnp.concatenate([tile_owner, tile_local, tile_counts[:, None]], axis=1)
    soon = [columns(k, 0, early) for k in (1, 2)]
    soon, mine = lax.optimization_barrier((soon, mine))
    soon = [swap(k, x) for k, x in zip((1, 2), soon)]
    main = pack(entries(0, MAIN), amplitudes, parts)
    table = lax.all_to_all(
        jnp.broadcast_to(mine, (owners * parts,) + mine.shape), AXES, 0, 0, tiled=True
    )
    main, table, late, soon = lax.optimization_barrier((main, table, amplitudes, soon))
    main = send(main)
    shared = [columns(0, 0, per_owner)]
    shared += [swap(k, columns(k, early, per_owner - early)) for k in (1, 2)]
    shared += [swap(k, columns(k, 0, per_owner)) for k in range(3, GROUP)]

    local_residual = residual(
        tile_owner, tile_local, tile_counts, pair_map, late, hole_weight, fock_tiles, per_owner
    )
    extras = [pack(entries(MAIN, length), late, parts) for length in (1, 2)]

    used = slot_at < table[:, :, 2 * slots :]
    owner, local = table[:, :, :slots], table[:, :, slots : 2 * slots]
    of_group = used[..., None] & ((owner // GROUP)[..., None] == group_at)
    longest = jnp.max(jnp.sum(of_group, axis=(1, 2)))

    def of_core(x):
        x = x.reshape(owners, parts, tiles, slots)
        x = lax.dynamic_index_in_dim(x, lax.axis_index("vir"), axis=1, keepdims=False)
        return x.reshape(owners, tiles * slots)

    hit = of_core(used & (owner // GROUP == me // GROUP))
    turn = jnp.cumsum(hit.astype(jnp.int32), axis=1) - hit
    tile = of_core(((owner % GROUP) ^ place) * per_owner + local)
    source = jnp.arange(owners, dtype=jnp.int32)
    source = ((source % GROUP) ^ place) * groups + ((source // GROUP) ^ (me // GROUP))
    row = source[:, None] * tiles + entry_at // slots

    def lists(first, length):
        at = first + jnp.arange(length, dtype=jnp.int32)
        chosen = hit[:, None, :] & (turn[:, None, :] == at[None, :, None])
        tiles_of = jnp.sum(jnp.where(chosen, tile[:, None, :] + 1, 0), axis=2) - 1
        rows_of = jnp.sum(jnp.where(chosen, row[:, None, :], 0), axis=2)
        return tiles_of.reshape(-1), rows_of.reshape(-1)

    main_lists = lists(0, MAIN)
    extra_lists = [lists(MAIN, length) for length in range(1, most - MAIN + 1)]
    here = source[None, :] == group_at[:, None]
    extra_tile = jnp.sum(jnp.where(here, extra_lists[0][1] % tiles, 0), axis=1)
    extra_lists[0] = (extra_lists[0][0], extra_lists[0][1] // tiles)
    extra_lists = [squeeze(*x) for x in extra_lists]
    extra_entries = [entries(MAIN, length) for length in range(3, most - MAIN + 1)]
    known = (main_lists, extra_lists, extra_tile, extra_entries)
    core_parts = (lax.axis_index("vir") + jnp.arange(parts, dtype=jnp.int32)) % parts
    shared = [shared[0], soon[0], shared[1], soon[1], shared[2]] + list(shared[3:])
    shared = jnp.concatenate(shared, axis=0)
    main, extras, local_residual, shared, known, core_parts = lax.optimization_barrier(
        (main, extras, local_residual, shared, known, core_parts)
    )

    def group_sum(acc):
        acc = acc.reshape((GROUP, acc.shape[0] // GROUP) + acc.shape[1:])
        return sum([swap(k, acc[k]) for k in range(1, GROUP)], acc[0])

    def some(length, main, shared, known, extras, amplitudes, core_parts):
        main_lists, extra_lists, extra_tile, extra_entries = known
        if length > len(extras):
            packed = pack(extra_entries[length - 1 - len(extras)], amplitudes, parts)
        elif length > 0:
            packed = extras[length - 1]
        if length > 0:
            blocks = send(packed).reshape(-1, pair_rows, across)
        panels = [[shared]]
        for r in range(1, parts):
            back = [(v, (v - r) % parts) for v in range(parts)]
            panels.append([lax.ppermute(shared, "vir", back)])
        main = main.reshape(-1, pair_rows, across)
        acc = (owners * tiles, pair_rows, panel_width)
        acc = ladder(main_lists, acc, main, core_parts[:1], panels[:1])
        if parts > 1:
            acc = ladder(main_lists, acc, main, core_parts[1:], panels[1:])
        acc = group_sum(acc).reshape(groups, tiles, pair_rows, panel_width)
        if length == 0:
            return acc
        blocks, acc = lax.optimization_barrier((blocks, acc))
        rows = owners if length == 1 else owners * tiles
        few = group_sum(ladder_few(extra_lists[length - 1], rows, blocks, core_parts, panels))
        if length == 1:
            at = jnp.arange(tiles, dtype=jnp.int32)
            chosen = (extra_tile[:, None] == at[None, :])[:, :, None, None]
            return acc + jnp.where(chosen, few[:, None], 0.0)
        return acc + few.reshape(acc.shape)

    acc = lax.switch(
        jnp.maximum(longest - MAIN, 0),
        [functools.partial(some, length) for length in range(most - MAIN + 1)],
        main,
        shared,
        known,
        extras,
        amplitudes,
        core_parts,
    )
    acc = sum([swap(q * GROUP, acc[q]) for q in range(1, groups)], acc[0])
    return (local_residual, acc.astype(jnp.bfloat16))


def solution(mesh):
    in_specs = (
        P(("occ", "vir"), None, None, None),
        P(("occ", "vir")),
        P(("occ", "vir"), None),
        P(("occ", "vir"), None),
        P(),
        P(("occ", "vir"), None, None),
        P(),
        P("occ", "vir", None),
    )
    out_specs = (P(("occ", "vir"), None, None, None), P(("occ", "vir"), None, None))
    return jax.shard_map(
        per_device, mesh=mesh, in_specs=in_specs, out_specs=out_specs, check_vma=False
    )
```

```python
import functools

import jax
import jax.numpy as jnp
from jax import lax
from jax.experimental import pallas as pl
from jax.experimental.pallas import tpu as pltpu
from jax.sharding import PartitionSpec as P

AXES = ("occ", "vir")
GROUP = 4
MAIN = 4
VMEM_LIMIT = 56 * 1024 * 1024


def pack_kernel(parts, entry_ref, amp_ref, out_ref, block_ref, in_sem, out_sem):
    groups, group, length, _, across = out_ref.shape
    slots = amp_ref.shape[1]
    width = across // parts

    def fetch(i):
        entry = jnp.maximum(entry_ref[i], 0)
        source = amp_ref.at[entry // slots, entry % slots]
        return pltpu.make_async_copy(source, block_ref.at[i], in_sem.at[i])

    def leave(i):
        return [
            pltpu.make_async_copy(
                block_ref.at[i, :, pl.ds((v * group + j) * width, width)],
                out_ref.at[i // length, j, i % length, :, pl.ds(v * width, width)],
                out_sem.at[i],
            )
            for j in range(group)
            for v in range(parts)
        ]

    def each(act):
        def step(i, carry):
            pl.when(entry_ref[i] >= 0)(lambda: act(i))
            return carry

        lax.fori_loop(0, groups * length, step, 0)

    def turn(i):
        fetch(i).wait()
        for copy in leave(i):
            copy.start()

    def finish(i):
        for copy in leave(i):
            copy.wait()

    each(lambda i: fetch(i).start())
    each(turn)
    each(finish)


def pack(entries, amplitudes, parts):
    _, slots, rows, size = amplitudes.shape
    groups, length = entries.shape
    across = size // GROUP
    return pl.pallas_call(
        functools.partial(pack_kernel, parts),
        grid_spec=pltpu.PrefetchScalarGridSpec(
            num_scalar_prefetch=1,
            grid=(1,),
            in_specs=[pl.BlockSpec(memory_space=pl.ANY)],
            out_specs=pl.BlockSpec(memory_space=pl.ANY),
            scratch_shapes=[
                pltpu.VMEM((groups * length, rows, size), amplitudes.dtype),
                pltpu.SemaphoreType.DMA((groups * length,)),
                pltpu.SemaphoreType.DMA((groups * length,)),
            ],
        ),
        out_shape=jax.ShapeDtypeStruct((groups, GROUP, length, rows, across), amplitudes.dtype),
        compiler_params=pltpu.CompilerParams(vmem_limit_bytes=VMEM_LIMIT),
        cost_estimate=pl.CostEstimate(
            flops=0, bytes_accessed=4 * groups * length * rows * size, transcendentals=0
        ),
        name="pack",
    )(entries.reshape(-1), amplitudes)


def ladder_kernel(counts, tile_ref, row_ref, part_ref, x_ref, *refs):
    refs, (acc_ref, panel_ref, sem) = refs[:-3], refs[-3:]
    pieces = panel_ref.shape[0] * len(counts)
    piece_refs, acc_in_refs = refs[:pieces], refs[pieces:]
    g = pl.program_id(0)
    here = x_ref.shape[0]
    parts, _, width, _ = panel_ref.shape

    @pl.when(g == 0)
    def _():
        copies = []
        for r in range(parts):
            first = 0
            for i, count in enumerate(counts):
                copies.append(
                    pltpu.make_async_copy(
                        piece_refs[r * len(counts) + i],
                        panel_ref.at[r, pl.ds(first, count)],
                        sem.at[r, i],
                    )
                )
                first += count
        for copy in copies:
            copy.start()
        acc_ref[...] = acc_in_refs[0][...] if acc_in_refs else jnp.zeros_like(acc_ref)
        for copy in copies:
            copy.wait()

    def value(i, tile):
        total = sum(
            jnp.dot(
                x_ref[i, :, pl.ds(pl.multiple_of(part_ref[r] * width, width), width)],
                panel_ref[r, jnp.maximum(tile, 0)],
                preferred_element_type=jnp.float32,
            )
            for r in range(parts)
        )
        return jnp.where(tile >= 0, total, 0.0)

    def step(p, carry):
        at = g * here + 2 * p
        one, two = tile_ref[at], tile_ref[at + 1]

        @pl.when(jnp.logical_or(one >= 0, two >= 0))
        def _():
            first, second = value(2 * p, one), value(2 * p + 1, two)
            acc_ref[row_ref[at]] = acc_ref[row_ref[at]] + first
            acc_ref[row_ref[at + 1]] = acc_ref[row_ref[at + 1]] + second

        return carry

    lax.fori_loop(0, here // 2, step, 0)


def ladder(lists, acc, blocks, parts, pieces):
    tile, row = lists
    count, rows, across = blocks.shape
    counts = tuple(x.shape[0] for x in pieces[0])
    _, width, panel_width = pieces[0][0].shape
    flat = [x for piece in pieces for x in piece]
    steps = 4
    shape = acc if isinstance(acc, tuple) else acc.shape
    before = () if isinstance(acc, tuple) else (acc,)
    whole = pl.BlockSpec(shape, lambda i, *_: (0, 0, 0))
    return pl.pallas_call(
        functools.partial(ladder_kernel, counts),
        grid_spec=pltpu.PrefetchScalarGridSpec(
            num_scalar_prefetch=3,
            grid=(steps,),
            in_specs=[pl.BlockSpec((count // steps, rows, across), lambda i, *_: (i, 0, 0))]
            + [pl.BlockSpec(memory_space=pl.ANY)] * len(flat)
            + [whole] * len(before),
            out_specs=whole,
            scratch_shapes=[
                pltpu.VMEM((len(pieces), sum(counts), width, panel_width), blocks.dtype),
                pltpu.SemaphoreType.DMA((len(pieces), len(counts))),
            ],
        ),
        out_shape=jax.ShapeDtypeStruct(shape, jnp.float32),
        input_output_aliases={4 + len(flat): 0} if before else {},
        compiler_params=pltpu.CompilerParams(vmem_limit_bytes=VMEM_LIMIT),
        cost_estimate=pl.CostEstimate(
            flops=2 * len(pieces) * count * rows * width * panel_width,
            bytes_accessed=2 * (blocks.size + sum(x.size for x in flat)),
            transcendentals=0,
        ),
        name="ladder",
    )(tile, row, parts, blocks, *flat, *before)


def few_kernel(counts, at_ref, tile_ref, row_ref, count_ref, part_ref, x_ref, *refs):
    piece_refs, (acc_ref, block_ref, panel_ref, sem) = refs[:-4], refs[-4:]
    parts, _, width, _ = panel_ref.shape
    count = count_ref[0]
    pairs = (count + 1) // 2

    def start(i, carry):
        pltpu.make_async_copy(x_ref.at[at_ref[i]], block_ref.at[i], sem.at[parts, i]).start()
        tile = tile_ref[i]
        for r in range(parts):
            first = 0
            for j, length in enumerate(counts):

                @pl.when(jnp.logical_and(tile >= first, tile < first + length))
                def _(r=r, j=j, first=first):
                    pltpu.make_async_copy(
                        piece_refs[r * len(counts) + j].at[tile - first],
                        panel_ref.at[r, i],
                        sem.at[r, i],
                    ).start()

                first += length
        return carry

    def value(i):
        pltpu.make_async_copy(x_ref.at[0], block_ref.at[i], sem.at[parts, i]).wait()
        for r in range(parts):
            pltpu.make_async_copy(piece_refs[0].at[0], panel_ref.at[r, i], sem.at[r, i]).wait()
        return sum(
            jnp.dot(
                block_ref[i, :, pl.ds(pl.multiple_of(part_ref[r] * width, width), width)],
                panel_ref[r, i],
                preferred_element_type=jnp.float32,
            )
            for r in range(parts)
        )

    def step(p, carry):
        i = 2 * p
        one, two = value(i), value(i + 1)
        acc_ref[row_ref[i]] = acc_ref[row_ref[i]] + one
        two = jnp.where(i + 1 < count, two, 0.0)
        acc_ref[row_ref[i + 1]] = acc_ref[row_ref[i + 1]] + two
        return carry

    lax.fori_loop(0, 2 * pairs, start, 0)
    acc_ref[...] = jnp.zeros_like(acc_ref)
    lax.fori_loop(0, pairs, step, 0)


def ladder_few(lists, acc_rows, blocks, parts, pieces):
    at, tile, row, count = lists
    length, rows, across = blocks.shape
    counts = tuple(x.shape[0] for x in pieces[0])
    _, width, panel_width = pieces[0][0].shape
    flat = [x for piece in pieces for x in piece]
    shape = (acc_rows, rows, panel_width)
    return pl.pallas_call(
        functools.partial(few_kernel, counts),
        grid_spec=pltpu.PrefetchScalarGridSpec(
            num_scalar_prefetch=5,
            grid=(1,),
            in_specs=[pl.BlockSpec(memory_space=pl.ANY)] * (1 + len(flat)),
            out_specs=pl.BlockSpec(shape, lambda i, *_: (0, 0, 0)),
            scratch_shapes=[
                pltpu.VMEM((length, rows, across), blocks.dtype),
                pltpu.VMEM((len(pieces), length, width, panel_width), blocks.dtype),
                pltpu.SemaphoreType.DMA((len(pieces) + 1, length)),
            ],
        ),
        out_shape=jax.ShapeDtypeStruct(shape, jnp.float32),
        compiler_params=pltpu.CompilerParams(vmem_limit_bytes=VMEM_LIMIT),
        name="ladder_few",
    )(at, tile, row, count, parts, blocks, *flat)


def squeeze(tile, row):
    length = tile.shape[0]
    at = jnp.arange(length, dtype=jnp.int32)
    valid = tile >= 0
    ahead = jnp.cumsum(valid.astype(jnp.int32))
    count = ahead[-1]
    wanted = jnp.minimum(at, jnp.maximum(count - 1, 0))
    chosen = (valid[None, :] & (ahead[None, :] - 1 == wanted[:, None])).astype(jnp.int32)
    return [jnp.sum(chosen * c[None, :], axis=1) for c in (at, tile, row)] + [count.reshape(1)]


def residual_kernel(
    owner_ref,
    local_ref,
    count_ref,
    map_ref,
    amp_ref,
    weight_ref,
    left_ref,
    right_ref,
    out_ref,
    diag_ref,
    rows_ref,
    turned_ref,
):
    slots = owner_ref.shape[1]
    i = pl.program_id(0)
    used = i % slots < count_ref[i // slots]
    _, _, rows, size = amp_ref.shape
    vt = left_ref.shape[1]
    half = vt // 2
    lanes = 2 * vt
    pieces = size // lanes
    wide = diag_ref.shape[0]

    @pl.when(i == 0)
    def _():
        diag_ref[...] = jnp.zeros_like(diag_ref)

    @pl.when(jnp.logical_not(used))
    def _():
        out_ref[...] = jnp.zeros_like(out_ref)

    @pl.when(used)
    def _():
        for k in range(wide // vt):
            diag_ref[k * vt : (k + 1) * vt, k * vt : (k + 1) * vt] = right_ref[0]
        low = lax.broadcasted_iota(jnp.int32, (half, lanes), 1) < vt
        for k in range(pieces):
            rows_ref[pl.ds(k, rows, stride=pieces), :] = amp_ref[
                0, 0, :, k * lanes : (k + 1) * lanes
            ].astype(jnp.float32)
        for j in range(rows // 2):
            even = rows_ref[(2 * j) * pieces : (2 * j + 1) * pieces, :]
            odd = rows_ref[(2 * j + 1) * pieces : (2 * j + 2) * pieces, :]
            top = jnp.where(low, even, pltpu.roll(odd, vt, 1))
            bottom = jnp.where(low, pltpu.roll(even, vt, 1), odd)
            turned_ref[:, j * lanes : (j + 1) * lanes] = jnp.concatenate([top, bottom], 0).astype(
                jnp.bfloat16
            )
        for j in range(rows // 2):
            both = jnp.dot(
                left_ref[0],
                turned_ref[:, j * lanes : (j + 1) * lanes],
                preferred_element_type=jnp.float32,
            )
            top, bottom = both[:half], both[half:]
            rows_ref[(2 * j) * pieces : (2 * j + 1) * pieces, :] = jnp.where(
                low, top, pltpu.roll(bottom, vt, 1)
            )
            rows_ref[(2 * j + 1) * pieces : (2 * j + 2) * pieces, :] = jnp.where(
                low, pltpu.roll(top, vt, 1), bottom
            )
        for j in range(size // wide):
            at = slice(j * wide, (j + 1) * wide)
            block = amp_ref[0, 0, :, at]
            total = jnp.dot(weight_ref[0], block, preferred_element_type=jnp.float32)
            total = total + jnp.dot(block, diag_ref[...], preferred_element_type=jnp.float32)
            for k in range(wide // lanes):
                piece = j * (wide // lanes) + k
                left = rows_ref[pl.ds(piece, rows, stride=pieces), :]
                out_ref[0, 0, :, piece * lanes : (piece + 1) * lanes] = (
                    total[:, k * lanes : (k + 1) * lanes] + left
                ).astype(jnp.bfloat16)


def residual(tile_owner, tile_local, tile_counts, pair_map, amplitudes, hole_weight, fock_tiles, per_owner):
    tiles, slots, rows, size = amplitudes.shape
    tile_count, vt, _ = fock_tiles.shape
    left = fock_tiles.reshape(tile_count, vt // 2, 2, vt // 2, 2).transpose(0, 2, 1, 4, 3)
    left = left.reshape(tile_count, vt, vt)
    wide = 4 * vt

    def ident(i, owner, local, pairs):
        t, s = i // slots, i % slots
        return pairs[owner[t, s] * per_owner + local[t, s]]

    return pl.pallas_call(
        residual_kernel,
        grid_spec=pltpu.PrefetchScalarGridSpec(
            num_scalar_prefetch=4,
            grid=(tiles * slots,),
            in_specs=[
                pl.BlockSpec((1, 1, rows, size), lambda i, *_: (i // slots, i % slots, 0, 0)),
                pl.BlockSpec((1, rows, rows), lambda i, *_: (i // slots, 0, 0)),
                pl.BlockSpec(
                    (1, vt, vt), lambda i, o, l, c, m: (ident(i, o, l, m) // tile_count, 0, 0)
                ),
                pl.BlockSpec(
                    (1, vt, vt), lambda i, o, l, c, m: (ident(i, o, l, m) % tile_count, 0, 0)
                ),
            ],
            out_specs=pl.BlockSpec((1, 1, rows, size), lambda i, *_: (i // slots, i % slots, 0, 0)),
            scratch_shapes=[
                pltpu.VMEM((wide, wide), jnp.bfloat16),
                pltpu.VMEM((rows * size // (2 * vt), 2 * vt), jnp.float32),
                pltpu.VMEM((vt, rows * vt), jnp.bfloat16),
            ],
        ),
        out_shape=jax.ShapeDtypeStruct(amplitudes.shape, jnp.bfloat16),
        compiler_params=pltpu.CompilerParams(vmem_limit_bytes=VMEM_LIMIT),
        cost_estimate=pl.CostEstimate(
            flops=40 * amplitudes.size * vt, bytes_accessed=4 * amplitudes.size, transcendentals=0
        ),
        name="residual",
    )(tile_owner, tile_local, tile_counts, pair_map, amplitudes, hole_weight, left, fock_tiles)


def per_device(
    amplitudes,
    tile_counts,
    tile_owner,
    tile_local,
    pair_map,
    hole_weight,
    fock_tiles,
    ladder_panels,
):
    owners, parts = lax.axis_size("occ"), lax.axis_size("vir")
    per_owner, part_rows, panel_width = ladder_panels.shape
    tiles, slots, pair_rows, tile_size = amplitudes.shape
    groups = owners // GROUP
    width = part_rows // GROUP
    across = parts * width
    me = lax.axis_index("occ")
    place = me % GROUP
    slot_at = jnp.arange(slots, dtype=jnp.int32)
    group_at = jnp.arange(groups, dtype=jnp.int32)

    named = (slot_at < tile_counts[:, None])[None] & (tile_owner // GROUP == group_at[:, None, None])
    named = named.reshape(groups, tiles * slots)
    own_turn = jnp.cumsum(named.astype(jnp.int32), axis=1) - named
    entry_at = jnp.arange(tiles * slots, dtype=jnp.int32)

    def entries(first, length):
        at = first + jnp.arange(length, dtype=jnp.int32)
        chosen = named[:, None, :] & (own_turn[:, None, :] == at[None, :, None])
        return jnp.sum(jnp.where(chosen, entry_at + 1, 0), axis=2).astype(jnp.int32) - 1

    def send(packed):
        packed = packed.reshape((owners,) + packed.shape[2:])
        return lax.all_to_all(packed, "occ", split_axis=0, concat_axis=0, tiled=True)

    most = tiles * GROUP

    def columns(k, first, count):
        start = (jnp.int32(first), (place ^ k) * width, jnp.int32(0))
        return lax.dynamic_slice(ladder_panels, start, (count, width, panel_width))

    def swap(k, x):
        return lax.ppermute(x, "occ", [(o, o ^ k) for o in range(owners)])

    early = per_owner // 8
    mine = jnp.concatenate([tile_owner, tile_local, tile_counts[:, None]], axis=1)
    soon = [columns(k, 0, early) for k in (1, 2)]
    soon, mine = lax.optimization_barrier((soon, mine))
    soon = [swap(k, x) for k, x in zip((1, 2), soon)]
    main = pack(entries(0, MAIN), amplitudes, parts)
    table = lax.all_to_all(
        jnp.broadcast_to(mine, (owners * parts,) + mine.shape), AXES, 0, 0, tiled=True
    )
    main, table, late, soon = lax.optimization_barrier((main, table, amplitudes, soon))
    main = send(main)
    shared = [columns(0, 0, per_owner)]
    shared += [swap(k, columns(k, early, per_owner - early)) for k in (1, 2)]
    shared += [swap(k, columns(k, 0, per_owner)) for k in range(3, GROUP)]

    local_residual = residual(
        tile_owner, tile_local, tile_counts, pair_map, late, hole_weight, fock_tiles, per_owner
    )
    extras = [pack(entries(MAIN, length), late, parts) for length in (1, 2)]

    used = slot_at < table[:, :, 2 * slots :]
    owner, local = table[:, :, :slots], table[:, :, slots : 2 * slots]
    of_group = used[..., None] & ((owner // GROUP)[..., None] == group_at)
    longest = jnp.max(jnp.sum(of_group, axis=(1, 2)))

    def of_core(x):
        x = x.reshape(owners, parts, tiles, slots)
        x = lax.dynamic_index_in_dim(x, lax.axis_index("vir"), axis=1, keepdims=False)
        return x.reshape(owners, tiles * slots)

    hit = of_core(used & (owner // GROUP == me // GROUP))
    turn = jnp.cumsum(hit.astype(jnp.int32), axis=1) - hit
    tile = of_core(((owner % GROUP) ^ place) * per_owner + local)
    source = jnp.arange(owners, dtype=jnp.int32)
    source = ((source % GROUP) ^ place) * groups + ((source // GROUP) ^ (me // GROUP))
    row = source[:, None] * tiles + entry_at // slots

    def lists(first, length):
        at = first + jnp.arange(length, dtype=jnp.int32)
        chosen = hit[:, None, :] & (turn[:, None, :] == at[None, :, None])
        tiles_of = jnp.sum(jnp.where(chosen, tile[:, None, :] + 1, 0), axis=2) - 1
        rows_of = jnp.sum(jnp.where(chosen, row[:, None, :], 0), axis=2)
        return tiles_of.reshape(-1), rows_of.reshape(-1)

    main_lists = lists(0, MAIN)
    extra_lists = [lists(MAIN, length) for length in range(1, most - MAIN + 1)]
    here = source[None, :] == group_at[:, None]
    extra_tile = jnp.sum(jnp.where(here, extra_lists[0][1] % tiles, 0), axis=1)
    extra_lists[0] = (extra_lists[0][0], extra_lists[0][1] // tiles)
    extra_lists = [squeeze(*x) for x in extra_lists]
    extra_entries = [entries(MAIN, length) for length in range(3, most - MAIN + 1)]
    known = (main_lists, extra_lists, extra_tile, extra_entries)
    core_parts = (lax.axis_index("vir") + jnp.arange(parts, dtype=jnp.int32)) % parts
    shared = [shared[0], soon[0], shared[1], soon[1], shared[2]] + list(shared[3:])
    shared = jnp.concatenate(shared, axis=0)
    main, extras, local_residual, shared, known, core_parts = lax.optimization_barrier(
        (main, extras, local_residual, shared, known, core_parts)
    )

    def group_sum(acc):
        acc = acc.reshape((GROUP, acc.shape[0] // GROUP) + acc.shape[1:])
        return sum([swap(k, acc[k]) for k in range(1, GROUP)], acc[0])

    def some(length, main, shared, known, extras, amplitudes, core_parts):
        main_lists, extra_lists, extra_tile, extra_entries = known
        if length > len(extras):
            packed = pack(extra_entries[length - 1 - len(extras)], amplitudes, parts)
        elif length > 0:
            packed = extras[length - 1]
        if length > 0:
            blocks = send(packed).reshape(-1, pair_rows, across)
        panels = [[shared]]
        for r in range(1, parts):
            back = [(v, (v - r) % parts) for v in range(parts)]
            panels.append([lax.ppermute(shared, "vir", back)])
        main = main.reshape(-1, pair_rows, across)
        acc = (owners * tiles, pair_rows, panel_width)
        acc = ladder(main_lists, acc, main, core_parts[:1], panels[:1])
        if parts > 1:
            acc = ladder(main_lists, acc, main, core_parts[1:], panels[1:])
        acc = group_sum(acc).reshape(groups, tiles, pair_rows, panel_width)
        if length == 0:
            return acc
        blocks, acc = lax.optimization_barrier((blocks, acc))
        rows = owners if length == 1 else owners * tiles
        few = group_sum(ladder_few(extra_lists[length - 1], rows, blocks, core_parts, panels))
        if length == 1:
            at = jnp.arange(tiles, dtype=jnp.int32)
            chosen = (extra_tile[:, None] == at[None, :])[:, :, None, None]
            return acc + jnp.where(chosen, few[:, None], 0.0)
        return acc + few.reshape(acc.shape)

    acc = lax.switch(
        jnp.maximum(longest - MAIN, 0),
        [functools.partial(some, length) for length in range(most - MAIN + 1)],
        main,
        shared,
        known,
        extras,
        amplitudes,
        core_parts,
    )
    acc = sum([swap(q * GROUP, acc[q]) for q in range(1, groups)], acc[0])
    return (local_residual, acc.astype(jnp.bfloat16))


def solution(mesh):
    in_specs = (
        P(("occ", "vir"), None, None, None),
        P(("occ", "vir")),
        P(("occ", "vir"), None),
        P(("occ", "vir"), None),
        P(),
        P(("occ", "vir"), None, None),
        P(),
        P("occ", "vir", None),
    )
    out_specs = (P(("occ", "vir"), None, None, None), P(("occ", "vir"), None, None))
    return jax.shard_map(
        per_device, mesh=mesh, in_specs=in_specs, out_specs=out_specs, check_vma=False
    )
```
